256 devices in a mesh: cfg: 2 (over x_lo), seq: 128 (over y, z, x_hi, core).
Axes of the slice: x: 4 (x_hi: 2, x_lo: 2; x = x_hi * 2 + x_lo), y: 4, z: 8, core: 2. Of those that a mesh axis runs over, the one named last changes fastest.
Arguments:
- coarse_hidden: bfloat16 [2, 256, 64, 2048], P('cfg', 'seq'), may hold values from -6 to 6
- coarse_modulation: float32 [2, 2, 2048], P('cfg'), may hold values from -3 to 3
- final_weight: bfloat16 [2048, 32], replicated, may hold values from -0.125 to 0.125
- coarse_latent: float32 [256, 2048], P('seq'), may hold values from -6 to 6
- step_index: int32 [1], replicated, may hold values from 0 to 49
- guide_index: int32 [1], replicated, may hold values from 0 to 4095
- guide_scales: float32 [4096], replicated, may hold values from 1.5 to 6
- upsample_weight: float32 [288, 32], replicated, may hold values from -0.375 to 0.375
- upsample_bias: float32 [32], replicated, may hold values from -3 to 3
- embed_weight: bfloat16 [32, 2048], replicated, may hold values from -1 to 1
- embed_bias: float32 [2048], replicated, may hold values from -3 to 3
- fine_modulation: float32 [3, 2048], replicated, may hold values from -3 to 3
- project_weight: bfloat16 [2048, 3072], P(('cfg', 'seq')), may hold values from -0.125 to 0.125
- query_gain: float32 [128], replicated, may hold values from 0.25 to 1.75
- key_gain: float32 [128], replicated, may hold values from 0.25 to 1.75
- text_keys: bfloat16 [256, 1024], replicated, may hold values from -6 to 6
- text_values: bfloat16 [256, 1024], replicated, may hold values from -6 to 6
- text_length: int32 [1], replicated, may hold values from 192 to 256
- output_weight: bfloat16 [1024, 2048], P(None, ('cfg', 'seq')), may hold values from -0.1875 to 0.1875
Outputs:
- guided_velocity: float32 [256, 2048], P('seq')
- fine_latent: float32 [256, 2, 4096], P('seq', 'cfg')
- fine_hidden: bfloat16 [256, 2, 128, 2048], P('seq', 'cfg')
The draws below stay inside these ranges and needn't reach their ends.
All inputs are finite; a program needn't handle non-finite values.
Results may differ from the reference program's by a relative error of at most 0.0053.
Values may be sent and summed in bfloat16 or wider, within the bound.
A program may use at most 128 MiB of HBM per device.

```python
import jax
import jax.numpy as jnp
from jax import lax

D = 2048
HEAD_DIM = 128
CHANNELS = 32
HEADS = 8
WA = 64
TEXT = 256
GUIDES = 4096
STEPS = 50
REACH = 1
HA = 256
INNER = 1024


def draw_fine_modulation(key, part):
    shift_key = jax.random.fold_in(key, 11)
    size_key = jax.random.fold_in(key, 12)
    sign_key = jax.random.fold_in(key, 13)
    leading = jnp.clip(0.5 * jax.random.normal(shift_key, (2, D), jnp.float32), -3.0, 3.0)
    magnitude = jax.random.uniform(size_key, (1, D), jnp.float32, 2.0, 3.0)
    signs = jnp.where(jax.random.bernoulli(sign_key, 0.5, (1, D)), 1.0, -1.0)
    return jnp.concatenate([leading, magnitude * signs], 0).astype(jnp.float32)


def levels(rng, extent, shards, smallest, top_value):
    def one(dim, parts):
        steps = jax.random.uniform(jax.random.fold_in(jax.random.fold_in(rng, 6), dim), (parts,), jnp.float32, smallest / len(shards), top_value / len(shards))
        return jnp.repeat(jnp.exp(steps), extent[dim] // parts).reshape((-1,) + (1,) * (len(extent) - dim - 1))

    factor_of = one(*shards[0])
    for cut in shards[1:]:
        factor_of = factor_of * one(*cut)
    return factor_of


def normal_values(rng, shape, scale, bound, cuts=(), kind=jnp.bfloat16):
    values = jax.random.normal(rng, shape, jnp.float32) * scale
    if len(cuts) > 0:
        values = levels(rng, shape, cuts, -0.22, 0.18) * values
    return jnp.clip(values, min=-bound, max=bound).astype(kind)


def setup_inputs(seed: int = 0) -> dict:
    seeds = jax.random.split(jax.random.key(seed), 20)
    coarse_hidden = normal_values(seeds[0], (2, HA, WA, D), 1.0, 6.0, ((0, 2), (1, 128)))
    coarse_modulation = normal_values(seeds[1], (2, 2, D), 0.5, 3.0, ((0, 2),), jnp.float32)
    final_weight = normal_values(seeds[2], (D, CHANNELS), D ** -0.5, 0.125)
    coarse_latent = normal_values(seeds[3], (HA, WA * CHANNELS), 1.0, 6.0, ((0, 128),), jnp.float32)
    step_index = jax.random.randint(seeds[4], (1,), 0, STEPS).astype(jnp.int32)
    guide_index = jax.random.randint(seeds[5], (1,), 0, GUIDES).astype(jnp.int32)
    guide_scales = jnp.clip(jax.random.uniform(seeds[6], (GUIDES,), jnp.float32, 1.5, 6.0), 1.5, 6.0)
    upsample_weight = normal_values(seeds[7], (9 * CHANNELS, CHANNELS), (9 * CHANNELS) ** -0.5, 0.375, (), jnp.float32)
    upsample_bias = normal_values(seeds[8], (CHANNELS,), 0.5, 3.0, (), jnp.float32)
    embed_weight = normal_values(seeds[9], (CHANNELS, D), CHANNELS ** -0.5, 1.0)
    embed_bias = normal_values(seeds[10], (D,), 0.5, 3.0, (), jnp.float32)
    fine_modulation = draw_fine_modulation(jax.random.fold_in(seeds[19], 71), 0)
    project_weight = normal_values(seeds[12], (D, 3 * INNER), D ** -0.5, 0.125, ((0, 256),))
    query_gain = jnp.clip(1.0 + 0.15 * jax.random.normal(seeds[13], (HEAD_DIM,), jnp.float32), 0.25, 1.75)
    key_gain = jnp.clip(1.0 + 0.15 * jax.random.normal(seeds[14], (HEAD_DIM,), jnp.float32), 0.25, 1.75)
    text_keys = normal_values(seeds[15], (TEXT, INNER), 1.0, 6.0)
    text_values = jnp.clip(jax.random.uniform(seeds[16], (TEXT, INNER), jnp.float32, -6.0, 6.0), -6.0, 6.0).astype(jnp.bfloat16)
    text_length = jax.random.randint(seeds[17], (1,), TEXT * 3 // 4, TEXT + 1).astype(jnp.int32)
    output_weight = normal_values(seeds[18], (INNER, D), INNER ** -0.5, 0.1875, ((1, 256),))
    return {"coarse_hidden": coarse_hidden, "coarse_modulation": coarse_modulation, "final_weight": final_weight, "coarse_latent": coarse_latent, "step_index": step_index, "guide_index": guide_index, "guide_scales": guide_scales, "upsample_weight": upsample_weight, "upsample_bias": upsample_bias, "embed_weight": embed_weight, "embed_bias": embed_bias, "fine_modulation": fine_modulation, "project_weight": project_weight, "query_gain": query_gain, "key_gain": key_gain, "text_keys": text_keys, "text_values": text_values, "text_length": text_length, "output_weight": output_weight}


epsilon = 1e-06
flow_shift = 5.0
highest = lax.Precision.HIGHEST

def layer_norm(values):
    centred = values - lax.optimization_barrier(jnp.mean(values, -1, keepdims=True))
    return centred * lax.rsqrt(lax.optimization_barrier(jnp.mean(centred * centred, -1, keepdims=True)) + epsilon)

def rms_heads(values, gain_vector, head_width):
    shaped = values.reshape(values.shape[0], -1, head_width)
    scaled = shaped * lax.rsqrt(lax.optimization_barrier(jnp.mean(shaped * shaped, -1, keepdims=True)) + epsilon) * gain_vector
    return scaled.reshape(values.shape[0], -1)

def sigma_at(step_value):
    fraction = 1.0 - step_value.astype(jnp.float32) / STEPS
    return flow_shift * fraction / (1.0 + (flow_shift - 1.0) * fraction)

def pick_scale(scale_table, slot_index):
    slots = jnp.arange(scale_table.shape[0], dtype=jnp.int32)
    return jnp.sum(jnp.where(slots == slot_index, scale_table, 0.0))

def attend(queries, image_keys, image_values, text_keys, text_values, image_mask, text_mask, heads):
    head_width = queries.shape[1] // heads
    score_scale = head_width ** (-0.5)
    dims = (((1,), (1,)), ((), ()))

    def one_head(head_index):
        column_start = head_index * head_width
        query_part = lax.dynamic_slice_in_dim(queries, column_start, head_width, 1)
        key_part = lax.dynamic_slice_in_dim(image_keys, column_start, head_width, 1)
        value_part = lax.dynamic_slice_in_dim(image_values, column_start, head_width, 1)
        text_key_part = lax.dynamic_slice_in_dim(text_keys, column_start, head_width, 1)
        text_value_part = lax.dynamic_slice_in_dim(text_values, column_start, head_width, 1)
        image_scores = lax.dot_general(query_part, key_part, dims, preferred_element_type=jnp.float32) * score_scale
        text_scores = lax.dot_general(query_part, text_key_part, dims, preferred_element_type=jnp.float32) * score_scale
        image_weights = jnp.where(image_mask, jnp.exp(image_scores), 0.0)
        text_weights = jnp.where(text_mask, jnp.exp(text_scores), 0.0)
        denominator = lax.optimization_barrier(jnp.sum(image_weights, 1, keepdims=True)) + lax.optimization_barrier(jnp.sum(text_weights, 1, keepdims=True))
        image_weights = (image_weights / denominator).astype(jnp.bfloat16)
        text_weights = (text_weights / denominator).astype(jnp.bfloat16)
        return jnp.dot(image_weights, value_part, preferred_element_type=jnp.float32) + jnp.dot(text_weights, text_value_part, preferred_element_type=jnp.float32)
    stacked = lax.map(one_head, jnp.arange(heads, dtype=jnp.int32))
    return stacked.transpose(1, 0, 2).reshape(queries.shape[0], -1).astype(jnp.bfloat16)

def upsample_conv(latent_grid, upsample_weight, upsample_bias):
    upsampled = jnp.repeat(jnp.repeat(latent_grid, 2, 0), 2, 1)
    padded = jnp.pad(upsampled, ((1, 1), (1, 1), (0, 0)))
    height, breadth = (upsampled.shape[0], upsampled.shape[1])
    tap_list = [padded[row_shift:row_shift + height, col_shift:col_shift + breadth] for row_shift in range(3) for col_shift in range(3)]
    patches = jnp.concatenate(tap_list, -1).reshape(height * breadth, -1)
    product = jnp.dot(patches, upsample_weight, precision=highest).reshape(height, breadth, -1)
    return product + upsample_bias + upsampled

def reference(coarse_hidden, coarse_modulation, final_weight, coarse_latent, step_index, guide_index, guide_scales, upsample_weight, upsample_bias, embed_weight, embed_bias, fine_modulation, project_weight, query_gain, key_gain, text_keys, text_values, text_length, output_weight):
    velocities = []
    for branch in range(2):
        normed = layer_norm(coarse_hidden[branch].astype(jnp.float32))
        modulated = (normed * (1.0 + coarse_modulation[branch, 1]) + coarse_modulation[branch, 0]).astype(jnp.bfloat16)
        flat_velocity = jnp.dot(modulated.reshape(-1, D), final_weight, preferred_element_type=jnp.float32)
        velocities.append(flat_velocity.reshape(HA, WA * CHANNELS))
    guidance = pick_scale(guide_scales, guide_index[0])
    guided = velocities[1] + guidance * (velocities[0] - velocities[1])
    stepped = coarse_latent + (sigma_at(step_index[0] + 1) - sigma_at(step_index[0])) * guided
    fine_full = upsample_conv(stepped.reshape(HA, WA, CHANNELS), upsample_weight, upsample_bias)
    fine_latent = fine_full.reshape(HA, 2, 2 * WA * CHANNELS)
    fine_tokens = fine_full.reshape(HA, 4 * WA, CHANNELS)
    normed_text_keys = rms_heads(text_keys.astype(jnp.float32), key_gain, HEAD_DIM).astype(jnp.bfloat16)

    def state_row(tokens):
        fine_state = jnp.dot(tokens.astype(jnp.bfloat16), embed_weight, preferred_element_type=jnp.float32) + embed_bias
        fine_normed = (layer_norm(fine_state) * (1.0 + fine_modulation[1]) + fine_modulation[0]).astype(jnp.bfloat16)
        return (fine_state, fine_normed)

    def project_row(tokens):
        fine_normed = state_row(tokens)[1]
        projected = jnp.dot(fine_normed, project_weight, preferred_element_type=jnp.float32)
        queries = rms_heads(projected[:, :INNER], query_gain, HEAD_DIM).astype(jnp.bfloat16)
        keys = rms_heads(projected[:, INNER:2 * INNER], key_gain, HEAD_DIM).astype(jnp.bfloat16)
        values = projected[:, 2 * INNER:].astype(jnp.bfloat16)
        return (queries, keys, values)
    all_queries, all_keys, all_values = lax.map(project_row, fine_tokens)
    padded_keys = jnp.pad(all_keys, ((REACH, REACH), (0, 0), (0, 0)))
    padded_values = jnp.pad(all_values, ((REACH, REACH), (0, 0), (0, 0)))
    text_mask = (jnp.arange(TEXT, dtype=jnp.int32) < text_length[0])[None, :]
    key_offsets = jnp.arange((2 * REACH + 1) * 4 * WA, dtype=jnp.int32) // (4 * WA)

    def attend_row(row_index):
        window_keys = lax.dynamic_slice_in_dim(padded_keys, row_index, 2 * REACH + 1, 0).reshape(-1, INNER)
        window_values = lax.dynamic_slice_in_dim(padded_values, row_index, 2 * REACH + 1, 0).reshape(-1, INNER)
        global_rows = row_index - REACH + key_offsets
        valid = (global_rows >= 0) & (global_rows < HA)
        image_mask = jnp.broadcast_to(valid[None, :], (4 * WA, valid.shape[0]))
        queries = lax.dynamic_index_in_dim(all_queries, row_index, 0, keepdims=False)
        attended = attend(queries, window_keys, window_values, normed_text_keys, text_values, image_mask, text_mask, HEADS)
        fine_state = state_row(lax.dynamic_index_in_dim(fine_tokens, row_index, 0, keepdims=False))[0]
        output_part = jnp.dot(attended, output_weight, preferred_element_type=jnp.float32)
        return (fine_state + fine_modulation[2] * output_part).astype(jnp.bfloat16).reshape(2, 2 * WA, D)
    fine_hidden = lax.map(attend_row, jnp.arange(HA, dtype=jnp.int32))
    return (guided, fine_latent, fine_hidden)
```

```python
import jax
import jax.numpy as jnp
from jax import lax
from jax.sharding import PartitionSpec as P

HEADS = 8
STEPS = 50


epsilon = 1e-06
flow_shift = 5.0
highest = lax.Precision.HIGHEST


def from_partner(shard, axis, bit):
    return lax.ppermute(shard, axis, [(i, i ^ 1 << bit) for i in range(lax.axis_size(axis))])


def with_halo(block, sides, width):
    for axis, dim in sides:
        count = lax.axis_size(axis)
        forward = [(i, i + 1) for i in range(count - 1)]
        backward = [(target, source) for source, target in forward]
        low = lax.ppermute(
            lax.slice_in_dim(block, block.shape[dim] - width, None, axis=dim), axis, forward
        )
        high = lax.ppermute(lax.slice_in_dim(block, 0, width, axis=dim), axis, backward)
        block = jnp.concatenate([low, block, high], axis=dim)
    return block


def layer_norm(values):
    centred = values - jnp.mean(values, -1, keepdims=True)
    return centred * lax.rsqrt(jnp.mean(centred * centred, -1, keepdims=True) + epsilon)


def rms_heads(values, gain_vector, head_width):
    shaped = values.reshape(values.shape[0], -1, head_width)
    scaled = (
        shaped * lax.rsqrt(jnp.mean(shaped * shaped, -1, keepdims=True) + epsilon) * gain_vector
    )
    return scaled.reshape(values.shape[0], -1)


def sigma_at(step_value):
    fraction = 1.0 - step_value.astype(jnp.float32) / STEPS
    return flow_shift * fraction / (1.0 + (flow_shift - 1.0) * fraction)


def pick_scale(scale_table, slot_index):
    slots = jnp.arange(scale_table.shape[0], dtype=jnp.int32)
    return jnp.sum(jnp.where(slots == slot_index, scale_table, 0.0))


def attend(queries, image_keys, image_values, text_keys, text_values, image_mask, text_mask, heads):
    head_width = queries.shape[1] // heads
    score_scale = head_width ** (-0.5)
    dims = (((1,), (1,)), ((), ()))

    def one_head(head_index):
        column_start = head_index * head_width
        query_part = lax.dynamic_slice_in_dim(queries, column_start, head_width, 1)
        key_part = lax.dynamic_slice_in_dim(image_keys, column_start, head_width, 1)
        value_part = lax.dynamic_slice_in_dim(image_values, column_start, head_width, 1)
        text_key_part = lax.dynamic_slice_in_dim(text_keys, column_start, head_width, 1)
        text_value_part = lax.dynamic_slice_in_dim(text_values, column_start, head_width, 1)
        image_scores = (
            lax.dot_general(query_part, key_part, dims, preferred_element_type=jnp.float32)
            * score_scale
        )
        text_scores = (
            lax.dot_general(query_part, text_key_part, dims, preferred_element_type=jnp.float32)
            * score_scale
        )
        image_weights = jnp.where(image_mask, jnp.exp(image_scores), 0.0)
        text_weights = jnp.where(text_mask, jnp.exp(text_scores), 0.0)
        denominator = jnp.sum(image_weights, 1, keepdims=True) + jnp.sum(
            text_weights, 1, keepdims=True
        )
        image_weights = (image_weights / denominator).astype(jnp.bfloat16)
        text_weights = (text_weights / denominator).astype(jnp.bfloat16)
        return jnp.dot(image_weights, value_part, preferred_element_type=jnp.float32) + jnp.dot(
            text_weights, text_value_part, preferred_element_type=jnp.float32
        )

    stacked = lax.map(one_head, jnp.arange(heads, dtype=jnp.int32))
    return stacked.transpose(1, 0, 2).reshape(queries.shape[0], -1).astype(jnp.bfloat16)


def conv_rows(above, centre, below, upsample_weight, upsample_bias):
    tap_list = []
    for row_set in (above, centre, below):
        breadth = row_set.shape[1]
        padded = jnp.pad(row_set, ((0, 0), (1, 1), (0, 0)))
        for col_shift in range(3):
            tap_list.append(padded[:, col_shift : col_shift + breadth])
    patches = jnp.concatenate(tap_list, -1)
    flat_patches = patches.reshape(-1, patches.shape[-1])
    product = jnp.dot(flat_patches, upsample_weight, precision=highest).reshape(centre.shape)
    return product + upsample_bias + centre


def per_device(
    coarse_hidden,
    coarse_modulation,
    final_weight,
    coarse_latent,
    step_index,
    guide_index,
    guide_scales,
    upsample_weight,
    upsample_bias,
    embed_weight,
    embed_bias,
    fine_modulation,
    project_weight,
    query_gain,
    key_gain,
    text_keys,
    text_values,
    text_length,
    output_weight,
):
    row_count = coarse_hidden.shape[1]
    row_cells = coarse_hidden.shape[2]
    model_width = coarse_hidden.shape[3]
    channels = final_weight.shape[1]
    head_width = query_gain.shape[0]
    inner = project_weight.shape[1] // 3
    reach = max(row_count // 2, 1)
    branch = lax.axis_index("cfg")
    seq_index = lax.axis_index("seq")
    normed = layer_norm(coarse_hidden[0].astype(jnp.float32))
    modulated = (normed * (1.0 + coarse_modulation[0, 1]) + coarse_modulation[0, 0]).astype(
        jnp.bfloat16
    )
    velocity = jnp.dot(
        modulated.reshape(row_count * row_cells, model_width),
        final_weight,
        preferred_element_type=jnp.float32,
    ).reshape(row_count, row_cells * channels)
    partner = from_partner(velocity, "cfg", 0)
    conditional = jnp.where(branch == 0, velocity, partner)
    unconditional = jnp.where(branch == 0, partner, velocity)
    guidance = pick_scale(guide_scales, guide_index[0])
    guided = unconditional + guidance * (conditional - unconditional)
    stepped = coarse_latent + (sigma_at(step_index[0] + 1) - sigma_at(step_index[0])) * guided

    scale = 1.0 + fine_modulation[1]
    embed32 = embed_weight.astype(jnp.float32)
    embed_centred = embed32 - jnp.mean(embed32, -1, keepdims=True)
    bias_centred = embed_bias - jnp.mean(embed_bias)
    folded_left = jnp.concatenate(
        [embed_centred * scale, (bias_centred * scale)[None], fine_modulation[0][None]], 0
    )
    depth = project_weight.shape[0]
    device = branch * lax.axis_size("seq") + seq_index
    left_part = lax.dynamic_slice_in_dim(folded_left, device * depth, depth, 1)
    folded = lax.psum(
        jnp.dot(left_part, project_weight.astype(jnp.float32), precision=highest), ("cfg", "seq")
    )
    output_rows = lax.all_gather(output_weight.T, ("cfg", "seq"), axis=0, tiled=True)

    def embed_rows(grid_rows):
        grid_tokens = grid_rows.reshape(-1, channels).astype(jnp.bfloat16)
        centred = (
            jnp.dot(grid_tokens.astype(jnp.float32), embed_centred, precision=highest)
            + bias_centred
        )
        rstd = lax.rsqrt(jnp.mean(centred * centred, -1, keepdims=True) + epsilon)
        return (grid_tokens, rstd)

    def project(tokens_rstd, start, stop):
        tokens, rstd = tokens_rstd
        part = folded[:, start:stop]
        product = jnp.dot(tokens.astype(jnp.float32), part[:channels], precision=highest)
        return rstd * (product + part[channels]) + part[channels + 1]

    latent_grid = stepped.reshape(row_count, row_cells, channels)
    rim_width = reach + 1
    rimmed = with_halo(latent_grid, (("seq", 0),), rim_width)
    upsampled = jnp.repeat(jnp.repeat(rimmed, 2, 0), 2, 1)
    span = row_count + 2 * reach
    wide_grid = conv_rows(
        upsampled[1 : 1 + 2 * span],
        upsampled[2 : 2 + 2 * span],
        upsampled[3 : 3 + 2 * span],
        upsample_weight,
        upsample_bias,
    )
    grouped = wide_grid.reshape(span, 2, 2 * row_cells, channels)
    fine_grid = lax.dynamic_index_in_dim(
        grouped[reach : reach + row_count], branch, 1, keepdims=False
    )
    own = embed_rows(fine_grid)
    fine_state = jnp.dot(own[0], embed_weight, preferred_element_type=jnp.float32) + embed_bias
    around = embed_rows(wide_grid)
    token_count = own[0].shape[0]
    query_sum = project(own, 0, inner)
    key_sum = project(around, inner, 2 * inner)
    value_sum = project(around, 2 * inner, 3 * inner)
    queries = rms_heads(query_sum, query_gain, head_width).astype(jnp.bfloat16)
    keys = rms_heads(key_sum, key_gain, head_width).astype(jnp.bfloat16)
    values = value_sum.astype(jnp.bfloat16)
    image_keys, image_values = (keys, values)
    normed_text_keys = rms_heads(text_keys.astype(jnp.float32), key_gain, head_width).astype(
        jnp.bfloat16
    )
    key_count = image_keys.shape[0]
    query_rows = jnp.arange(token_count, dtype=jnp.int32) // (2 * row_cells)
    key_rows = jnp.arange(key_count, dtype=jnp.int32) // (4 * row_cells)
    distance = key_rows[None, :] - query_rows[:, None]
    global_rows = seq_index * row_count + key_rows - reach
    row_valid = (global_rows >= 0) & (global_rows < row_count * lax.axis_size("seq"))
    image_mask = (distance >= 0) & (distance <= 2 * reach) & row_valid[None, :]
    text_mask = (jnp.arange(text_keys.shape[0], dtype=jnp.int32) < text_length[0])[None, :]
    attended = attend(
        queries,
        image_keys,
        image_values,
        normed_text_keys,
        text_values,
        image_mask,
        text_mask,
        HEADS,
    )
    output_part = lax.dot_general(
        attended, output_rows, (((1,), (1,)), ((), ())), preferred_element_type=jnp.float32
    )
    fine_hidden = (fine_state + fine_modulation[2] * output_part).astype(jnp.bfloat16)
    fine_hidden = fine_hidden.reshape(row_count, 1, 2 * row_cells, model_width)
    fine_latent = fine_grid.reshape(row_count, 1, 2 * row_cells * channels)
    return (guided, fine_latent, fine_hidden)


def solution(mesh):
    placed = (
        P("cfg", "seq", None, None),
        P("cfg", None, None),
        P(),
        P("seq", None),
        P(),
        P(),
        P(),
        P(),
        P(),
        P(),
        P(),
        P(),
        P(("cfg", "seq"), None),
        P(),
        P(),
        P(),
        P(),
        P(),
        P(None, ("cfg", "seq")),
    )
    return jax.shard_map(
        per_device,
        mesh=mesh,
        in_specs=placed,
        out_specs=(P("seq", None), P("seq", "cfg", None), P("seq", "cfg", None, None)),
        check_vma=False,
    )
```

```python
import jax
import jax.numpy as jnp
from jax import lax
from jax.experimental import pallas as pl
from jax.experimental.pallas import tpu as pltpu
from jax.sharding import PartitionSpec as P

HEADS = 8
STEPS = 50


epsilon = 1e-06
flow_shift = 5.0
highest = lax.Precision.HIGHEST


MESH = pl.DeviceIdType.MESH


def remote(src, dst, send_sem, recv_sem, device):
    return pltpu.make_async_remote_copy(
        src_ref=src, dst_ref=dst, send_sem=send_sem, recv_sem=recv_sem,
        device_id=device, device_id_type=MESH,
    )


class Place:
    def __init__(self):
        self.x_lo = lax.axis_index("cfg")
        seq = lax.axis_index("seq")
        self.seq = seq
        self.core = lax.rem(seq, 2)
        self.x_hi = lax.rem(lax.div(seq, 2), 2)
        self.z = lax.rem(lax.div(seq, 4), 8)
        self.y = lax.div(seq, 32)
        self.x = self.x_hi * 2 + self.x_lo
        self.member = self.x_lo * 4 + self.x_hi * 2 + self.core
        self.line = lax.div(seq, 4)

    def at(self, x=None, y=None, z=None, core=None):
        x = self.x if x is None else x
        y = self.y if y is None else y
        z = self.z if z is None else z
        core = self.core if core is None else core
        return (lax.rem(x, 2), ((y * 8 + z) * 2 + lax.div(x, 2)) * 2 + core)

    def member_device(self, member):
        return (lax.div(member, 4), self.line * 4 + lax.rem(member, 4))


def greet(place):
    barrier = pltpu.get_barrier_semaphore()
    partners = [place.member_device(lax.rem(place.member + d, 8)) for d in range(1, 8)]
    partners += [place.at(y=lax.rem(place.y + d, 4)) for d in range(1, 4)]
    partners += [place.at(z=lax.rem(place.z + d, 8)) for d in range(1, 8)]
    for partner in partners:
        pl.semaphore_signal(barrier, inc=1, device_id=partner, device_id_type=MESH)
    return barrier, len(partners)


def comm_kernel(
    weight_ref, output_ref, embed_ref, bias_ref, modulation_ref,
    folded_out, rows_out,
    left, own_rows, group_rows, partial, z_parts, y_parts, folded,
    out_chunk, out_sibling, out_rows,
    a_send, a_recv, rz_send, rz_recv, ry_send, ry_recv, gz_send, gz_recv, gx_send, gx_recv,
    s_send, s_recv, wz_send, wz_recv, wp_send, wp_recv, wq_send, wq_recv, ws_send, ws_recv,
):
    place = Place()
    core, z, y, member = place.core, place.z, place.y, place.member
    group_rows[...] = jnp.zeros_like(group_rows)
    barrier, count = greet(place)
    for part in range(8):
        own_rows[part] = weight_ref[:, part * 384 : (part + 1) * 384].astype(jnp.float32)
    eye = (
        lax.broadcasted_iota(jnp.int32, (8, 8), 0) == lax.broadcasted_iota(jnp.int32, (8, 8), 1)
    ).astype(jnp.bfloat16)
    turned = lax.dot_general(
        eye, output_ref[...], (((1,), (1,)), ((), ())), preferred_element_type=jnp.float32
    )
    out_chunk[0] = turned[:, :512]
    out_chunk[1] = turned[:, 512:]
    pl.semaphore_wait(barrier, count)
    sibling = place.at(core=1 - core)
    swap = remote(out_chunk.at[1 - core], out_sibling, s_send, s_recv, sibling)
    swap.start()
    quarter = lax.rem(place.line, 4)
    spread = []
    for d in range(1, 8):
        target = lax.rem(member + d, 8)
        copy = remote(
            own_rows.at[target],
            group_rows.at[place.x_lo, quarter, place.x_hi * 2 + core],
            a_send.at[d], a_recv.at[d], place.member_device(target),
        )
        copy.start()
        spread.append(copy)
    group_rows[place.x_lo, quarter, place.x_hi * 2 + core] = own_rows[member]
    embed = embed_ref[...].astype(jnp.float32)
    scale = 1.0 + modulation_ref[1:2, :]
    left[0:32] = (embed - jnp.mean(embed, -1, keepdims=True)) * scale
    bias = bias_ref[...]
    left[32:40] = jnp.concatenate(
        [
            (bias - jnp.mean(bias, -1, keepdims=True)) * scale,
            modulation_ref[0:1, :],
            jnp.zeros((6, left.shape[1]), jnp.float32),
        ],
        0,
    )
    swap.wait()
    mine, other = out_chunk[core], out_sibling[...]
    first = core == 0
    out_rows[core, place.x_lo, y, z, place.x_hi] = jnp.concatenate(
        [jnp.where(first, mine, other), jnp.where(first, other, mine)], 0
    ).astype(jnp.bfloat16)
    along_z = []
    for d in range(1, 8):
        slot = out_rows.at[core, place.x_lo, y, z, place.x_hi]
        copy = remote(
            slot, slot, wz_send.at[d], wz_recv.at[d], place.at(z=lax.rem(z + d, 8))
        )
        copy.start()
        along_z.append(copy)
    for copy in spread:
        copy.wait()
    column = pl.multiple_of(lax.div(place.line, 4) * 128, 128)
    total = jnp.dot(
        left[:, pl.ds(column, 128)], group_rows[0].reshape(128, 384), precision=highest
    ) + jnp.dot(
        left[:, pl.ds(1024 + column, 128)], group_rows[1].reshape(128, 384), precision=highest
    )
    for row in range(5):
        for block in range(3):
            partial[row * 3 + block] = total[
                row * 8 : row * 8 + 8, block * 128 : block * 128 + 128
            ]
    partial[15] = jnp.zeros((8, 128), jnp.float32)
    scatter = []
    for d in range(1, 8):
        target = lax.rem(z + d, 8)
        copy = remote(
            partial.at[pl.ds(target * 2, 2)], z_parts.at[z],
            rz_send.at[d], rz_recv.at[d], place.at(z=target),
        )
        copy.start()
        scatter.append(copy)
    z_parts[z] = partial[pl.ds(z * 2, 2)]
    for copy in along_z:
        copy.wait()
    first_at = y * (1 - core) + place.x * core
    second_at = place.x * (1 - core) + y * core

    def piece(p, q):
        px, py = q * (1 - core) + p * core, p * (1 - core) + q * core
        return out_rows.at[core, lax.rem(px, 2), py, :, lax.div(px, 2)]

    def piece_device(p, q):
        return place.at(x=q * (1 - core) + p * core, y=p * (1 - core) + q * core)

    along_p = []
    for d in range(1, 4):
        slot = piece(first_at, second_at)
        copy = remote(
            slot, slot, wp_send.at[d], wp_recv.at[d],
            piece_device(lax.rem(first_at + d, 4), second_at),
        )
        copy.start()
        along_p.append(copy)
    along_q = []

    def send_q(e):
        for d in range(1, 4):
            slot = piece(lax.rem(first_at + 4 - e, 4), second_at)
            copy = remote(
                slot, slot, wq_send.at[e, d], wq_recv.at[e, d],
                piece_device(first_at, lax.rem(second_at + d, 4)),
            )
            copy.start()
            along_q.append(copy)

    to_sibling = []

    def send_sibling(e, d):
        slot = piece(lax.rem(first_at + 4 - e, 4), lax.rem(second_at + 4 - d, 4))
        copy = remote(slot, slot, ws_send.at[e, d], ws_recv.at[e, d], sibling)
        copy.start()
        to_sibling.append(copy)

    send_q(0)
    send_sibling(0, 0)
    for copy in scatter:
        copy.wait()
    y_parts[y] = jnp.sum(z_parts[...], 0)
    over_y = []
    for d in range(1, 4):
        copy = remote(
            y_parts.at[y], y_parts.at[y], ry_send.at[d], ry_recv.at[d],
            place.at(y=lax.rem(y + d, 4)),
        )
        copy.start()
        over_y.append(copy)
    for copy in over_y:
        copy.wait()
    folded[member, pl.ds(z * 2, 2)] = jnp.sum(y_parts[...], 0)
    gather_z = []
    for d in range(1, 8):
        slot = folded.at[member, pl.ds(z * 2, 2)]
        copy = remote(slot, slot, gz_send.at[d], gz_recv.at[d], place.at(z=lax.rem(z + d, 8)))
        copy.start()
        gather_z.append(copy)
    for e in range(1, 4):
        along_p[e - 1].wait()
        send_q(e)
        send_sibling(e, 0)
    for copy in gather_z:
        copy.wait()
    gather_x = []
    for d in range(1, 8):
        slot = folded.at[member]
        copy = remote(
            slot, slot, gx_send.at[d], gx_recv.at[d],
            place.member_device(lax.rem(member + d, 8)),
        )
        copy.start()
        gather_x.append(copy)
    for copy in gather_x:
        copy.wait()
    for e in range(4):
        for d in range(1, 4):
            along_q[e * 3 + d - 1].wait()
            send_sibling(e, d)
    for copy in to_sibling:
        copy.wait()
    folded_out[...] = folded[...]
    rows_out[...] = out_rows[...]


def gather_parts(project_weight, output_weight, embed_weight, embed_bias, fine_modulation):
    dma = pltpu.SemaphoreType.DMA
    pairs = [(8,), (8,), (4,), (8,), (8,)]
    sems = []
    for shape in pairs:
        sems += [dma(shape), dma(shape)]
    sems += [dma, dma]
    for shape in [(8,), (4,), (4, 4), (4, 4)]:
        sems += [dma(shape), dma(shape)]
    vmem = pl.BlockSpec(memory_space=pltpu.VMEM)
    rows_shape = (2, 2, 4, 8, 2, 16, 512)
    folded, rows = pl.pallas_call(
        comm_kernel,
        out_shape=(
            jax.ShapeDtypeStruct((8, 16, 8, 128), jnp.float32),
            jax.ShapeDtypeStruct(rows_shape, jnp.bfloat16),
        ),
        in_specs=[vmem] * 5,
        out_specs=(vmem, vmem),
        scratch_shapes=[
            pltpu.VMEM((40, 2048), jnp.float32),
            pltpu.VMEM((8, 8, 384), jnp.float32),
            pltpu.VMEM((2, 4, 4, 8, 384), jnp.float32),
            pltpu.VMEM((16, 8, 128), jnp.float32),
            pltpu.VMEM((8, 2, 8, 128), jnp.float32),
            pltpu.VMEM((4, 2, 8, 128), jnp.float32),
            pltpu.VMEM((8, 16, 8, 128), jnp.float32),
            pltpu.VMEM((2, 8, 512), jnp.float32),
            pltpu.VMEM((8, 512), jnp.float32),
            pltpu.VMEM(rows_shape, jnp.bfloat16),
        ] + sems,
        compiler_params=pltpu.CompilerParams(
            collective_id=0, has_side_effects=True, vmem_limit_bytes=48 * 1024 * 1024
        ),
    )(project_weight, output_weight, embed_weight, embed_bias[None], fine_modulation)
    matrix = (
        folded[:, :15].reshape(8, 5, 3, 8, 128).transpose(1, 3, 0, 2, 4).reshape(40, 3072)
    )
    output_rows = rows.transpose(1, 2, 3, 4, 5, 0, 6).reshape(2048, 1024)
    return matrix, output_rows


def from_partner(shard, axis, bit):
    return lax.ppermute(shard, axis, [(i, i ^ 1 << bit) for i in range(lax.axis_size(axis))])


def with_halo(block, sides, width):
    for axis, dim in sides:
        count = lax.axis_size(axis)
        forward = [(i, i + 1) for i in range(count - 1)]
        backward = [(target, source) for source, target in forward]
        low = lax.ppermute(
            lax.slice_in_dim(block, block.shape[dim] - width, None, axis=dim), axis, forward
        )
        high = lax.ppermute(lax.slice_in_dim(block, 0, width, axis=dim), axis, backward)
        block = jnp.concatenate([low, block, high], axis=dim)
    return block


def layer_norm(values):
    centred = values - jnp.mean(values, -1, keepdims=True)
    return centred * lax.rsqrt(jnp.mean(centred * centred, -1, keepdims=True) + epsilon)


def rms_heads(values, gain_vector, head_width):
    shaped = values.reshape(values.shape[0], -1, head_width)
    scaled = (
        shaped * lax.rsqrt(jnp.mean(shaped * shaped, -1, keepdims=True) + epsilon) * gain_vector
    )
    return scaled.reshape(values.shape[0], -1)


def sigma_at(step_value):
    fraction = 1.0 - step_value.astype(jnp.float32) / STEPS
    return flow_shift * fraction / (1.0 + (flow_shift - 1.0) * fraction)


def pick_scale(scale_table, slot_index):
    slots = jnp.arange(scale_table.shape[0], dtype=jnp.int32)
    return jnp.sum(jnp.where(slots == slot_index, scale_table, 0.0))


def attend(queries, image_keys, image_values, text_keys, text_values, image_mask, text_mask, heads):
    head_width = queries.shape[1] // heads
    score_scale = head_width ** (-0.5)
    dims = (((1,), (1,)), ((), ()))

    def one_head(head_index):
        column_start = head_index * head_width
        query_part = lax.dynamic_slice_in_dim(queries, column_start, head_width, 1)
        key_part = lax.dynamic_slice_in_dim(image_keys, column_start, head_width, 1)
        value_part = lax.dynamic_slice_in_dim(image_values, column_start, head_width, 1)
        text_key_part = lax.dynamic_slice_in_dim(text_keys, column_start, head_width, 1)
        text_value_part = lax.dynamic_slice_in_dim(text_values, column_start, head_width, 1)
        image_scores = (
            lax.dot_general(query_part, key_part, dims, preferred_element_type=jnp.float32)
            * score_scale
        )
        text_scores = (
            lax.dot_general(query_part, text_key_part, dims, preferred_element_type=jnp.float32)
            * score_scale
        )
        image_weights = jnp.where(image_mask, jnp.exp(image_scores), 0.0)
        text_weights = jnp.where(text_mask, jnp.exp(text_scores), 0.0)
        denominator = jnp.sum(image_weights, 1, keepdims=True) + jnp.sum(
            text_weights, 1, keepdims=True
        )
        image_weights = (image_weights / denominator).astype(jnp.bfloat16)
        text_weights = (text_weights / denominator).astype(jnp.bfloat16)
        return jnp.dot(image_weights, value_part, preferred_element_type=jnp.float32) + jnp.dot(
            text_weights, text_value_part, preferred_element_type=jnp.float32
        )

    stacked = lax.map(one_head, jnp.arange(heads, dtype=jnp.int32))
    return stacked.transpose(1, 0, 2).reshape(queries.shape[0], -1).astype(jnp.bfloat16)


def conv_rows(above, centre, below, upsample_weight, upsample_bias):
    tap_list = []
    for row_set in (above, centre, below):
        breadth = row_set.shape[1]
        padded = jnp.pad(row_set, ((0, 0), (1, 1), (0, 0)))
        for col_shift in range(3):
            tap_list.append(padded[:, col_shift : col_shift + breadth])
    patches = jnp.concatenate(tap_list, -1)
    flat_patches = patches.reshape(-1, patches.shape[-1])
    product = jnp.dot(flat_patches, upsample_weight, precision=highest).reshape(centre.shape)
    return product + upsample_bias + centre


def per_device(
    coarse_hidden,
    coarse_modulation,
    final_weight,
    coarse_latent,
    step_index,
    guide_index,
    guide_scales,
    upsample_weight,
    upsample_bias,
    embed_weight,
    embed_bias,
    fine_modulation,
    project_weight,
    query_gain,
    key_gain,
    text_keys,
    text_values,
    text_length,
    output_weight,
):
    row_count = coarse_hidden.shape[1]
    row_cells = coarse_hidden.shape[2]
    model_width = coarse_hidden.shape[3]
    channels = final_weight.shape[1]
    head_width = query_gain.shape[0]
    inner = project_weight.shape[1] // 3
    reach = max(row_count // 2, 1)
    branch = lax.axis_index("cfg")
    seq_index = lax.axis_index("seq")
    normed = layer_norm(coarse_hidden[0].astype(jnp.float32))
    modulated = (normed * (1.0 + coarse_modulation[0, 1]) + coarse_modulation[0, 0]).astype(
        jnp.bfloat16
    )
    velocity = jnp.dot(
        modulated.reshape(row_count * row_cells, model_width),
        final_weight,
        preferred_element_type=jnp.float32,
    ).reshape(row_count, row_cells * channels)
    partner = from_partner(velocity, "cfg", 0)
    conditional = jnp.where(branch == 0, velocity, partner)
    unconditional = jnp.where(branch == 0, partner, velocity)
    guidance = pick_scale(guide_scales, guide_index[0])
    guided = unconditional + guidance * (conditional - unconditional)
    stepped = coarse_latent + (sigma_at(step_index[0] + 1) - sigma_at(step_index[0])) * guided

    embed32 = embed_weight.astype(jnp.float32)
    embed_centred = embed32 - jnp.mean(embed32, -1, keepdims=True)
    bias_centred = embed_bias - jnp.mean(embed_bias)
    folded, output_rows = gather_parts(
        project_weight, output_weight, embed_weight, embed_bias, fine_modulation
    )

    def embed_rows(grid_rows):
        grid_tokens = grid_rows.reshape(-1, channels).astype(jnp.bfloat16)
        centred = (
            jnp.dot(grid_tokens.astype(jnp.float32), embed_centred, precision=highest)
            + bias_centred
        )
        rstd = lax.rsqrt(jnp.mean(centred * centred, -1, keepdims=True) + epsilon)
        return (grid_tokens, rstd)

    def project(tokens_rstd, start, stop):
        tokens, rstd = tokens_rstd
        part = folded[:, start:stop]
        product = jnp.dot(tokens.astype(jnp.float32), part[:channels], precision=highest)
        return rstd * (product + part[channels]) + part[channels + 1]

    latent_grid = stepped.reshape(row_count, row_cells, channels)
    rim_width = reach + 1
    rimmed = with_halo(latent_grid, (("seq", 0),), rim_width)
    upsampled = jnp.repeat(jnp.repeat(rimmed, 2, 0), 2, 1)
    span = row_count + 2 * reach
    wide_grid = conv_rows(
        upsampled[1 : 1 + 2 * span],
        upsampled[2 : 2 + 2 * span],
        upsampled[3 : 3 + 2 * span],
        upsample_weight,
        upsample_bias,
    )
    grouped = wide_grid.reshape(span, 2, 2 * row_cells, channels)
    fine_grid = lax.dynamic_index_in_dim(
        grouped[reach : reach + row_count], branch, 1, keepdims=False
    )
    own = embed_rows(fine_grid)
    fine_state = jnp.dot(own[0], embed_weight, preferred_element_type=jnp.float32) + embed_bias
    around = embed_rows(wide_grid)
    token_count = own[0].shape[0]
    query_sum = project(own, 0, inner)
    key_sum = project(around, inner, 2 * inner)
    value_sum = project(around, 2 * inner, 3 * inner)
    queries = rms_heads(query_sum, query_gain, head_width).astype(jnp.bfloat16)
    keys = rms_heads(key_sum, key_gain, head_width).astype(jnp.bfloat16)
    values = value_sum.astype(jnp.bfloat16)
    image_keys, image_values = (keys, values)
    normed_text_keys = rms_heads(text_keys.astype(jnp.float32), key_gain, head_width).astype(
        jnp.bfloat16
    )
    key_count = image_keys.shape[0]
    query_rows = jnp.arange(token_count, dtype=jnp.int32) // (2 * row_cells)
    key_rows = jnp.arange(key_count, dtype=jnp.int32) // (4 * row_cells)
    distance = key_rows[None, :] - query_rows[:, None]
    global_rows = seq_index * row_count + key_rows - reach
    row_valid = (global_rows >= 0) & (global_rows < row_count * lax.axis_size("seq"))
    image_mask = (distance >= 0) & (distance <= 2 * reach) & row_valid[None, :]
    text_mask = (jnp.arange(text_keys.shape[0], dtype=jnp.int32) < text_length[0])[None, :]
    attended = attend(
        queries,
        image_keys,
        image_values,
        normed_text_keys,
        text_values,
        image_mask,
        text_mask,
        HEADS,
    )
    output_part = lax.dot_general(
        attended, output_rows, (((1,), (1,)), ((), ())), preferred_element_type=jnp.float32
    )
    fine_hidden = (fine_state + fine_modulation[2] * output_part).astype(jnp.bfloat16)
    fine_hidden = fine_hidden.reshape(row_count, 1, 2 * row_cells, model_width)
    fine_latent = fine_grid.reshape(row_count, 1, 2 * row_cells * channels)
    return (guided, fine_latent, fine_hidden)


def solution(mesh):
    placed = (
        P("cfg", "seq", None, None),
        P("cfg", None, None),
        P(),
        P("seq", None),
        P(),
        P(),
        P(),
        P(),
        P(),
        P(),
        P(),
        P(),
        P(("cfg", "seq"), None),
        P(),
        P(),
        P(),
        P(),
        P(),
        P(None, ("cfg", "seq")),
    )
    return jax.shard_map(
        per_device,
        mesh=mesh,
        in_specs=placed,
        out_specs=(P("seq", None), P("seq", "cfg", None), P("seq", "cfg", None, None)),
        check_vma=False,
    )
```

```python
import jax
import jax.numpy as jnp
from jax import lax
from jax.experimental import pallas as pl
from jax.experimental.pallas import tpu as pltpu
from jax.sharding import PartitionSpec as P

HEADS = 8
STEPS = 50
MESH = pl.DeviceIdType.MESH
LOG2E = 1.4426950408889634

epsilon = 1e-06
flow_shift = 5.0
highest = lax.Precision.HIGHEST
f32 = jnp.float32
bf16 = jnp.bfloat16

def remote(src, dst, send_sem, recv_sem, device):
    return pltpu.make_async_remote_copy(
        src_ref=src, dst_ref=dst, send_sem=send_sem, recv_sem=recv_sem,
        device_id=device, device_id_type=MESH,
    )


class Place:
    def __init__(self):
        self.x_lo = lax.axis_index("cfg")
        seq = lax.axis_index("seq")
        self.seq = seq
        self.core = lax.rem(seq, 2)
        self.x_hi = lax.rem(lax.div(seq, 2), 2)
        self.z = lax.rem(lax.div(seq, 4), 8)
        self.y = lax.div(seq, 32)
        self.x = self.x_hi * 2 + self.x_lo
        self.member = self.x_lo * 4 + self.x_hi * 2 + self.core
        self.line = lax.div(seq, 4)

    def at(self, x=None, y=None, z=None, core=None):
        x = self.x if x is None else x
        y = self.y if y is None else y
        z = self.z if z is None else z
        core = self.core if core is None else core
        return (lax.rem(x, 2), ((y * 8 + z) * 2 + lax.div(x, 2)) * 2 + core)

    def member_device(self, member):
        return (lax.div(member, 4), self.line * 4 + lax.rem(member, 4))


def greet(place):
    barrier = pltpu.get_barrier_semaphore()
    partners = [place.member_device(lax.rem(place.member + d, 8)) for d in range(1, 8)]
    partners += [place.at(y=lax.rem(place.y + d, 4)) for d in range(1, 4)]
    partners += [place.at(z=lax.rem(place.z + d, 8)) for d in range(1, 8)]
    for other in (lax.rem(place.seq + 1, 128), lax.rem(place.seq + 127, 128)):
        partners += [(place.x_lo, other), (1 - place.x_lo, other)]
    for partner in partners:
        pl.semaphore_signal(barrier, inc=1, device_id=partner, device_id_type=MESH)
    return barrier, len(partners)

def layer_norm(values):
    centred = values - jnp.mean(values, -1, keepdims=True)
    return centred * lax.rsqrt(jnp.mean(centred * centred, -1, keepdims=True) + epsilon)


def sigma_at(step_value):
    fraction = 1.0 - step_value / STEPS
    return flow_shift * fraction / (1.0 + (flow_shift - 1.0) * fraction)


def split_two(values):
    high = values.astype(bf16).astype(f32)
    return high, values - high


def dot_nt(a, b):
    return lax.dot_general(a, b, (((1,), (1,)), ((), ())), preferred_element_type=f32)


def dot_nn(a, b):
    return jnp.dot(a, b, preferred_element_type=f32)


TAPS = (((0,), (1, 2), ()), ((), (0, 1), (2,)))


def coarse_weights(up_ref, offset):
    eye = (
        lax.broadcasted_iota(jnp.int32, (32, 32), 0) == lax.broadcasted_iota(jnp.int32, (32, 32), 1)
    ).astype(f32)
    bands = []
    for column in range(3):
        blocks = []
        for a in range(2):
            for c in range(2):
                block = eye if offset == 1 and column == 1 else jnp.zeros((32, 32), f32)
                for r in TAPS[a][offset]:
                    for k in TAPS[c][column]:
                        tap = (3 * r + k) * 32
                        block = block + up_ref[tap : tap + 32, :]
                blocks.append(block)
        bands.append(jnp.concatenate(blocks, 1))
    return jnp.concatenate(bands, 0)


def kernel(
    step_ref, guide_ref, length_ref,
    hidden_ref, coarse_mod_ref, final_ref, latent_ref, scales_ref, up_ref, up_bias_ref,
    embed_ref, bias_ref, modulation_ref, weight_ref, query_gain_ref, key_gain_ref,
    text_keys_ref, text_values_ref, output_ref,
    guided_out, fine_out, hidden_out,
    left, own_rows, group_rows, partial, z_parts, y_parts, folded,
    out_chunk, out_sibling, out_rows,
    velocity, latents, cells, grid_cells, pairs, query_tokens, key_tokens,
    centred_right, state_right, folded_right, shift_row,
    query_buf, key_buf, value_buf, text_key_buf, text_value_buf, ones_buf, attended,
    *sems,
):
    (
        a_send, a_recv, rz_send, rz_recv, ry_send, ry_recv, gz_send, gz_recv, gx_send, gx_recv,
        s_send, s_recv, wz_send, wz_recv, wp_send, wp_recv, wq_send, wq_recv, ws_send, ws_recv,
        v_send, v_recv, l_send, l_recv,
    ) = sems
    place = Place()
    core, z, y, member, seq, branch = (
        place.core, place.z, place.y, place.member, place.seq, place.x_lo
    )
    group_rows[...] = jnp.zeros_like(group_rows)
    barrier, count = greet(place)
    for part in range(8):
        own_rows[part] = weight_ref[:, part * 384 : (part + 1) * 384].astype(f32)
    eye = (
        lax.broadcasted_iota(jnp.int32, (8, 8), 0) == lax.broadcasted_iota(jnp.int32, (8, 8), 1)
    ).astype(bf16)
    turned = dot_nt(eye, output_ref[...])
    out_chunk[0] = turned[:, :512]
    out_chunk[1] = turned[:, 512:]
    for m in range(32):
        latents[1, m : m + 1, :] = latent_ref[m // 16 : m // 16 + 1, m % 16 * 128 : m % 16 * 128 + 128]
    pl.semaphore_wait(barrier, count)
    sibling = place.at(core=1 - core)
    swap = remote(out_chunk.at[1 - core], out_sibling, s_send, s_recv, sibling)
    swap.start()
    quarter = lax.rem(place.line, 4)
    spread = []
    for d in range(1, 8):
        target = lax.rem(member + d, 8)
        copy = remote(
            own_rows.at[target],
            group_rows.at[place.x_lo, quarter, place.x_hi * 2 + core],
            a_send.at[d], a_recv.at[d], place.member_device(target),
        )
        copy.start()
        spread.append(copy)
    after, before = lax.rem(seq + 1, 128), lax.rem(seq + 127, 128)
    latent_copies = [
        remote(latents.at[1], latents.at[0], l_send.at[0], l_recv.at[0], (branch, after)),
        remote(latents.at[1], latents.at[2], l_send.at[1], l_recv.at[1], (branch, before)),
    ]
    for copy in latent_copies:
        copy.start()
    group_rows[place.x_lo, quarter, place.x_hi * 2 + core] = own_rows[member]

    embed = embed_ref[...].astype(f32)
    scale = 1.0 + modulation_ref[1:2, :]
    embed_centred = embed - jnp.mean(embed, -1, keepdims=True)
    bias = bias_ref[...]
    bias_centred = bias - jnp.mean(bias, -1, keepdims=True)
    width = embed.shape[1]
    left[0:32] = embed_centred * scale
    left[32:40] = jnp.concatenate(
        [bias_centred * scale, modulation_ref[0:1, :], jnp.zeros((6, width), f32)], 0
    )

    swap.wait()
    mine, other = out_chunk[core], out_sibling[...]
    first = core == 0
    out_rows[core, place.x_lo, y, z, place.x_hi] = jnp.concatenate(
        [jnp.where(first, mine, other), jnp.where(first, other, mine)], 0
    ).astype(bf16)
    along_z = []
    for d in range(1, 8):
        slot = out_rows.at[core, place.x_lo, y, z, place.x_hi]
        copy = remote(slot, slot, wz_send.at[d], wz_recv.at[d], place.at(z=lax.rem(z + d, 8)))
        copy.start()
        along_z.append(copy)

    for copy in spread:
        copy.wait()
    column = pl.multiple_of(lax.div(place.line, 4) * 128, 128)
    total = jnp.dot(
        left[:, pl.ds(column, 128)], group_rows[0].reshape(128, 384), precision=highest
    ) + jnp.dot(
        left[:, pl.ds(1024 + column, 128)], group_rows[1].reshape(128, 384), precision=highest
    )
    for row in range(5):
        for block in range(3):
            partial[row * 3 + block] = total[
                row * 8 : row * 8 + 8, block * 128 : block * 128 + 128
            ]
    partial[15] = jnp.zeros((8, 128), f32)
    scatter = []
    for d in range(1, 8):
        target = lax.rem(z + d, 8)
        copy = remote(
            partial.at[pl.ds(target * 2, 2)], z_parts.at[z],
            rz_send.at[d], rz_recv.at[d], place.at(z=target),
        )
        copy.start()
        scatter.append(copy)
    z_parts[z] = partial[pl.ds(z * 2, 2)]

    for row in range(2):
        modulated = (
            layer_norm(hidden_ref[row * 64 : row * 64 + 64, :].astype(f32))
            * (1.0 + coarse_mod_ref[1:2, :])
            + coarse_mod_ref[0:1, :]
        ).astype(bf16)
        cells[row * 64 : row * 64 + 64, :] = dot_nn(modulated, final_ref[...])
    velocity[branch, 1] = jnp.concatenate(
        [cells[pl.ds(c, 32, stride=4), :] for c in range(4)], 1
    )
    velocity_copies = []
    targets = [
        ((1 - branch, seq), 1), ((branch, after), 0), ((1 - branch, after), 0),
        ((branch, before), 2), ((1 - branch, before), 2),
    ]
    for d, (target, slot) in enumerate(targets):
        copy = remote(
            velocity.at[branch, 1], velocity.at[branch, slot], v_send.at[d], v_recv.at[d], target
        )
        copy.start()
        velocity_copies.append(copy)

    for copy in along_z:
        copy.wait()
    first_at = y * (1 - core) + place.x * core
    second_at = place.x * (1 - core) + y * core

    def piece(p, q):
        px, py = q * (1 - core) + p * core, p * (1 - core) + q * core
        return out_rows.at[core, lax.rem(px, 2), py, :, lax.div(px, 2)]

    def piece_device(p, q):
        return place.at(x=q * (1 - core) + p * core, y=p * (1 - core) + q * core)

    along_p = []
    for d in range(1, 4):
        slot = piece(first_at, second_at)
        copy = remote(
            slot, slot, wp_send.at[d], wp_recv.at[d],
            piece_device(lax.rem(first_at + d, 4), second_at),
        )
        copy.start()
        along_p.append(copy)
    along_q = []

    def send_q(e):
        for d in range(1, 4):
            slot = piece(lax.rem(first_at + 4 - e, 4), second_at)
            copy = remote(
                slot, slot, wq_send.at[e, d], wq_recv.at[e, d],
                piece_device(first_at, lax.rem(second_at + d, 4)),
            )
            copy.start()
            along_q.append(copy)

    to_sibling = []

    def send_sibling(e, d):
        slot = piece(lax.rem(first_at + 4 - e, 4), lax.rem(second_at + 4 - d, 4))
        copy = remote(slot, slot, ws_send.at[e, d], ws_recv.at[e, d], sibling)
        copy.start()
        to_sibling.append(copy)

    send_q(0)
    send_sibling(0, 0)

    for copy in scatter:
        copy.wait()
    y_parts[y] = jnp.sum(z_parts[...], 0)
    over_y = []
    for d in range(1, 4):
        copy = remote(
            y_parts.at[y], y_parts.at[y], ry_send.at[d], ry_recv.at[d],
            place.at(y=lax.rem(y + d, 4)),
        )
        copy.start()
        over_y.append(copy)

    lane_zeros = jnp.zeros((61, width), f32)
    high, low = split_two(embed_centred)
    bias_high, bias_low = split_two(bias_centred)
    centred_right[...] = jnp.concatenate(
        [high, low, bias_high, bias_low, jnp.zeros((1, width), f32), lane_zeros], 0
    ).astype(bf16)
    bias_high, bias_rest = split_two(bias)
    bias_middle, bias_low = split_two(bias_rest)
    state_right[...] = jnp.concatenate(
        [embed, jnp.zeros((32, width), f32), bias_high, bias_middle, bias_low, lane_zeros], 0
    ).astype(bf16)
    same_head = (
        lax.div(lax.broadcasted_iota(jnp.int32, (256, 256), 0), 128)
        == lax.div(lax.broadcasted_iota(jnp.int32, (256, 256), 1), 128)
    ).astype(bf16)
    key_gain = jnp.concatenate([key_gain_ref[...]] * 2, 1)
    query_gain = jnp.concatenate([query_gain_ref[...]] * 2, 1) * (LOG2E * 128 ** (-0.5))

    def head_norm(values, gain):
        squares = dot_nn((values * values).astype(bf16), same_head)
        return (values * lax.rsqrt(squares * (1.0 / 128) + epsilon) * gain).astype(bf16)

    for pair in range(4):
        cols = slice(pair * 256, pair * 256 + 256)
        text_key_buf[:, cols] = head_norm(text_keys_ref[:, cols].astype(f32), key_gain)
    length = length_ref[0]
    real = lax.broadcasted_iota(jnp.int32, (256, 1), 0) < length
    text_value_buf[...] = jnp.where(real, text_values_ref[...].astype(f32), 0.0).astype(bf16)
    row_ok = [jnp.where(seq > 0, 1.0, 0.0), 1.0, 1.0, jnp.where(seq < 127, 1.0, 0.0)]
    for row in range(4):
        ones_buf[row * 256 : row * 256 + 256, :] = (
            jnp.ones((256, 128), f32) * row_ok[row]
        ).astype(bf16)
    ones_buf[1024:1280, :] = jnp.where(real, jnp.ones((256, 128), f32), 0.0).astype(bf16)

    for copy in over_y:
        copy.wait()
    folded[member, pl.ds(z * 2, 2)] = jnp.sum(y_parts[...], 0)
    gather_z = []
    for d in range(1, 8):
        slot = folded.at[member, pl.ds(z * 2, 2)]
        copy = remote(slot, slot, gz_send.at[d], gz_recv.at[d], place.at(z=lax.rem(z + d, 8)))
        copy.start()
        gather_z.append(copy)

    for copy in latent_copies + velocity_copies:
        copy.wait()
    slots = (
        lax.broadcasted_iota(jnp.int32, (32, 128), 0) * 128
        + lax.broadcasted_iota(jnp.int32, (32, 128), 1)
    )
    guidance = jnp.sum(
        jnp.where(slots == guide_ref[0], scales_ref[...], 0.0), axis=(0, 1), keepdims=True
    )
    step = jnp.full((1, 128), step_ref[0], jnp.int32)
    sigma_step = sigma_at((step + 1).astype(f32)) - sigma_at(step.astype(f32))
    for block in range(3):
        conditional, unconditional = velocity[0, block], velocity[1, block]
        guided = unconditional + guidance * (conditional - unconditional)
        if block == 1:
            for m in range(32):
                guided_out[m // 16 : m // 16 + 1, m % 16 * 128 : m % 16 * 128 + 128] = guided[
                    m : m + 1, :
                ]
        stepped = latents[block] + sigma_step * guided
        if block == 0:
            stepped = jnp.where(seq > 0, stepped, 0.0)
        if block == 2:
            stepped = jnp.where(seq < 127, stepped, 0.0)
        for c in range(4):
            grid_cells[pl.ds(8 + block * 128 + c, 32, stride=4), :] = stepped[
                :, c * 32 : c * 32 + 32
            ]
    grid_cells[0:8, :] = jnp.zeros((8, 32), f32)
    grid_cells[392:400, :] = jnp.zeros((8, 32), f32)
    cell = lax.rem(lax.broadcasted_iota(jnp.int32, (384, 32), 0), 64)
    around = jnp.concatenate(
        [
            jnp.where(cell == 0, 0.0, grid_cells[7:391, :]),
            grid_cells[8:392, :],
            jnp.where(cell == 63, 0.0, grid_cells[9:393, :]),
        ],
        1,
    )
    fine = jnp.concatenate([up_bias_ref[...]] * 4, 1)
    for offset in range(3):
        fine = fine + jnp.dot(
            around[offset * 64 : offset * 64 + 256],
            coarse_weights(up_ref, offset),
            precision=highest,
            preferred_element_type=f32,
        )
    own = fine[64:192]
    pairs[...] = jnp.where(branch == 0, own[:, :64], own[:, 64:])
    flat = jnp.concatenate([pairs[pl.ds(0, 64, stride=2), :], pairs[pl.ds(1, 64, stride=2), :]], 1)
    for m in range(64):
        fine_out[m // 32 : m // 32 + 1, m % 32 * 128 : m % 32 * 128 + 128] = flat[m : m + 1, :]

    lane = lax.broadcasted_iota(jnp.int32, (256, 128), 1)
    turns = [fine] + [pltpu.roll(fine, 32 * turn, axis=1) for turn in range(1, 4)]
    tail = jnp.where(lane < 67, 1.0, 0.0)
    groups = [
        jnp.where(lane < 32, turns[(4 - g) % 4], jnp.where(lane < 64, turns[(5 - g) % 4], tail))
        for g in range(4)
    ]
    for g in range(4):
        for row in range(4):
            start = row * 256 + g * 64
            key_tokens[start : start + 64, :] = groups[g][row * 64 : row * 64 + 64].astype(bf16)
    for c in range(2):
        chosen = jnp.where(branch == 0, groups[c], groups[2 + c])
        for row in range(2):
            query_tokens[pl.ds(row * 128 + c, 64, stride=2), :] = chosen[
                64 + row * 64 : 128 + row * 64
            ]
    own_tokens = query_tokens[...].astype(bf16)

    for e in range(1, 4):
        along_p[e - 1].wait()
        send_q(e)
        send_sibling(e, 0)
    for copy in gather_z:
        copy.wait()
    gather_x = []
    for d in range(1, 8):
        slot = folded.at[member]
        copy = remote(
            slot, slot, gx_send.at[d], gx_recv.at[d],
            place.member_device(lax.rem(member + d, 8)),
        )
        copy.start()
        gather_x.append(copy)

    def rstd_of(tokens):
        centred = dot_nn(tokens, centred_right[...])
        return lax.rsqrt(jnp.mean(centred * centred, -1, keepdims=True) + epsilon)

    query_rstd = rstd_of(own_tokens)
    key_rstd = [rstd_of(key_tokens[row * 256 : row * 256 + 256, :]) for row in range(4)]

    for copy in gather_x:
        copy.wait()
    for part in range(8):
        for block in range(3):
            rows = jnp.concatenate([folded[part, k * 3 + block] for k in range(4)], 0)
            rest = folded[part, 12 + block]
            high, low = split_two(rows)
            rest_high, rest_low = split_two(rest[0:1])
            at = part * 384 + block * 128
            folded_right[:, at : at + 128] = jnp.concatenate(
                [high, low, rest_high, rest_low, jnp.zeros((62, 128), f32)], 0
            ).astype(bf16)
            shift_row[:, at : at + 128] = rest[1:2]

    def project(tokens, rstd, start):
        cols = slice(start, start + 256)
        return rstd * dot_nn(tokens, folded_right[:, cols]) + shift_row[:, cols]

    for pair in range(4):
        cols = slice(pair * 256, pair * 256 + 256)
        query_buf[:, cols] = head_norm(project(own_tokens, query_rstd, pair * 256), query_gain)
    for row in range(4):
        rows = slice(row * 256, row * 256 + 256)
        tokens = key_tokens[rows, :]
        for pair in range(4):
            cols = slice(pair * 256, pair * 256 + 256)
            key_buf[rows, cols] = head_norm(
                project(tokens, key_rstd[row], 1024 + pair * 256), key_gain
            )
            value_buf[rows, cols] = (
                project(tokens, key_rstd[row], 2048 + pair * 256) * row_ok[row]
            ).astype(bf16)

    for head in range(HEADS):
        cols = slice(head * 128, head * 128 + 128)
        text_right = jnp.concatenate([text_value_buf[:, cols], ones_buf[1024:1280, :]], 1)
        for row in range(2):
            window = slice(row * 256, row * 256 + 768)
            query = query_buf[row * 128 : row * 128 + 128, cols]
            weights = jnp.exp2(dot_nt(query, key_buf[window, cols])).astype(bf16)
            text_weights = jnp.exp2(dot_nt(query, text_key_buf[:, cols])).astype(bf16)
            right = jnp.concatenate([value_buf[window, cols], ones_buf[window, :]], 1)
            sums = dot_nn(weights, right) + dot_nn(text_weights, text_right)
            attended[row * 128 : row * 128 + 128, cols] = (sums[:, :128] / sums[:, 128:]).astype(
                bf16
            )
        if head >= 2:
            for item in range((head - 2) * 2, (head - 2) * 2 + 2):
                along_q[item].wait()
                send_sibling(item // 3, item % 3 + 1)

    for copy in to_sibling:
        copy.wait()
    for block in range(8):
        cols = slice(block * 256, block * 256 + 256)
        total = dot_nn(own_tokens, state_right[:, cols])
        output = jnp.zeros((256, 256), f32)
        for half in range(2):
            rows = out_rows[half, block // 4, block % 4].reshape(256, 512)
            output = output + dot_nt(attended[:, half * 512 : half * 512 + 512], rows)
        hidden_out[:, cols] = (total + modulation_ref[2:3, cols] * output).astype(bf16)


def per_device(
    coarse_hidden,
    coarse_modulation,
    final_weight,
    coarse_latent,
    step_index,
    guide_index,
    guide_scales,
    upsample_weight,
    upsample_bias,
    embed_weight,
    embed_bias,
    fine_modulation,
    project_weight,
    query_gain,
    key_gain,
    text_keys,
    text_values,
    text_length,
    output_weight,
):
    dma = pltpu.SemaphoreType.DMA
    sems = []
    for shape in [(8,), (8,), (4,), (8,), (8,)]:
        sems += [dma(shape), dma(shape)]
    sems += [dma, dma]
    for shape in [(8,), (4,), (4, 4), (4, 4), (5,), (2,)]:
        sems += [dma(shape), dma(shape)]
    vmem = pl.BlockSpec(memory_space=pltpu.VMEM)
    smem = pl.BlockSpec(memory_space=pltpu.SMEM)
    guided, fine, hidden = pl.pallas_call(
        kernel,
        out_shape=(
            jax.ShapeDtypeStruct((2, 2048), f32),
            jax.ShapeDtypeStruct((2, 4096), f32),
            jax.ShapeDtypeStruct((256, 2048), bf16),
        ),
        in_specs=[smem] * 3 + [vmem] * 16,
        out_specs=(vmem, vmem, vmem),
        scratch_shapes=[
            pltpu.VMEM((40, 2048), f32),
            pltpu.VMEM((8, 8, 384), f32),
            pltpu.VMEM((2, 4, 4, 8, 384), f32),
            pltpu.VMEM((16, 8, 128), f32),
            pltpu.VMEM((8, 2, 8, 128), f32),
            pltpu.VMEM((4, 2, 8, 128), f32),
            pltpu.VMEM((8, 16, 8, 128), f32),
            pltpu.VMEM((2, 8, 512), f32),
            pltpu.VMEM((8, 512), f32),
            pltpu.VMEM((2, 2, 4, 8, 2, 16, 512), bf16),
            pltpu.VMEM((2, 3, 32, 128), f32),
            pltpu.VMEM((3, 32, 128), f32),
            pltpu.VMEM((128, 32), f32),
            pltpu.VMEM((400, 32), f32),
            pltpu.VMEM((128, 64), f32),
            pltpu.VMEM((256, 128), f32),
            pltpu.VMEM((1024, 128), bf16),
            pltpu.VMEM((128, 2048), bf16),
            pltpu.VMEM((128, 2048), bf16),
            pltpu.VMEM((128, 3072), bf16),
            pltpu.VMEM((1, 3072), f32),
            pltpu.VMEM((256, 1024), bf16),
            pltpu.VMEM((1024, 1024), bf16),
            pltpu.VMEM((1024, 1024), bf16),
            pltpu.VMEM((256, 1024), bf16),
            pltpu.VMEM((256, 1024), bf16),
            pltpu.VMEM((1280, 128), bf16),
            pltpu.VMEM((256, 1024), bf16),
        ]
        + sems,
        compiler_params=pltpu.CompilerParams(
            collective_id=0, has_side_effects=True, vmem_limit_bytes=48 * 1024 * 1024
        ),
    )(
        step_index,
        guide_index,
        text_length,
        coarse_hidden.reshape(128, 2048),
        coarse_modulation[0],
        final_weight,
        coarse_latent,
        guide_scales.reshape(32, 128),
        upsample_weight,
        upsample_bias[None],
        embed_weight,
        embed_bias[None],
        fine_modulation,
        project_weight,
        query_gain[None],
        key_gain[None],
        text_keys,
        text_values,
        output_weight,
    )
    return guided, fine.reshape(2, 1, 4096), hidden.reshape(2, 1, 128, 2048)


def solution(mesh):
    placed = (
        P("cfg", "seq", None, None),
        P("cfg", None, None),
        P(),
        P("seq", None),
        P(),
        P(),
        P(),
        P(),
        P(),
        P(),
        P(),
        P(),
        P(("cfg", "seq"), None),
        P(),
        P(),
        P(),
        P(),
        P(),
        P(None, ("cfg", "seq")),
    )
    return jax.shard_map(
        per_device,
        mesh=mesh,
        in_specs=placed,
        out_specs=(P("seq", None), P("seq", "cfg", None), P("seq", "cfg", None, None)),
        check_vma=False,
    )
```

```python
import jax
import jax.numpy as jnp
from jax import lax
from jax.experimental import pallas as pl
from jax.experimental.pallas import tpu as pltpu
from jax.sharding import PartitionSpec as P

HEADS = 8
STEPS = 50
MESH = pl.DeviceIdType.MESH
LOG2E = 1.4426950408889634

epsilon = 1e-06
flow_shift = 5.0
highest = lax.Precision.HIGHEST
f32 = jnp.float32
bf16 = jnp.bfloat16

def remote(src, dst, send_sem, recv_sem, device):
    return pltpu.make_async_remote_copy(
        src_ref=src, dst_ref=dst, send_sem=send_sem, recv_sem=recv_sem,
        device_id=device, device_id_type=MESH,
    )


class Place:
    def __init__(self):
        self.x_lo = lax.axis_index("cfg")
        seq = lax.axis_index("seq")
        self.seq = seq
        self.core = lax.rem(seq, 2)
        self.x_hi = lax.rem(lax.div(seq, 2), 2)
        self.z = lax.rem(lax.div(seq, 4), 8)
        self.y = lax.div(seq, 32)
        self.x = self.x_hi * 2 + self.x_lo
        self.member = self.x_lo * 4 + self.x_hi * 2 + self.core
        self.line = lax.div(seq, 4)

    def at(self, x=None, y=None, z=None, core=None):
        x = self.x if x is None else x
        y = self.y if y is None else y
        z = self.z if z is None else z
        core = self.core if core is None else core
        return (lax.rem(x, 2), ((y * 8 + z) * 2 + lax.div(x, 2)) * 2 + core)

    def member_device(self, member):
        return (lax.div(member, 4), self.line * 4 + lax.rem(member, 4))


def greet(place):
    barrier = pltpu.get_barrier_semaphore()
    partners = [place.member_device(lax.rem(place.member + d, 8)) for d in range(1, 8)]
    partners += [place.at(y=lax.rem(place.y + d, 4)) for d in range(1, 4)]
    partners += [place.at(z=lax.rem(place.z + d, 8)) for d in range(1, 8)]
    for other in (lax.rem(place.seq + 1, 128), lax.rem(place.seq + 127, 128)):
        partners += [(place.x_lo, other), (1 - place.x_lo, other)]
    for partner in partners:
        pl.semaphore_signal(barrier, inc=1, device_id=partner, device_id_type=MESH)
    return barrier, len(partners)

def layer_norm(values):
    centred = values - jnp.mean(values, -1, keepdims=True)
    return centred * lax.rsqrt(jnp.mean(centred * centred, -1, keepdims=True) + epsilon)


def sigma_at(step_value):
    fraction = 1.0 - step_value / STEPS
    return flow_shift * fraction / (1.0 + (flow_shift - 1.0) * fraction)


def split_two(values):
    high = values.astype(bf16).astype(f32)
    return high, values - high


def dot_nt(a, b):
    return lax.dot_general(a, b, (((1,), (1,)), ((), ())), preferred_element_type=f32)


def dot_nn(a, b):
    return jnp.dot(a, b, preferred_element_type=f32)


TAPS = (((0,), (1, 2), ()), ((), (0, 1), (2,)))


def coarse_weights(up_ref, offset):
    eye = (
        lax.broadcasted_iota(jnp.int32, (32, 32), 0) == lax.broadcasted_iota(jnp.int32, (32, 32), 1)
    ).astype(f32)
    bands = []
    for a in range(2):
        for c in range(2):
            blocks = []
            for column in range(3):
                block = eye if offset == 1 and column == 1 else jnp.zeros((32, 32), f32)
                for r in TAPS[a][offset]:
                    for k in TAPS[c][column]:
                        tap = (3 * r + k) * 32
                        block = block + up_ref[:, tap : tap + 32]
                blocks.append(block)
            bands.append(jnp.concatenate(blocks, 1))
    return jnp.concatenate(bands, 0)


def kernel(
    step_ref, guide_ref, length_ref, weight_ref, output_ref, *refs
):
    stored, refs = refs[:14], refs[14:]
    (guided_out, fine_out, hidden_out), held, refs = refs[:3], refs[3:17], refs[17:]
    (
        embed_ref, modulation_ref, bias_ref, latent_ref, hidden_ref, coarse_mod_ref, final_ref,
        text_keys_ref, key_gain_ref, text_values_ref, scales_ref, up_ref, up_bias_ref,
        query_gain_ref,
    ) = held
    run(
        step_ref, guide_ref, length_ref, weight_ref, output_ref, stored, held,
        embed_ref, modulation_ref, bias_ref, latent_ref, hidden_ref, coarse_mod_ref, final_ref,
        text_keys_ref, key_gain_ref, text_values_ref, scales_ref, up_ref, up_bias_ref,
        query_gain_ref, guided_out, fine_out, hidden_out, *refs
    )


def run(
    step_ref, guide_ref, length_ref, weight_ref, output_ref, stored, held,
    embed_ref, modulation_ref, bias_ref, latent_ref, hidden_ref, coarse_mod_ref, final_ref,
    text_keys_ref, key_gain_ref, text_values_ref, scales_ref, up_ref, up_bias_ref,
    query_gain_ref, guided_out, fine_out, hidden_out,
    left, own_rows, group_rows, partial, z_parts, y_parts, folded,
    out_chunk, out_sibling, out_rows,
    velocity, latents, cells, grid_cells, pairs, query_tokens, key_tokens,
    centred_right, state_right, folded_right, shift_row,
    query_buf, key_buf, value_buf, text_key_buf, text_value_buf, ones_buf, attended,
    *sems,
):
    (
        a_send, a_recv, rz_send, rz_recv, ry_send, ry_recv, gz_send, gz_recv, gx_send, gx_recv,
        s_send, s_recv, wz_send, wz_recv, wp_send, wp_recv, wq_send, wq_recv, ws_send, ws_recv,
        v_send, v_recv, l_send, l_recv, load_sem,
    ) = sems
    loads = [
        pltpu.make_async_copy(source, target, load_sem.at[i])
        for i, (source, target) in enumerate(zip(stored, held))
    ]
    for load in loads:
        load.start()
    place = Place()
    core, z, y, member, seq, branch = (
        place.core, place.z, place.y, place.member, place.seq, place.x_lo
    )
    group_rows[...] = jnp.zeros_like(group_rows)
    barrier, count = greet(place)
    for part in range(8):
        own_rows[part] = weight_ref[:, part * 384 : (part + 1) * 384].astype(f32)
    turned = output_ref[...].astype(f32)
    out_chunk[0] = turned[:, :512]
    out_chunk[1] = turned[:, 512:]
    for load in loads[:4]:
        load.wait()
    for m in range(32):
        latents[1, m : m + 1, :] = latent_ref[m // 16 : m // 16 + 1, m % 16 * 128 : m % 16 * 128 + 128]
    pl.semaphore_wait(barrier, count)
    sibling = place.at(core=1 - core)
    swap = remote(out_chunk.at[1 - core], out_sibling, s_send, s_recv, sibling)
    swap.start()
    quarter = lax.rem(place.line, 4)
    spread = []
    for d in range(1, 8):
        target = lax.rem(member + d, 8)
        copy = remote(
            own_rows.at[target],
            group_rows.at[place.x_lo, quarter, place.x_hi * 2 + core],
            a_send.at[d], a_recv.at[d], place.member_device(target),
        )
        copy.start()
        spread.append(copy)
    after, before = lax.rem(seq + 1, 128), lax.rem(seq + 127, 128)
    latent_copies = [
        remote(latents.at[1], latents.at[0], l_send.at[0], l_recv.at[0], (branch, after)),
        remote(latents.at[1], latents.at[2], l_send.at[1], l_recv.at[1], (branch, before)),
    ]
    for copy in latent_copies:
        copy.start()
    group_rows[place.x_lo, quarter, place.x_hi * 2 + core] = own_rows[member]

    embed = embed_ref[...].astype(f32)
    scale = 1.0 + modulation_ref[1:2, :]
    embed_centred = embed - jnp.mean(embed, -1, keepdims=True)
    bias = bias_ref[...]
    bias_centred = bias - jnp.mean(bias, -1, keepdims=True)
    width = embed.shape[1]
    left[0:32] = embed_centred * scale
    left[32:40] = jnp.concatenate(
        [bias_centred * scale, modulation_ref[0:1, :], jnp.zeros((6, width), f32)], 0
    )

    for copy in spread:
        copy.wait()
    column = pl.multiple_of(lax.div(place.line, 4) * 128, 128)
    total = jnp.dot(
        left[:, pl.ds(column, 128)], group_rows[0].reshape(128, 384), precision=highest
    ) + jnp.dot(
        left[:, pl.ds(1024 + column, 128)], group_rows[1].reshape(128, 384), precision=highest
    )
    for row in range(5):
        for block in range(3):
            place_at = block * 4 + row if row < 4 else 12 + block
            partial[place_at] = total[row * 8 : row * 8 + 8, block * 128 : block * 128 + 128]
    partial[15] = jnp.zeros((8, 128), f32)
    scatter = []
    for d in range(1, 8):
        target = lax.rem(z + d, 8)
        copy = remote(
            partial.at[pl.ds(target * 2, 2)], z_parts.at[z],
            rz_send.at[d], rz_recv.at[d], place.at(z=target),
        )
        copy.start()
        scatter.append(copy)
    z_parts[z] = partial[pl.ds(z * 2, 2)]

    swap.wait()
    mine, other = out_chunk[core], out_sibling[...]
    first = core == 0
    out_rows[core, place.x_lo, y, z, place.x_hi] = jnp.concatenate(
        [jnp.where(first, mine, other), jnp.where(first, other, mine)], 0
    ).astype(bf16)
    along_z = []
    for d in range(1, 8):
        slot = out_rows.at[core, place.x_lo, y, z, place.x_hi]
        copy = remote(slot, slot, wz_send.at[d], wz_recv.at[d], place.at(z=lax.rem(z + d, 8)))
        copy.start()
        along_z.append(copy)

    for load in loads[4:7]:
        load.wait()
    for row in range(2):
        modulated = (
            layer_norm(hidden_ref[row * 64 : row * 64 + 64, :].astype(f32))
            * (1.0 + coarse_mod_ref[1:2, :])
            + coarse_mod_ref[0:1, :]
        ).astype(bf16)
        cells[row * 64 : row * 64 + 64, :] = dot_nt(modulated, final_ref[...])
    velocity[branch, 1] = jnp.concatenate(
        [cells[pl.ds(c, 32, stride=4), :] for c in range(4)], 1
    )
    velocity_copies = []
    targets = [
        ((1 - branch, seq), 1), ((branch, after), 0), ((1 - branch, after), 0),
        ((branch, before), 2), ((1 - branch, before), 2),
    ]
    for d, (target, slot) in enumerate(targets):
        copy = remote(
            velocity.at[branch, 1], velocity.at[branch, slot], v_send.at[d], v_recv.at[d], target
        )
        copy.start()
        velocity_copies.append(copy)

    for copy in scatter:
        copy.wait()
    y_parts[y] = jnp.sum(z_parts[...], 0)
    over_y = []
    for d in range(1, 4):
        copy = remote(
            y_parts.at[y], y_parts.at[y], ry_send.at[d], ry_recv.at[d],
            place.at(y=lax.rem(y + d, 4)),
        )
        copy.start()
        over_y.append(copy)

    for copy in along_z:
        copy.wait()
    first_at = y * (1 - core) + place.x * core
    second_at = place.x * (1 - core) + y * core

    def piece(p, q):
        px, py = q * (1 - core) + p * core, p * (1 - core) + q * core
        return out_rows.at[core, lax.rem(px, 2), py, :, lax.div(px, 2)]

    def piece_device(p, q):
        return place.at(x=q * (1 - core) + p * core, y=p * (1 - core) + q * core)

    along_p = []
    for d in range(1, 4):
        slot = piece(first_at, second_at)
        copy = remote(
            slot, slot, wp_send.at[d], wp_recv.at[d],
            piece_device(lax.rem(first_at + d, 4), second_at),
        )
        copy.start()
        along_p.append(copy)
    along_q = []

    def send_q(e):
        for d in range(1, 4):
            slot = piece(lax.rem(first_at + 4 - e, 4), second_at)
            copy = remote(
                slot, slot, wq_send.at[e, d], wq_recv.at[e, d],
                piece_device(first_at, lax.rem(second_at + d, 4)),
            )
            copy.start()
            along_q.append(copy)

    to_sibling = []

    def send_sibling(e, d):
        slot = piece(lax.rem(first_at + 4 - e, 4), lax.rem(second_at + 4 - d, 4))
        copy = remote(slot, slot, ws_send.at[e, d], ws_recv.at[e, d], sibling)
        copy.start()
        to_sibling.append(copy)

    send_q(0)
    send_sibling(0, 0)

    for load in loads[7:]:
        load.wait()

    lane_zeros = jnp.zeros((61, width), f32)
    high, low = split_two(embed_centred)
    bias_high, bias_low = split_two(bias_centred)
    centred_right[...] = jnp.concatenate(
        [high, low, bias_high, bias_low, jnp.zeros((1, width), f32), lane_zeros], 0
    ).astype(bf16)
    bias_high, bias_rest = split_two(bias)
    bias_middle, bias_low = split_two(bias_rest)
    state_right[...] = jnp.concatenate(
        [embed, jnp.zeros((32, width), f32), bias_high, bias_middle, bias_low, lane_zeros], 0
    ).astype(bf16)
    same_head = (
        lax.div(lax.broadcasted_iota(jnp.int32, (256, 256), 0), 128)
        == lax.div(lax.broadcasted_iota(jnp.int32, (256, 256), 1), 128)
    ).astype(bf16)
    key_gain = jnp.concatenate([key_gain_ref[...]] * 2, 1)
    query_gain = jnp.concatenate([query_gain_ref[...]] * 2, 1) * (LOG2E * 128 ** (-0.5))

    def head_norm(values, gain):
        squares = dot_nn((values * values).astype(bf16), same_head)
        return (values * lax.rsqrt(squares * (1.0 / 128) + epsilon) * gain).astype(bf16)

    for pair in range(4):
        cols = slice(pair * 256, pair * 256 + 256)
        text_key_buf[:, cols] = head_norm(text_keys_ref[:, cols].astype(f32), key_gain)
    length = length_ref[0]
    real = lax.broadcasted_iota(jnp.int32, (256, 1), 0) < length
    text_value_buf[...] = jnp.where(real, text_values_ref[...].astype(f32), 0.0).astype(bf16)
    row_ok = [jnp.where(seq > 0, 1.0, 0.0), 1.0, 1.0, jnp.where(seq < 127, 1.0, 0.0)]
    for row in range(4):
        ones_buf[row * 256 : row * 256 + 256, :] = (
            jnp.ones((256, 128), f32) * row_ok[row]
        ).astype(bf16)
    ones_buf[1024:1280, :] = jnp.where(real, jnp.ones((256, 128), f32), 0.0).astype(bf16)

    for copy in over_y:
        copy.wait()
    summed = jnp.sum(y_parts[...], 0)
    high, low = split_two(summed)
    low = jnp.concatenate([jnp.zeros((2, 2, 128), f32), low[:, :6]], 1)
    folded[member, z] = jnp.where(z >= 6, high + low, summed).reshape(16, 128).astype(bf16)
    gather_z = []
    for d in range(1, 8):
        slot = folded.at[member, z]
        copy = remote(slot, slot, gz_send.at[d], gz_recv.at[d], place.at(z=lax.rem(z + d, 8)))
        copy.start()
        gather_z.append(copy)

    for copy in latent_copies + velocity_copies:
        copy.wait()
    slots = (
        lax.broadcasted_iota(jnp.int32, (32, 128), 0) * 128
        + lax.broadcasted_iota(jnp.int32, (32, 128), 1)
    )
    guidance = jnp.sum(
        jnp.where(slots == guide_ref[0], scales_ref[...], 0.0), axis=(0, 1), keepdims=True
    )
    step = jnp.full((1, 128), step_ref[0], jnp.int32)
    sigma_step = sigma_at((step + 1).astype(f32)) - sigma_at(step.astype(f32))
    for block in range(3):
        conditional, unconditional = velocity[0, block], velocity[1, block]
        guided = unconditional + guidance * (conditional - unconditional)
        if block == 1:
            for m in range(32):
                guided_out[m // 16 : m // 16 + 1, m % 16 * 128 : m % 16 * 128 + 128] = guided[
                    m : m + 1, :
                ]
        stepped = latents[block] + sigma_step * guided
        if block == 0:
            stepped = jnp.where(seq > 0, stepped, 0.0)
        if block == 2:
            stepped = jnp.where(seq < 127, stepped, 0.0)
        for c in range(4):
            grid_cells[pl.ds(8 + block * 128 + c, 32, stride=4), :] = stepped[
                :, c * 32 : c * 32 + 32
            ]
    grid_cells[0:8, :] = jnp.zeros((8, 32), f32)
    grid_cells[392:400, :] = jnp.zeros((8, 32), f32)
    cell = lax.rem(lax.broadcasted_iota(jnp.int32, (384, 32), 0), 64)
    around = jnp.concatenate(
        [
            jnp.where(cell == 0, 0.0, grid_cells[7:391, :]),
            grid_cells[8:392, :],
            jnp.where(cell == 63, 0.0, grid_cells[9:393, :]),
        ],
        1,
    )
    fine = jnp.concatenate([up_bias_ref[...]] * 4, 1)
    for offset in range(3):
        fine = fine + lax.dot_general(
            around[offset * 64 : offset * 64 + 256],
            coarse_weights(up_ref, offset),
            (((1,), (1,)), ((), ())),
            precision=highest,
            preferred_element_type=f32,
        )
    own = fine[64:192]
    pairs[...] = jnp.where(branch == 0, own[:, :64], own[:, 64:])
    flat = jnp.concatenate([pairs[pl.ds(0, 64, stride=2), :], pairs[pl.ds(1, 64, stride=2), :]], 1)
    for m in range(64):
        fine_out[m // 32, :, m % 32 * 128 : m % 32 * 128 + 128] = flat[m : m + 1, :]

    lane = lax.broadcasted_iota(jnp.int32, (256, 128), 1)
    turns = [fine] + [pltpu.roll(fine, 32 * turn, axis=1) for turn in range(1, 4)]
    tail = jnp.where(lane < 67, 1.0, 0.0)
    groups = [
        jnp.where(lane < 32, turns[(4 - g) % 4], jnp.where(lane < 64, turns[(5 - g) % 4], tail))
        for g in range(4)
    ]
    for g in range(4):
        for row in range(4):
            start = row * 256 + g * 64
            key_tokens[start : start + 64, :] = groups[g][row * 64 : row * 64 + 64].astype(bf16)
    for c in range(2):
        chosen = jnp.where(branch == 0, groups[c], groups[2 + c])
        for row in range(2):
            query_tokens[pl.ds(row * 128 + c, 64, stride=2), :] = chosen[
                64 + row * 64 : 128 + row * 64
            ]
    own_tokens = query_tokens[...].astype(bf16)

    for copy in gather_z:
        copy.wait()
    gather_x = []
    for d in range(1, 8):
        slot = folded.at[member]
        copy = remote(
            slot, slot, gx_send.at[d], gx_recv.at[d],
            place.member_device(lax.rem(member + d, 8)),
        )
        copy.start()
        gather_x.append(copy)

    for e in range(1, 4):
        along_p[e - 1].wait()
        send_q(e)
        send_sibling(e, 0)
    def rstd_of(tokens):
        centred = dot_nn(tokens, centred_right[...])
        return lax.rsqrt(jnp.mean(centred * centred, -1, keepdims=True) + epsilon)

    query_rstd = rstd_of(own_tokens)
    key_rstd = [rstd_of(key_tokens[row * 256 : row * 256 + 256, :]) for row in range(4)]

    for copy in gather_x:
        copy.wait()
    for part in range(8):
        for block in range(3):
            at = part * 384 + block * 128
            folded_right[0:32, at : at + 128] = folded[part, block * 2 : block * 2 + 2].reshape(
                32, 128
            )
            rest = folded[part, 6 + block // 2].astype(f32)[block % 2 * 8 : block % 2 * 8 + 8]
            folded_right[32:80, at : at + 128] = jnp.concatenate(
                [jnp.zeros((32, 128), f32), rest[0:1], rest[2:3], jnp.zeros((14, 128), f32)], 0
            ).astype(bf16)
            folded_right[80:128, at : at + 128] = jnp.zeros((48, 128), bf16)
            shift_row[:, at : at + 128] = rest[1:2] + rest[3:4]

    def project(tokens, rstd, start):
        cols = slice(start, start + 256)
        return rstd * dot_nn(tokens, folded_right[:, cols]) + shift_row[:, cols]

    for pair in range(4):
        cols = slice(pair * 256, pair * 256 + 256)
        query_buf[:, cols] = head_norm(project(own_tokens, query_rstd, pair * 256), query_gain)
    for row in range(4):
        rows = slice(row * 256, row * 256 + 256)
        tokens = key_tokens[rows, :]
        for pair in range(4):
            cols = slice(pair * 256, pair * 256 + 256)
            key_buf[rows, cols] = head_norm(
                project(tokens, key_rstd[row], 1024 + pair * 256), key_gain
            )
            value_buf[rows, cols] = (
                project(tokens, key_rstd[row], 2048 + pair * 256) * row_ok[row]
            ).astype(bf16)

    for head in range(HEADS):
        cols = slice(head * 128, head * 128 + 128)
        text_right = jnp.concatenate([text_value_buf[:, cols], ones_buf[1024:1280, :]], 1)
        for row in range(2):
            window = slice(row * 256, row * 256 + 768)
            query = query_buf[row * 128 : row * 128 + 128, cols]
            weights = jnp.exp2(dot_nt(query, key_buf[window, cols])).astype(bf16)
            text_weights = jnp.exp2(dot_nt(query, text_key_buf[:, cols])).astype(bf16)
            right = jnp.concatenate([value_buf[window, cols], ones_buf[window, :]], 1)
            sums = dot_nn(weights, right) + dot_nn(text_weights, text_right)
            attended[row * 128 : row * 128 + 128, cols] = (sums[:, :128] / sums[:, 128:]).astype(
                bf16
            )
        if head >= 2:
            for item in range((head - 2) * 2, (head - 2) * 2 + 2):
                along_q[item].wait()
                send_sibling(item // 3, item % 3 + 1)

    for copy in to_sibling:
        copy.wait()
    for block in range(8):
        cols = slice(block * 256, block * 256 + 256)
        total = dot_nn(own_tokens, state_right[:, cols])
        output = jnp.zeros((256, 256), f32)
        for half in range(2):
            rows = out_rows[half, block // 4, block % 4].reshape(256, 512)
            output = output + dot_nt(attended[:, half * 512 : half * 512 + 512], rows)
        hidden_out[:, cols] = (total + modulation_ref[2:3, cols] * output).astype(bf16)


def per_device(
    coarse_hidden,
    coarse_modulation,
    final_weight,
    coarse_latent,
    step_index,
    guide_index,
    guide_scales,
    upsample_weight,
    upsample_bias,
    embed_weight,
    embed_bias,
    fine_modulation,
    project_weight,
    query_gain,
    key_gain,
    text_keys,
    text_values,
    text_length,
    output_weight,
):
    dma = pltpu.SemaphoreType.DMA
    sems = []
    for shape in [(8,), (8,), (4,), (8,), (8,)]:
        sems += [dma(shape), dma(shape)]
    sems += [dma, dma]
    for shape in [(8,), (4,), (4, 4), (4, 4), (5,), (2,)]:
        sems += [dma(shape), dma(shape)]
    sems += [dma((14,))]
    stored = [
        embed_weight, fine_modulation, embed_bias[None], coarse_latent,
        coarse_hidden.reshape(128, 2048), coarse_modulation[0], final_weight.T,
        text_keys, key_gain[None], text_values, guide_scales.reshape(32, 128),
        upsample_weight.T, upsample_bias[None], query_gain[None],
    ]
    hbm = pl.BlockSpec(memory_space=pltpu.HBM)
    vmem = pl.BlockSpec(memory_space=pltpu.VMEM)
    smem = pl.BlockSpec(memory_space=pltpu.SMEM)
    guided, fine, hidden = pl.pallas_call(
        kernel,
        out_shape=(
            jax.ShapeDtypeStruct((2, 2048), f32),
            jax.ShapeDtypeStruct((2, 1, 4096), f32),
            jax.ShapeDtypeStruct((256, 2048), bf16),
        ),
        in_specs=[smem] * 3 + [vmem] * 2 + [hbm] * 14,
        out_specs=(vmem, vmem, vmem),
        scratch_shapes=[pltpu.VMEM(array.shape, array.dtype) for array in stored]
        + [
            pltpu.VMEM((40, 2048), f32),
            pltpu.VMEM((8, 8, 384), f32),
            pltpu.VMEM((2, 4, 4, 8, 384), f32),
            pltpu.VMEM((16, 8, 128), f32),
            pltpu.VMEM((8, 2, 8, 128), f32),
            pltpu.VMEM((4, 2, 8, 128), f32),
            pltpu.VMEM((8, 8, 16, 128), bf16),
            pltpu.VMEM((2, 8, 512), f32),
            pltpu.VMEM((8, 512), f32),
            pltpu.VMEM((2, 2, 4, 8, 2, 16, 512), bf16),
            pltpu.VMEM((2, 3, 32, 128), f32),
            pltpu.VMEM((3, 32, 128), f32),
            pltpu.VMEM((128, 32), f32),
            pltpu.VMEM((400, 32), f32),
            pltpu.VMEM((128, 64), f32),
            pltpu.VMEM((256, 128), f32),
            pltpu.VMEM((1024, 128), bf16),
            pltpu.VMEM((128, 2048), bf16),
            pltpu.VMEM((128, 2048), bf16),
            pltpu.VMEM((128, 3072), bf16),
            pltpu.VMEM((1, 3072), f32),
            pltpu.VMEM((256, 1024), bf16),
            pltpu.VMEM((1024, 1024), bf16),
            pltpu.VMEM((1024, 1024), bf16),
            pltpu.VMEM((256, 1024), bf16),
            pltpu.VMEM((256, 1024), bf16),
            pltpu.VMEM((1280, 128), bf16),
            pltpu.VMEM((256, 1024), bf16),
        ]
        + sems,
        compiler_params=pltpu.CompilerParams(
            collective_id=0, has_side_effects=True, vmem_limit_bytes=56 * 1024 * 1024
        ),
    )(
        step_index, guide_index, text_length, project_weight, output_weight.T, *stored
    )
    return guided, fine, hidden.reshape(2, 1, 128, 2048)


def solution(mesh):
    placed = (
        P("cfg", "seq", None, None),
        P("cfg", None, None),
        P(),
        P("seq", None),
        P(),
        P(),
        P(),
        P(),
        P(),
        P(),
        P(),
        P(),
        P(("cfg", "seq"), None),
        P(),
        P(),
        P(),
        P(),
        P(),
        P(None, ("cfg", "seq")),
    )
    return jax.shard_map(
        per_device,
        mesh=mesh,
        in_specs=placed,
        out_specs=(P("seq", None), P("seq", "cfg", None), P("seq", "cfg", None, None)),
        check_vma=False,
    )
```

```python
import jax
import jax.numpy as jnp
from jax import lax
from jax.experimental import pallas as pl
from jax.experimental.pallas import tpu as pltpu
from jax.sharding import PartitionSpec as P

HEADS = 8
STEPS = 50
MESH = pl.DeviceIdType.MESH
LOG2E = 1.4426950408889634

epsilon = 1e-06
flow_shift = 5.0
highest = lax.Precision.HIGHEST
f32 = jnp.float32
bf16 = jnp.bfloat16

def remote(src, dst, send_sem, recv_sem, device):
    return pltpu.make_async_remote_copy(
        src_ref=src, dst_ref=dst, send_sem=send_sem, recv_sem=recv_sem,
        device_id=device, device_id_type=MESH,
    )


class Place:
    def __init__(self):
        self.x_lo = lax.axis_index("cfg")
        seq = lax.axis_index("seq")
        self.seq = seq
        self.core = lax.rem(seq, 2)
        self.x_hi = lax.rem(lax.div(seq, 2), 2)
        self.z = lax.rem(lax.div(seq, 4), 8)
        self.y = lax.div(seq, 32)
        self.x = self.x_hi * 2 + self.x_lo
        self.member = self.x_lo * 4 + self.x_hi * 2 + self.core
        self.line = lax.div(seq, 4)

    def at(self, x=None, y=None, z=None, core=None):
        x = self.x if x is None else x
        y = self.y if y is None else y
        z = self.z if z is None else z
        core = self.core if core is None else core
        return (lax.rem(x, 2), ((y * 8 + z) * 2 + lax.div(x, 2)) * 2 + core)

    def member_device(self, member):
        return (lax.div(member, 4), self.line * 4 + lax.rem(member, 4))


def greet(place):
    barrier = pltpu.get_barrier_semaphore()
    partners = [place.member_device(lax.rem(place.member + d, 8)) for d in range(1, 8)]
    partners += [place.at(y=lax.rem(place.y + d, 4)) for d in range(1, 4)]
    partners += [place.at(z=lax.rem(place.z + d, 8)) for d in range(1, 8)]
    for other in (lax.rem(place.seq + 1, 128), lax.rem(place.seq + 127, 128)):
        partners += [(place.x_lo, other), (1 - place.x_lo, other)]
    for partner in partners:
        pl.semaphore_signal(barrier, inc=1, device_id=partner, device_id_type=MESH)
    return barrier, len(partners)

def layer_norm(values):
    centred = values - jnp.mean(values, -1, keepdims=True)
    return centred * lax.rsqrt(jnp.mean(centred * centred, -1, keepdims=True) + epsilon)


def sigma_at(step_value):
    fraction = 1.0 - step_value / STEPS
    return flow_shift * fraction / (1.0 + (flow_shift - 1.0) * fraction)


def split_two(values):
    high = values.astype(bf16).astype(f32)
    return high, values - high


def dot_nt(a, b):
    return lax.dot_general(a, b, (((1,), (1,)), ((), ())), preferred_element_type=f32)


def dot_nn(a, b):
    return jnp.dot(a, b, preferred_element_type=f32)


TAPS = (((0,), (1, 2), ()), ((), (0, 1), (2,)))


def coarse_weights(up_ref, offset):
    eye = (
        lax.broadcasted_iota(jnp.int32, (32, 32), 0) == lax.broadcasted_iota(jnp.int32, (32, 32), 1)
    ).astype(f32)
    bands = []
    for a in range(2):
        for c in range(2):
            blocks = []
            for column in range(3):
                block = eye if offset == 1 and column == 1 else jnp.zeros((32, 32), f32)
                for r in TAPS[a][offset]:
                    for k in TAPS[c][column]:
                        tap = (3 * r + k) * 32
                        block = block + up_ref[:, tap : tap + 32]
                blocks.append(block)
            bands.append(jnp.concatenate(blocks, 1))
    return jnp.concatenate(bands, 0)


def kernel(
    weight_ref, output_ref, *refs
):
    stored, scalars, refs = refs[:14], refs[14:17], refs[17:]
    (guided_out, fine_out, hidden_out), held, refs = refs[:3], refs[3:17], refs[17:]
    (
        embed_ref, modulation_ref, bias_ref, latent_ref, hidden_ref, coarse_mod_ref, final_ref,
        text_keys_ref, key_gain_ref, text_values_ref, scales_ref, up_ref, up_bias_ref,
        query_gain_ref,
    ) = held
    step_ref, guide_ref, length_ref = scalars
    run(
        step_ref, guide_ref, length_ref, weight_ref, output_ref, stored, held,
        embed_ref, modulation_ref, bias_ref, latent_ref, hidden_ref, coarse_mod_ref, final_ref,
        text_keys_ref, key_gain_ref, text_values_ref, scales_ref, up_ref, up_bias_ref,
        query_gain_ref, guided_out, fine_out, hidden_out, *refs
    )


def run(
    step_ref, guide_ref, length_ref, weight_ref, output_ref, stored, held,
    embed_ref, modulation_ref, bias_ref, latent_ref, hidden_ref, coarse_mod_ref, final_ref,
    text_keys_ref, key_gain_ref, text_values_ref, scales_ref, up_ref, up_bias_ref,
    query_gain_ref, guided_out, fine_out, hidden_out,
    left, own_rows, group_rows, partial, z_parts, y_parts, folded,
    out_chunk, out_sibling, out_rows,
    velocity, latents, cells, grid_cells, pairs, query_tokens, key_tokens,
    key_left, centred_right, state_right, folded_right,
    query_buf, key_buf, value_buf, text_key_buf, text_value_buf, ones_buf, attended,
    *sems,
):
    (
        a_send, a_recv, rz_send, rz_recv, ry_send, ry_recv, gz_send, gz_recv, gx_send, gx_recv,
        s_send, s_recv, wz_send, wz_recv, wp_send, wp_recv, wq_send, wq_recv, ws_send, ws_recv,
        v_send, v_recv, l_send, l_recv, gs_send, gs_recv, load_sem,
    ) = sems
    loads = [
        pltpu.make_async_copy(source, target, load_sem.at[i])
        for i, (source, target) in enumerate(zip(stored, held))
    ]
    for load in loads:
        load.start()
    place = Place()
    core, z, y, member, seq, branch = (
        place.core, place.z, place.y, place.member, place.seq, place.x_lo
    )
    group_rows[...] = jnp.zeros_like(group_rows)
    barrier, count = greet(place)
    for part in range(8):
        own_rows[part] = weight_ref[:, part * 384 : (part + 1) * 384].astype(f32)
    turned = output_ref[...].astype(f32)
    out_chunk[0] = turned[:, :512]
    out_chunk[1] = turned[:, 512:]
    for load in loads[:4]:
        load.wait()
    for m in range(32):
        latents[1, m : m + 1, :] = latent_ref[m // 16 : m // 16 + 1, m % 16 * 128 : m % 16 * 128 + 128]
    pl.semaphore_wait(barrier, count)
    sibling = place.at(core=1 - core)
    swap = remote(out_chunk.at[1 - core], out_sibling, s_send, s_recv, sibling)
    swap.start()
    quarter = lax.rem(place.line, 4)
    spread = []
    for d in range(1, 8):
        target = lax.rem(member + d, 8)
        copy = remote(
            own_rows.at[target],
            group_rows.at[place.x_lo, quarter, place.x_hi * 2 + core],
            a_send.at[d], a_recv.at[d], place.member_device(target),
        )
        copy.start()
        spread.append(copy)
    after, before = lax.rem(seq + 1, 128), lax.rem(seq + 127, 128)
    latent_copies = [
        remote(latents.at[1], latents.at[0], l_send.at[0], l_recv.at[0], (branch, after)),
        remote(latents.at[1], latents.at[2], l_send.at[1], l_recv.at[1], (branch, before)),
    ]
    for copy in latent_copies:
        copy.start()
    group_rows[place.x_lo, quarter, place.x_hi * 2 + core] = own_rows[member]

    embed = embed_ref[...].astype(f32)
    scale = 1.0 + modulation_ref[1:2, :]
    embed_centred = embed - jnp.mean(embed, -1, keepdims=True)
    bias = bias_ref[...]
    bias_centred = bias - jnp.mean(bias, -1, keepdims=True)
    width = embed.shape[1]
    left[0:32] = embed_centred * scale
    left[32:40] = jnp.concatenate(
        [bias_centred * scale, modulation_ref[0:1, :], jnp.zeros((6, width), f32)], 0
    )

    swap.wait()
    mine, other = out_chunk[core], out_sibling[...]
    first = core == 0
    out_rows[core, place.x_lo, y, z, place.x_hi] = jnp.concatenate(
        [jnp.where(first, mine, other), jnp.where(first, other, mine)], 0
    ).astype(bf16)
    along_z = []
    for d in range(1, 8):
        slot = out_rows.at[core, place.x_lo, y, z, place.x_hi]
        copy = remote(slot, slot, wz_send.at[d], wz_recv.at[d], place.at(z=lax.rem(z + d, 8)))
        copy.start()
        along_z.append(copy)

    for copy in spread:
        copy.wait()
    column = pl.multiple_of(lax.div(place.line, 4) * 128, 128)
    total = jnp.dot(
        left[:, pl.ds(column, 128)], group_rows[0].reshape(128, 384), precision=highest
    ) + jnp.dot(
        left[:, pl.ds(1024 + column, 128)], group_rows[1].reshape(128, 384), precision=highest
    )
    for row in range(5):
        for block in range(3):
            place_at = block * 4 + row if row < 4 else 12 + block
            partial[place_at] = total[row * 8 : row * 8 + 8, block * 128 : block * 128 + 128]
    partial[15] = jnp.zeros((8, 128), f32)
    scatter = []
    for d in range(1, 8):
        target = lax.rem(z + d, 8)
        copy = remote(
            partial.at[pl.ds(target * 2, 2)], z_parts.at[z],
            rz_send.at[d], rz_recv.at[d], place.at(z=target),
        )
        copy.start()
        scatter.append(copy)
    z_parts[z] = partial[pl.ds(z * 2, 2)]

    for load in loads[4:7]:
        load.wait()
    for row in range(2):
        modulated = (
            layer_norm(hidden_ref[row * 64 : row * 64 + 64, :].astype(f32))
            * (1.0 + coarse_mod_ref[1:2, :])
            + coarse_mod_ref[0:1, :]
        ).astype(bf16)
        cells[row * 64 : row * 64 + 64, :] = dot_nt(modulated, final_ref[...])
    velocity[branch, 1] = jnp.concatenate(
        [cells[pl.ds(c, 32, stride=4), :] for c in range(4)], 1
    )
    velocity_copies = []
    targets = [
        ((1 - branch, seq), 1), ((branch, after), 0), ((1 - branch, after), 0),
        ((branch, before), 2), ((1 - branch, before), 2),
    ]
    for d, (target, slot) in enumerate(targets):
        copy = remote(
            velocity.at[branch, 1], velocity.at[branch, slot], v_send.at[d], v_recv.at[d], target
        )
        copy.start()
        velocity_copies.append(copy)

    for copy in scatter:
        copy.wait()
    y_parts[y] = jnp.sum(z_parts[...], 0)
    over_y = []
    for d in range(1, 4):
        copy = remote(
            y_parts.at[y], y_parts.at[y], ry_send.at[d], ry_recv.at[d],
            place.at(y=lax.rem(y + d, 4)),
        )
        copy.start()
        over_y.append(copy)

    for copy in along_z:
        copy.wait()
    first_at = y * (1 - core) + place.x * core
    second_at = place.x * (1 - core) + y * core

    def piece(p, q):
        px, py = q * (1 - core) + p * core, p * (1 - core) + q * core
        return out_rows.at[core, lax.rem(px, 2), py, :, lax.div(px, 2)]

    def piece_device(p, q):
        return place.at(x=q * (1 - core) + p * core, y=p * (1 - core) + q * core)

    along_p = []
    for d in range(1, 4):
        slot = piece(first_at, second_at)
        copy = remote(
            slot, slot, wp_send.at[d], wp_recv.at[d],
            piece_device(lax.rem(first_at + d, 4), second_at),
        )
        copy.start()
        along_p.append(copy)
    along_q = []

    def send_q(e):
        for d in range(1, 4):
            slot = piece(lax.rem(first_at + 4 - e, 4), second_at)
            copy = remote(
                slot, slot, wq_send.at[e, d], wq_recv.at[e, d],
                piece_device(first_at, lax.rem(second_at + d, 4)),
            )
            copy.start()
            along_q.append(copy)

    to_sibling = []

    def send_sibling(e, d):
        slot = piece(lax.rem(first_at + 4 - e, 4), lax.rem(second_at + 4 - d, 4))
        copy = remote(slot, slot, ws_send.at[e, d], ws_recv.at[e, d], sibling)
        copy.start()
        to_sibling.append(copy)

    send_q(0)
    send_sibling(0, 0)

    for load in loads[7:]:
        load.wait()

    lane_zeros = jnp.zeros((61, width), f32)
    high, low = split_two(embed_centred)
    bias_high, bias_low = split_two(bias_centred)
    centred_right[...] = jnp.concatenate(
        [high, low, bias_high, bias_low, jnp.zeros((1, width), f32), lane_zeros], 0
    ).astype(bf16)
    bias_high, bias_rest = split_two(bias)
    bias_middle, bias_low = split_two(bias_rest)
    state_right[...] = jnp.concatenate(
        [embed, jnp.zeros((32, width), f32), bias_high, bias_middle, bias_low, lane_zeros], 0
    ).astype(bf16)
    same_head = (
        lax.div(lax.broadcasted_iota(jnp.int32, (256, 256), 0), 128)
        == lax.div(lax.broadcasted_iota(jnp.int32, (256, 256), 1), 128)
    ).astype(bf16)
    key_gain = jnp.concatenate([key_gain_ref[...]] * 2, 1)
    query_gain = jnp.concatenate([query_gain_ref[...]] * 2, 1) * (LOG2E * 128 ** (-0.5))

    def head_norm(values, gain):
        squares = dot_nn((values * values).astype(bf16), same_head)
        return (values * lax.rsqrt(squares * (1.0 / 128) + epsilon) * gain).astype(bf16)

    for pair in range(4):
        cols = slice(pair * 256, pair * 256 + 256)
        text_key_buf[:, cols] = head_norm(text_keys_ref[:, cols].astype(f32), key_gain)
    length = length_ref[0]
    real = lax.broadcasted_iota(jnp.int32, (256, 1), 0) < length
    text_value_buf[...] = jnp.where(real, text_values_ref[...].astype(f32), 0.0).astype(bf16)
    row_ok = [jnp.where(seq > 0, 1.0, 0.0), 1.0, 1.0, jnp.where(seq < 127, 1.0, 0.0)]
    for row in range(4):
        ones_buf[row * 256 : row * 256 + 256, :] = (
            jnp.ones((256, 128), f32) * row_ok[row]
        ).astype(bf16)
    ones_buf[1024:1280, :] = jnp.where(real, jnp.ones((256, 128), f32), 0.0).astype(bf16)

    for copy in over_y:
        copy.wait()
    summed = jnp.sum(y_parts[...], 0)
    high, low = split_two(summed)
    low = jnp.concatenate([jnp.zeros((2, 2, 128), f32), low[:, :6]], 1)
    folded[member, z] = jnp.where(z >= 6, high + low, summed).reshape(16, 128).astype(bf16)
    gather_z = []
    for d in range(1, 8):
        slot = folded.at[member, z]
        copy = remote(slot, slot, gz_send.at[d], gz_recv.at[d], place.at(z=lax.rem(z + d, 8)))
        copy.start()
        gather_z.append(copy)

    for copy in latent_copies + velocity_copies:
        copy.wait()
    slots = (
        lax.broadcasted_iota(jnp.int32, (32, 128), 0) * 128
        + lax.broadcasted_iota(jnp.int32, (32, 128), 1)
    )
    guidance = jnp.sum(
        jnp.where(slots == guide_ref[0], scales_ref[...], 0.0), axis=(0, 1), keepdims=True
    )
    step = jnp.full((1, 128), step_ref[0], jnp.int32)
    sigma_step = sigma_at((step + 1).astype(f32)) - sigma_at(step.astype(f32))
    for block in range(3):
        conditional, unconditional = velocity[0, block], velocity[1, block]
        guided = unconditional + guidance * (conditional - unconditional)
        if block == 1:
            for m in range(32):
                guided_out[m // 16 : m // 16 + 1, m % 16 * 128 : m % 16 * 128 + 128] = guided[
                    m : m + 1, :
                ]
        stepped = latents[block] + sigma_step * guided
        if block == 0:
            stepped = jnp.where(seq > 0, stepped, 0.0)
        if block == 2:
            stepped = jnp.where(seq < 127, stepped, 0.0)
        for c in range(4):
            grid_cells[pl.ds(8 + block * 128 + c, 32, stride=4), :] = stepped[
                :, c * 32 : c * 32 + 32
            ]
    grid_cells[0:8, :] = jnp.zeros((8, 32), f32)
    grid_cells[392:400, :] = jnp.zeros((8, 32), f32)
    cell = lax.rem(lax.broadcasted_iota(jnp.int32, (384, 32), 0), 64)
    around = jnp.concatenate(
        [
            jnp.where(cell == 0, 0.0, grid_cells[7:391, :]),
            grid_cells[8:392, :],
            jnp.where(cell == 63, 0.0, grid_cells[9:393, :]),
        ],
        1,
    )
    fine = jnp.concatenate([up_bias_ref[...]] * 4, 1)
    for offset in range(3):
        fine = fine + lax.dot_general(
            around[offset * 64 : offset * 64 + 256],
            coarse_weights(up_ref, offset),
            (((1,), (1,)), ((), ())),
            precision=highest,
            preferred_element_type=f32,
        )
    own = fine[64:192]
    pairs[...] = jnp.where(branch == 0, own[:, :64], own[:, 64:])
    flat = jnp.concatenate([pairs[pl.ds(0, 64, stride=2), :], pairs[pl.ds(1, 64, stride=2), :]], 1)
    for m in range(64):
        fine_out[m // 32, :, m % 32 * 128 : m % 32 * 128 + 128] = flat[m : m + 1, :]

    lane = lax.broadcasted_iota(jnp.int32, (256, 128), 1)
    turns = [fine] + [pltpu.roll(fine, 32 * turn, axis=1) for turn in range(1, 4)]
    tail = jnp.where(lane < 67, 1.0, 0.0)
    groups = [
        jnp.where(lane < 32, turns[(4 - g) % 4], jnp.where(lane < 64, turns[(5 - g) % 4], tail))
        for g in range(4)
    ]
    for g in range(4):
        for row in range(4):
            start = row * 256 + g * 64
            key_tokens[start : start + 64, :] = groups[g][row * 64 : row * 64 + 64].astype(bf16)
    for c in range(2):
        chosen = jnp.where(branch == 0, groups[c], groups[2 + c])
        for row in range(2):
            query_tokens[pl.ds(row * 128 + c, 64, stride=2), :] = chosen[
                64 + row * 64 : 128 + row * 64
            ]
    own_tokens = query_tokens[...].astype(bf16)

    for e in range(1, 4):
        along_p[e - 1].wait()
        send_q(e)
        send_sibling(e, 0)
    for copy in gather_z:
        copy.wait()
    gather_x, to_twin = [], []

    def send_twin(d):
        source = lax.rem(place.x + 4 - d, 4)
        slot = folded.at[lax.rem(source, 2) * 4 + lax.div(source, 2) * 2 + core]
        copy = remote(slot, slot, gs_send.at[d], gs_recv.at[d], sibling)
        copy.start()
        to_twin.append(copy)

    for d in range(1, 4):
        slot = folded.at[member]
        copy = remote(
            slot, slot, gx_send.at[d], gx_recv.at[d], place.at(x=lax.rem(place.x + d, 4))
        )
        copy.start()
        gather_x.append(copy)
    send_twin(0)

    def rstd_of(tokens):
        centred = dot_nn(tokens, centred_right[...])
        return lax.rsqrt(jnp.mean(centred * centred, -1, keepdims=True) + epsilon)

    is_low = ((lane >= 32) & (lane < 64)) | (lane == 65)
    is_one = (lane == 67) | (lane == 68)

    def scaled(tokens):
        high, low = split_two(rstd_of(tokens) * tokens.astype(f32))
        return jnp.where(is_one, 1.0, jnp.where(is_low, low, high))

    own_left = scaled(own_tokens).astype(bf16)
    for row in range(4):
        rows = slice(row * 256, row * 256 + 256)
        key_left[rows, :] = (scaled(key_tokens[rows, :]) * row_ok[row]).astype(bf16)
    folded_right[64:128, :] = jnp.zeros((64, 3072), bf16)

    for d in range(1, 4):
        gather_x[d - 1].wait()
        send_twin(d)
    for copy in to_twin:
        copy.wait()
    for part in range(8):
        for block in range(3):
            at = part * 384 + block * 128
            rows = folded[part, block * 2 : block * 2 + 2].reshape(32, 128)
            folded_right[0:32, at : at + 128] = rows
            folded_right[32:64, at : at + 128] = rows
            rest = folded[part, 6 + block // 2].astype(f32)[block % 2 * 8 : block % 2 * 8 + 8]
            folded_right[64:80, at : at + 128] = jnp.concatenate(
                [rest[0:1], rest[0:1], rest[2:3], rest[1:2], rest[3:4], jnp.zeros((11, 128), f32)],
                0,
            ).astype(bf16)

    def project(tokens, start):
        return dot_nn(tokens, folded_right[:, start : start + 256])

    for pair in range(4):
        cols = slice(pair * 256, pair * 256 + 256)
        query_buf[:, cols] = head_norm(project(own_left, pair * 256), query_gain)
    for row in range(4):
        rows = slice(row * 256, row * 256 + 256)
        tokens = key_left[rows, :]
        for pair in range(4):
            cols = slice(pair * 256, pair * 256 + 256)
            key_buf[rows, cols] = head_norm(project(tokens, 1024 + pair * 256), key_gain)
            value_buf[rows, cols] = project(tokens, 2048 + pair * 256).astype(bf16)

    for head in range(HEADS):
        cols = slice(head * 128, head * 128 + 128)
        text_right = jnp.concatenate([text_value_buf[:, cols], ones_buf[1024:1280, :]], 1)
        for row in range(2):
            window = slice(row * 256, row * 256 + 768)
            query = query_buf[row * 128 : row * 128 + 128, cols]
            weights = jnp.exp2(dot_nt(query, key_buf[window, cols])).astype(bf16)
            text_weights = jnp.exp2(dot_nt(query, text_key_buf[:, cols])).astype(bf16)
            right = jnp.concatenate([value_buf[window, cols], ones_buf[window, :]], 1)
            sums = dot_nn(weights, right) + dot_nn(text_weights, text_right)
            attended[row * 128 : row * 128 + 128, cols] = (sums[:, :128] / sums[:, 128:]).astype(
                bf16
            )
        if head >= 2:
            for item in range((head - 2) * 2, (head - 2) * 2 + 2):
                along_q[item].wait()
                send_sibling(item // 3, item % 3 + 1)

    for copy in to_sibling:
        copy.wait()
    for block in range(8):
        cols = slice(block * 256, block * 256 + 256)
        total = dot_nn(own_tokens, state_right[:, cols])
        output = jnp.zeros((256, 256), f32)
        for half in range(2):
            rows = out_rows[half, block // 4, block % 4].reshape(256, 512)
            output = output + dot_nt(attended[:, half * 512 : half * 512 + 512], rows)
        hidden_out[:, cols] = (total + modulation_ref[2:3, cols] * output).astype(bf16)


def store_kernel(*refs):
    copies = [
        pltpu.make_async_copy(refs[i], refs[3 + i], refs[6].at[i]) for i in (2, 1, 0)
    ]
    for copy in copies:
        copy.start()
    for copy in copies:
        copy.wait()


def in_hbm(arrays):
    return [pltpu.with_memory_space_constraint(array, pltpu.HBM) for array in arrays]


def per_device(
    coarse_hidden,
    coarse_modulation,
    final_weight,
    coarse_latent,
    step_index,
    guide_index,
    guide_scales,
    upsample_weight,
    upsample_bias,
    embed_weight,
    embed_bias,
    fine_modulation,
    project_weight,
    query_gain,
    key_gain,
    text_keys,
    text_values,
    text_length,
    output_weight,
):
    dma = pltpu.SemaphoreType.DMA
    sems = []
    for shape in [(8,), (8,), (4,), (8,), (4,)]:
        sems += [dma(shape), dma(shape)]
    sems += [dma, dma]
    for shape in [(8,), (4,), (4, 4), (4, 4), (5,), (2,), (4,)]:
        sems += [dma(shape), dma(shape)]
    sems += [dma((14,))]
    stored = [
        embed_weight, fine_modulation, embed_bias[None], coarse_latent,
        coarse_hidden.reshape(128, 2048), coarse_modulation[0], final_weight.T,
        text_keys, key_gain[None], text_values, guide_scales.reshape(32, 128),
        upsample_weight.T, upsample_bias[None], query_gain[None], step_index, guide_index,
        text_length,
    ]
    hbm = pl.BlockSpec(memory_space=pltpu.HBM)
    vmem = pl.BlockSpec(memory_space=pltpu.VMEM)
    guided, fine, hidden = pl.pallas_call(
        kernel,
        out_shape=(
            jax.ShapeDtypeStruct((2, 2048), f32),
            jax.ShapeDtypeStruct((2, 1, 4096), f32),
            jax.ShapeDtypeStruct((256, 2048), bf16),
        ),
        in_specs=[vmem] * 2 + [hbm] * 14 + [pl.BlockSpec(memory_space=pltpu.SMEM)] * 3,
        out_specs=(vmem, vmem, vmem),
        scratch_shapes=[pltpu.VMEM(array.shape, array.dtype) for array in stored[:14]]
        + [
            pltpu.VMEM((40, 2048), f32),
            pltpu.VMEM((8, 8, 384), f32),
            pltpu.VMEM((2, 4, 4, 8, 384), f32),
            pltpu.VMEM((16, 8, 128), f32),
            pltpu.VMEM((8, 2, 8, 128), f32),
            pltpu.VMEM((4, 2, 8, 128), f32),
            pltpu.VMEM((8, 8, 16, 128), bf16),
            pltpu.VMEM((2, 8, 512), f32),
            pltpu.VMEM((8, 512), f32),
            pltpu.VMEM((2, 2, 4, 8, 2, 16, 512), bf16),
            pltpu.VMEM((2, 3, 32, 128), f32),
            pltpu.VMEM((3, 32, 128), f32),
            pltpu.VMEM((128, 32), f32),
            pltpu.VMEM((400, 32), f32),
            pltpu.VMEM((128, 64), f32),
            pltpu.VMEM((256, 128), f32),
            pltpu.VMEM((1024, 128), bf16),
            pltpu.VMEM((1024, 128), bf16),
            pltpu.VMEM((128, 2048), bf16),
            pltpu.VMEM((128, 2048), bf16),
            pltpu.VMEM((128, 3072), bf16),
            pltpu.VMEM((256, 1024), bf16),
            pltpu.VMEM((1024, 1024), bf16),
            pltpu.VMEM((1024, 1024), bf16),
            pltpu.VMEM((256, 1024), bf16),
            pltpu.VMEM((256, 1024), bf16),
            pltpu.VMEM((1280, 128), bf16),
            pltpu.VMEM((256, 1024), bf16),
        ]
        + sems,
        compiler_params=pltpu.CompilerParams(
            collective_id=0, has_side_effects=True, vmem_limit_bytes=48 * 1024 * 1024
        ),
    )(
        *in_hbm([project_weight, output_weight.T]), *in_hbm(stored[:14]), *stored[14:]
    )
    results = (guided, fine, hidden)
    guided, fine, hidden = pl.pallas_call(
        store_kernel,
        out_shape=[jax.ShapeDtypeStruct(array.shape, array.dtype) for array in results],
        in_specs=[vmem] * 3,
        out_specs=[hbm] * 3,
        scratch_shapes=[dma((3,))],
    )(*[pltpu.with_memory_space_constraint(array, pltpu.VMEM) for array in results])
    return guided, fine, hidden.reshape(2, 1, 128, 2048)


def solution(mesh):
    placed = (
        P("cfg", "seq", None, None),
        P("cfg", None, None),
        P(),
        P("seq", None),
        P(),
        P(),
        P(),
        P(),
        P(),
        P(),
        P(),
        P(),
        P(("cfg", "seq"), None),
        P(),
        P(),
        P(),
        P(),
        P(),
        P(None, ("cfg", "seq")),
    )
    return jax.shard_map(
        per_device,
        mesh=mesh,
        in_specs=placed,
        out_specs=(P("seq", None), P("seq", "cfg", None), P("seq", "cfg", None, None)),
        check_vma=False,
    )
```

```python
import jax
import jax.numpy as jnp
from jax import lax
from jax.experimental import pallas as pl
from jax.experimental.pallas import tpu as pltpu
from jax.sharding import PartitionSpec as P

HEADS = 8
STEPS = 50
MESH = pl.DeviceIdType.MESH
LOG2E = 1.4426950408889634

epsilon = 1e-06
flow_shift = 5.0
highest = lax.Precision.HIGHEST
f32 = jnp.float32
bf16 = jnp.bfloat16

def remote(src, dst, send_sem, recv_sem, device):
    return pltpu.make_async_remote_copy(
        src_ref=src, dst_ref=dst, send_sem=send_sem, recv_sem=recv_sem,
        device_id=device, device_id_type=MESH,
    )


class Place:
    def __init__(self):
        self.x_lo = lax.axis_index("cfg")
        seq = lax.axis_index("seq")
        self.seq = seq
        self.core = lax.rem(seq, 2)
        self.x_hi = lax.rem(lax.div(seq, 2), 2)
        self.z = lax.rem(lax.div(seq, 4), 8)
        self.y = lax.div(seq, 32)
        self.x = self.x_hi * 2 + self.x_lo
        self.member = self.x_lo * 4 + self.x_hi * 2 + self.core
        self.line = lax.div(seq, 4)

    def at(self, x=None, y=None, z=None, core=None):
        x = self.x if x is None else x
        y = self.y if y is None else y
        z = self.z if z is None else z
        core = self.core if core is None else core
        return (lax.rem(x, 2), ((y * 8 + z) * 2 + lax.div(x, 2)) * 2 + core)

    def member_device(self, member):
        return (lax.div(member, 4), self.line * 4 + lax.rem(member, 4))


def greet(place):
    barrier = pltpu.get_barrier_semaphore()
    partners = [place.member_device(lax.rem(place.member + d, 8)) for d in range(1, 8)]
    partners += [place.at(y=lax.rem(place.y + d, 4)) for d in range(1, 4)]
    partners += [place.at(z=lax.rem(place.z + d, 8)) for d in range(1, 8)]
    for other in (lax.rem(place.seq + 1, 128), lax.rem(place.seq + 127, 128)):
        partners += [(place.x_lo, other), (1 - place.x_lo, other)]
    for partner in partners:
        pl.semaphore_signal(barrier, inc=1, device_id=partner, device_id_type=MESH)
    return barrier, len(partners)

def layer_norm(values):
    centred = values - jnp.mean(values, -1, keepdims=True)
    return centred * lax.rsqrt(jnp.mean(centred * centred, -1, keepdims=True) + epsilon)


def sigma_at(step_value):
    fraction = 1.0 - step_value / STEPS
    return flow_shift * fraction / (1.0 + (flow_shift - 1.0) * fraction)


def split_two(values):
    high = values.astype(bf16).astype(f32)
    return high, values - high


def dot_nt(a, b):
    return lax.dot_general(a, b, (((1,), (1,)), ((), ())), preferred_element_type=f32)


def dot_nn(a, b):
    return jnp.dot(a, b, preferred_element_type=f32)


TAPS = (((0,), (1, 2), ()), ((), (0, 1), (2,)))


def coarse_weights(up_ref, offset):
    eye = (
        lax.broadcasted_iota(jnp.int32, (32, 32), 0) == lax.broadcasted_iota(jnp.int32, (32, 32), 1)
    ).astype(f32)
    bands = []
    for a in range(2):
        for c in range(2):
            blocks = []
            for column in range(3):
                block = eye if offset == 1 and column == 1 else jnp.zeros((32, 32), f32)
                for r in TAPS[a][offset]:
                    for k in TAPS[c][column]:
                        tap = (3 * r + k) * 32
                        block = block + up_ref[:, tap : tap + 32]
                blocks.append(block)
            bands.append(jnp.concatenate(blocks, 1))
    return jnp.concatenate(bands, 0)


def kernel(
    weight_ref, output_ref, *refs
):
    stored, scalars, refs = refs[:14], refs[14:17], refs[17:]
    (guided_out, fine_out, hidden_out), held, refs = refs[:3], refs[3:17], refs[17:]
    (
        embed_ref, modulation_ref, bias_ref, latent_ref, hidden_ref, coarse_mod_ref, final_ref,
        text_keys_ref, key_gain_ref, text_values_ref, scales_ref, up_ref, up_bias_ref,
        query_gain_ref,
    ) = held
    step_ref, guide_ref, length_ref = scalars
    run(
        step_ref, guide_ref, length_ref, weight_ref, output_ref, stored, held,
        embed_ref, modulation_ref, bias_ref, latent_ref, hidden_ref, coarse_mod_ref, final_ref,
        text_keys_ref, key_gain_ref, text_values_ref, scales_ref, up_ref, up_bias_ref,
        query_gain_ref, guided_out, fine_out, hidden_out, *refs
    )


def run(
    step_ref, guide_ref, length_ref, weight_ref, output_ref, stored, held,
    embed_ref, modulation_ref, bias_ref, latent_ref, hidden_ref, coarse_mod_ref, final_ref,
    text_keys_ref, key_gain_ref, text_values_ref, scales_ref, up_ref, up_bias_ref,
    query_gain_ref, guided_out, fine_out, hidden_out,
    left, own_rows, group_rows, partial, z_parts, y_parts, folded,
    out_chunk, out_sibling, out_rows,
    velocity, latents, cells, grid_cells, pairs, query_tokens, key_tokens,
    key_left, centred_right, state_right, folded_right,
    query_buf, key_buf, value_buf, text_key_buf, text_value_buf, ones_buf, attended,
    *sems,
):
    (
        a_send, a_recv, rz_send, rz_recv, ry_send, ry_recv, gz_send, gz_recv, gx_send, gx_recv,
        s_send, s_recv, wz_send, wz_recv, wp_send, wp_recv, wq_send, wq_recv, ws_send, ws_recv,
        v_send, v_recv, l_send, l_recv, gs_send, gs_recv, load_sem,
    ) = sems
    loads = [
        pltpu.make_async_copy(source, target, load_sem.at[i])
        for i, (source, target) in enumerate(zip(stored, held))
    ]
    for load in loads:
        load.start()
    place = Place()
    core, z, y, member, seq, branch = (
        place.core, place.z, place.y, place.member, place.seq, place.x_lo
    )
    group_rows[...] = jnp.zeros_like(group_rows)
    barrier, count = greet(place)
    for part in range(8):
        own_rows[part] = weight_ref[:, part * 384 : (part + 1) * 384].astype(f32)
    turned = output_ref[...].astype(f32)
    out_chunk[0] = turned[:, :512]
    out_chunk[1] = turned[:, 512:]
    for load in loads[:4]:
        load.wait()
    for m in range(32):
        latents[1, m : m + 1, :] = latent_ref[m // 16 : m // 16 + 1, m % 16 * 128 : m % 16 * 128 + 128]
    pl.semaphore_wait(barrier, count)
    sibling = place.at(core=1 - core)
    swap = remote(out_chunk.at[1 - core], out_sibling, s_send, s_recv, sibling)
    swap.start()
    quarter = lax.rem(place.line, 4)
    spread = []
    for d in range(1, 8):
        target = lax.rem(member + d, 8)
        copy = remote(
            own_rows.at[target],
            group_rows.at[place.x_lo, quarter, place.x_hi * 2 + core],
            a_send.at[d], a_recv.at[d], place.member_device(target),
        )
        copy.start()
        spread.append(copy)
    after, before = lax.rem(seq + 1, 128), lax.rem(seq + 127, 128)
    latent_copies = [
        remote(latents.at[1], latents.at[0], l_send.at[0], l_recv.at[0], (branch, after)),
        remote(latents.at[1], latents.at[2], l_send.at[1], l_recv.at[1], (branch, before)),
    ]
    for copy in latent_copies:
        copy.start()
    group_rows[place.x_lo, quarter, place.x_hi * 2 + core] = own_rows[member]

    embed = embed_ref[...].astype(f32)
    scale = 1.0 + modulation_ref[1:2, :]
    embed_centred = embed - jnp.mean(embed, -1, keepdims=True)
    bias = bias_ref[...]
    bias_centred = bias - jnp.mean(bias, -1, keepdims=True)
    width = embed.shape[1]
    left[0:32] = embed_centred * scale
    left[32:40] = jnp.concatenate(
        [bias_centred * scale, modulation_ref[0:1, :], jnp.zeros((6, width), f32)], 0
    )

    for copy in spread:
        copy.wait()
    column = pl.multiple_of(lax.div(place.line, 4) * 128, 128)
    total = jnp.dot(
        left[:, pl.ds(column, 128)], group_rows[0].reshape(128, 384), precision=highest
    ) + jnp.dot(
        left[:, pl.ds(1024 + column, 128)], group_rows[1].reshape(128, 384), precision=highest
    )
    for row in range(5):
        for block in range(3):
            place_at = block * 4 + row if row < 4 else 12 + block
            partial[place_at] = total[row * 8 : row * 8 + 8, block * 128 : block * 128 + 128]
    partial[15] = jnp.zeros((8, 128), f32)
    scatter = []
    for d in range(1, 8):
        target = lax.rem(z + d, 8)
        copy = remote(
            partial.at[pl.ds(target * 2, 2)], z_parts.at[z],
            rz_send.at[d], rz_recv.at[d], place.at(z=target),
        )
        copy.start()
        scatter.append(copy)
    z_parts[z] = partial[pl.ds(z * 2, 2)]

    swap.wait()
    mine, other = out_chunk[core], out_sibling[...]
    first = core == 0
    out_rows[core, place.x_lo, y, z, place.x_hi] = jnp.concatenate(
        [jnp.where(first, mine, other), jnp.where(first, other, mine)], 0
    ).astype(bf16)
    along_z = []
    for d in range(1, 8):
        slot = out_rows.at[core, place.x_lo, y, z, place.x_hi]
        copy = remote(slot, slot, wz_send.at[d], wz_recv.at[d], place.at(z=lax.rem(z + d, 8)))
        copy.start()
        along_z.append(copy)

    for load in loads[4:7]:
        load.wait()
    for row in range(2):
        modulated = (
            layer_norm(hidden_ref[row * 64 : row * 64 + 64, :].astype(f32))
            * (1.0 + coarse_mod_ref[1:2, :])
            + coarse_mod_ref[0:1, :]
        ).astype(bf16)
        cells[row * 64 : row * 64 + 64, :] = dot_nt(modulated, final_ref[...])
    velocity[branch, 1] = jnp.concatenate(
        [cells[pl.ds(c, 32, stride=4), :] for c in range(4)], 1
    )
    velocity_copies = []
    targets = [
        ((1 - branch, seq), 1), ((branch, after), 0), ((1 - branch, after), 0),
        ((branch, before), 2), ((1 - branch, before), 2),
    ]
    for d, (target, slot) in enumerate(targets):
        copy = remote(
            velocity.at[branch, 1], velocity.at[branch, slot], v_send.at[d], v_recv.at[d], target
        )
        copy.start()
        velocity_copies.append(copy)

    for copy in scatter:
        copy.wait()
    y_parts[y] = jnp.sum(z_parts[...], 0)
    over_y = []
    for d in range(1, 4):
        copy = remote(
            y_parts.at[y], y_parts.at[y], ry_send.at[d], ry_recv.at[d],
            place.at(y=lax.rem(y + d, 4)),
        )
        copy.start()
        over_y.append(copy)

    for copy in along_z:
        copy.wait()
    first_at = y * (1 - core) + place.x * core
    second_at = place.x * (1 - core) + y * core

    def piece(p, q):
        px, py = q * (1 - core) + p * core, p * (1 - core) + q * core
        return out_rows.at[core, lax.rem(px, 2), py, :, lax.div(px, 2)]

    def piece_device(p, q):
        return place.at(x=q * (1 - core) + p * core, y=p * (1 - core) + q * core)

    along_p = []
    for d in range(1, 4):
        slot = piece(first_at, second_at)
        copy = remote(
            slot, slot, wp_send.at[d], wp_recv.at[d],
            piece_device(lax.rem(first_at + d, 4), second_at),
        )
        copy.start()
        along_p.append(copy)
    along_q = []

    def send_q(e):
        for d in range(1, 4):
            slot = piece(lax.rem(first_at + 4 - e, 4), second_at)
            copy = remote(
                slot, slot, wq_send.at[e, d], wq_recv.at[e, d],
                piece_device(first_at, lax.rem(second_at + d, 4)),
            )
            copy.start()
            along_q.append(copy)

    to_sibling = []

    def send_sibling(e, d):
        slot = piece(lax.rem(first_at + 4 - e, 4), lax.rem(second_at + 4 - d, 4))
        copy = remote(slot, slot, ws_send.at[e, d], ws_recv.at[e, d], sibling)
        copy.start()
        to_sibling.append(copy)


    for load in loads[7:]:
        load.wait()

    lane_zeros = jnp.zeros((61, width), f32)
    high, low = split_two(embed_centred)
    bias_high, bias_low = split_two(bias_centred)
    centred_right[...] = jnp.concatenate(
        [high, low, bias_high, bias_low, jnp.zeros((1, width), f32), lane_zeros], 0
    ).astype(bf16)
    bias_high, bias_rest = split_two(bias)
    bias_middle, bias_low = split_two(bias_rest)
    state_right[...] = jnp.concatenate(
        [embed, jnp.zeros((32, width), f32), bias_high, bias_middle, bias_low, lane_zeros], 0
    ).astype(bf16)
    same_head = (
        lax.div(lax.broadcasted_iota(jnp.int32, (256, 256), 0), 128)
        == lax.div(lax.broadcasted_iota(jnp.int32, (256, 256), 1), 128)
    ).astype(bf16)
    key_gain = jnp.concatenate([key_gain_ref[...]] * 2, 1)
    query_gain = jnp.concatenate([query_gain_ref[...]] * 2, 1) * (LOG2E * 128 ** (-0.5))

    def head_norm(values, gain):
        squares = dot_nn((values * values).astype(bf16), same_head)
        return (values * lax.rsqrt(squares * (1.0 / 128) + epsilon) * gain).astype(bf16)

    for pair in range(4):
        cols = slice(pair * 256, pair * 256 + 256)
        text_key_buf[:, cols] = head_norm(text_keys_ref[:, cols].astype(f32), key_gain)
    length = length_ref[0]
    real = lax.broadcasted_iota(jnp.int32, (256, 1), 0) < length
    text_value_buf[...] = jnp.where(real, text_values_ref[...].astype(f32), 0.0).astype(bf16)
    row_ok = [jnp.where(seq > 0, 1.0, 0.0), 1.0, 1.0, jnp.where(seq < 127, 1.0, 0.0)]
    for row in range(4):
        ones_buf[row * 256 : row * 256 + 256, :] = (
            jnp.ones((256, 128), f32) * row_ok[row]
        ).astype(bf16)
    ones_buf[1024:1280, :] = jnp.where(real, jnp.ones((256, 128), f32), 0.0).astype(bf16)

    for copy in over_y:
        copy.wait()
    summed = jnp.sum(y_parts[...], 0)
    high, low = split_two(summed)
    low = jnp.concatenate([jnp.zeros((2, 2, 128), f32), low[:, :6]], 1)
    folded[member, z] = jnp.where(z >= 6, high + low, summed).reshape(16, 128).astype(bf16)
    gather_z = []
    for d in range(1, 8):
        slot = folded.at[member, z]
        copy = remote(slot, slot, gz_send.at[d], gz_recv.at[d], place.at(z=lax.rem(z + d, 8)))
        copy.start()
        gather_z.append(copy)

    send_q(0)
    send_sibling(0, 0)

    for copy in latent_copies + velocity_copies:
        copy.wait()
    slots = (
        lax.broadcasted_iota(jnp.int32, (32, 128), 0) * 128
        + lax.broadcasted_iota(jnp.int32, (32, 128), 1)
    )
    guidance = jnp.sum(
        jnp.where(slots == guide_ref[0], scales_ref[...], 0.0), axis=(0, 1), keepdims=True
    )
    step = jnp.full((1, 128), step_ref[0], jnp.int32)
    sigma_step = sigma_at((step + 1).astype(f32)) - sigma_at(step.astype(f32))
    for block in range(3):
        conditional, unconditional = velocity[0, block], velocity[1, block]
        guided = unconditional + guidance * (conditional - unconditional)
        if block == 1:
            for m in range(32):
                guided_out[m // 16 : m // 16 + 1, m % 16 * 128 : m % 16 * 128 + 128] = guided[
                    m : m + 1, :
                ]
        stepped = latents[block] + sigma_step * guided
        if block == 0:
            stepped = jnp.where(seq > 0, stepped, 0.0)
        if block == 2:
            stepped = jnp.where(seq < 127, stepped, 0.0)
        for c in range(4):
            grid_cells[pl.ds(8 + block * 128 + c, 32, stride=4), :] = stepped[
                :, c * 32 : c * 32 + 32
            ]
    grid_cells[0:8, :] = jnp.zeros((8, 32), f32)
    grid_cells[392:400, :] = jnp.zeros((8, 32), f32)
    cell = lax.rem(lax.broadcasted_iota(jnp.int32, (384, 32), 0), 64)
    around = jnp.concatenate(
        [
            jnp.where(cell == 0, 0.0, grid_cells[7:391, :]),
            grid_cells[8:392, :],
            jnp.where(cell == 63, 0.0, grid_cells[9:393, :]),
        ],
        1,
    )
    fine = jnp.concatenate([up_bias_ref[...]] * 4, 1)
    for offset in range(3):
        fine = fine + lax.dot_general(
            around[offset * 64 : offset * 64 + 256],
            coarse_weights(up_ref, offset),
            (((1,), (1,)), ((), ())),
            precision=highest,
            preferred_element_type=f32,
        )
    own = fine[64:192]
    pairs[...] = jnp.where(branch == 0, own[:, :64], own[:, 64:])
    flat = jnp.concatenate([pairs[pl.ds(0, 64, stride=2), :], pairs[pl.ds(1, 64, stride=2), :]], 1)
    for m in range(64):
        fine_out[m // 32, :, m % 32 * 128 : m % 32 * 128 + 128] = flat[m : m + 1, :]

    lane = lax.broadcasted_iota(jnp.int32, (256, 128), 1)
    turns = [fine] + [pltpu.roll(fine, 32 * turn, axis=1) for turn in range(1, 4)]
    tail = jnp.where(lane < 67, 1.0, 0.0)
    groups = [
        jnp.where(lane < 32, turns[(4 - g) % 4], jnp.where(lane < 64, turns[(5 - g) % 4], tail))
        for g in range(4)
    ]
    for g in range(4):
        for row in range(4):
            start = row * 256 + g * 64
            key_tokens[start : start + 64, :] = groups[g][row * 64 : row * 64 + 64].astype(bf16)
    for c in range(2):
        chosen = jnp.where(branch == 0, groups[c], groups[2 + c])
        for row in range(2):
            query_tokens[pl.ds(row * 128 + c, 64, stride=2), :] = chosen[
                64 + row * 64 : 128 + row * 64
            ]
    own_tokens = query_tokens[...].astype(bf16)

    for copy in gather_z:
        copy.wait()
    gather_x, to_twin = [], []

    def send_twin(d):
        source = lax.rem(place.x + 4 - d, 4)
        slot = folded.at[lax.rem(source, 2) * 4 + lax.div(source, 2) * 2 + core]
        copy = remote(slot, slot, gs_send.at[d], gs_recv.at[d], sibling)
        copy.start()
        to_twin.append(copy)

    for d in range(1, 4):
        slot = folded.at[member]
        copy = remote(
            slot, slot, gx_send.at[d], gx_recv.at[d], place.at(x=lax.rem(place.x + d, 4))
        )
        copy.start()
        gather_x.append(copy)
    send_twin(0)

    for e in range(1, 4):
        along_p[e - 1].wait()
        send_q(e)
        send_sibling(e, 0)
    def rstd_of(tokens):
        centred = dot_nn(tokens, centred_right[...])
        return lax.rsqrt(jnp.mean(centred * centred, -1, keepdims=True) + epsilon)

    is_low = ((lane >= 32) & (lane < 64)) | (lane == 65)
    is_one = (lane == 67) | (lane == 68)

    def scaled(tokens):
        high, low = split_two(rstd_of(tokens) * tokens.astype(f32))
        return jnp.where(is_one, 1.0, jnp.where(is_low, low, high))

    own_left = scaled(own_tokens).astype(bf16)
    for row in range(4):
        rows = slice(row * 256, row * 256 + 256)
        key_left[rows, :] = (scaled(key_tokens[rows, :]) * row_ok[row]).astype(bf16)
    folded_right[64:128, :] = jnp.zeros((64, 3072), bf16)

    for d in range(1, 4):
        gather_x[d - 1].wait()
        send_twin(d)
    for copy in to_twin:
        copy.wait()
    for part in range(8):
        for block in range(3):
            at = part * 384 + block * 128
            rows = folded[part, block * 2 : block * 2 + 2].reshape(32, 128)
            folded_right[0:32, at : at + 128] = rows
            folded_right[32:64, at : at + 128] = rows
            rest = folded[part, 6 + block // 2].astype(f32)[block % 2 * 8 : block % 2 * 8 + 8]
            folded_right[64:80, at : at + 128] = jnp.concatenate(
                [rest[0:1], rest[0:1], rest[2:3], rest[1:2], rest[3:4], jnp.zeros((11, 128), f32)],
                0,
            ).astype(bf16)

    def project(tokens, start):
        return dot_nn(tokens, folded_right[:, start : start + 256])

    for pair in range(4):
        cols = slice(pair * 256, pair * 256 + 256)
        query_buf[:, cols] = head_norm(project(own_left, pair * 256), query_gain)
    for row in range(4):
        rows = slice(row * 256, row * 256 + 256)
        tokens = key_left[rows, :]
        for pair in range(4):
            cols = slice(pair * 256, pair * 256 + 256)
            key_buf[rows, cols] = head_norm(project(tokens, 1024 + pair * 256), key_gain)
            value_buf[rows, cols] = project(tokens, 2048 + pair * 256).astype(bf16)

    for head in range(HEADS):
        cols = slice(head * 128, head * 128 + 128)
        text_right = jnp.concatenate([text_value_buf[:, cols], ones_buf[1024:1280, :]], 1)
        for row in range(2):
            window = slice(row * 256, row * 256 + 768)
            query = query_buf[row * 128 : row * 128 + 128, cols]
            weights = jnp.exp2(dot_nt(query, key_buf[window, cols])).astype(bf16)
            text_weights = jnp.exp2(dot_nt(query, text_key_buf[:, cols])).astype(bf16)
            right = jnp.concatenate([value_buf[window, cols], ones_buf[window, :]], 1)
            sums = dot_nn(weights, right) + dot_nn(text_weights, text_right)
            attended[row * 128 : row * 128 + 128, cols] = (sums[:, :128] / sums[:, 128:]).astype(
                bf16
            )
        if head >= 2:
            for item in range((head - 2) * 2, (head - 2) * 2 + 2):
                along_q[item].wait()
                send_sibling(item // 3, item % 3 + 1)

    for copy in to_sibling:
        copy.wait()
    for block in range(8):
        cols = slice(block * 256, block * 256 + 256)
        total = dot_nn(own_tokens, state_right[:, cols])
        output = jnp.zeros((256, 256), f32)
        for half in range(2):
            rows = out_rows[half, block // 4, block % 4].reshape(256, 512)
            output = output + dot_nt(attended[:, half * 512 : half * 512 + 512], rows)
        hidden_out[:, cols] = (total + modulation_ref[2:3, cols] * output).astype(bf16)


def store_kernel(*refs):
    copies = [
        pltpu.make_async_copy(refs[i], refs[3 + i], refs[6].at[i]) for i in (2, 1, 0)
    ]
    for copy in copies:
        copy.start()
    for copy in copies:
        copy.wait()


def in_hbm(arrays):
    return [pltpu.with_memory_space_constraint(array, pltpu.HBM) for array in arrays]


def per_device(
    coarse_hidden,
    coarse_modulation,
    final_weight,
    coarse_latent,
    step_index,
    guide_index,
    guide_scales,
    upsample_weight,
    upsample_bias,
    embed_weight,
    embed_bias,
    fine_modulation,
    project_weight,
    query_gain,
    key_gain,
    text_keys,
    text_values,
    text_length,
    output_weight,
):
    dma = pltpu.SemaphoreType.DMA
    sems = []
    for shape in [(8,), (8,), (4,), (8,), (4,)]:
        sems += [dma(shape), dma(shape)]
    sems += [dma, dma]
    for shape in [(8,), (4,), (4, 4), (4, 4), (5,), (2,), (4,)]:
        sems += [dma(shape), dma(shape)]
    sems += [dma((14,))]
    stored = [
        embed_weight, fine_modulation, embed_bias[None], coarse_latent,
        coarse_hidden.reshape(128, 2048), coarse_modulation[0], final_weight.T,
        text_keys, key_gain[None], text_values, guide_scales.reshape(32, 128),
        upsample_weight.T, upsample_bias[None], query_gain[None], step_index, guide_index,
        text_length,
    ]
    hbm = pl.BlockSpec(memory_space=pltpu.HBM)
    vmem = pl.BlockSpec(memory_space=pltpu.VMEM)
    guided, fine, hidden = pl.pallas_call(
        kernel,
        out_shape=(
            jax.ShapeDtypeStruct((2, 2048), f32),
            jax.ShapeDtypeStruct((2, 1, 4096), f32),
            jax.ShapeDtypeStruct((256, 2048), bf16),
        ),
        in_specs=[vmem] * 2 + [hbm] * 14 + [pl.BlockSpec(memory_space=pltpu.SMEM)] * 3,
        out_specs=(vmem, vmem, vmem),
        scratch_shapes=[pltpu.VMEM(array.shape, array.dtype) for array in stored[:14]]
        + [
            pltpu.VMEM((40, 2048), f32),
            pltpu.VMEM((8, 8, 384), f32),
            pltpu.VMEM((2, 4, 4, 8, 384), f32),
            pltpu.VMEM((16, 8, 128), f32),
            pltpu.VMEM((8, 2, 8, 128), f32),
            pltpu.VMEM((4, 2, 8, 128), f32),
            pltpu.VMEM((8, 8, 16, 128), bf16),
            pltpu.VMEM((2, 8, 512), f32),
            pltpu.VMEM((8, 512), f32),
            pltpu.VMEM((2, 2, 4, 8, 2, 16, 512), bf16),
            pltpu.VMEM((2, 3, 32, 128), f32),
            pltpu.VMEM((3, 32, 128), f32),
            pltpu.VMEM((128, 32), f32),
            pltpu.VMEM((400, 32), f32),
            pltpu.VMEM((128, 64), f32),
            pltpu.VMEM((256, 128), f32),
            pltpu.VMEM((1024, 128), bf16),
            pltpu.VMEM((1024, 128), bf16),
            pltpu.VMEM((128, 2048), bf16),
            pltpu.VMEM((128, 2048), bf16),
            pltpu.VMEM((128, 3072), bf16),
            pltpu.VMEM((256, 1024), bf16),
            pltpu.VMEM((1024, 1024), bf16),
            pltpu.VMEM((1024, 1024), bf16),
            pltpu.VMEM((256, 1024), bf16),
            pltpu.VMEM((256, 1024), bf16),
            pltpu.VMEM((1280, 128), bf16),
            pltpu.VMEM((256, 1024), bf16),
        ]
        + sems,
        compiler_params=pltpu.CompilerParams(
            collective_id=0, has_side_effects=True, vmem_limit_bytes=48 * 1024 * 1024
        ),
    )(
        *in_hbm([project_weight, output_weight.T]), *in_hbm(stored[:14]), *stored[14:]
    )
    results = (guided, fine, hidden)
    guided, fine, hidden = pl.pallas_call(
        store_kernel,
        out_shape=[jax.ShapeDtypeStruct(array.shape, array.dtype) for array in results],
        in_specs=[vmem] * 3,
        out_specs=[hbm] * 3,
        scratch_shapes=[dma((3,))],
    )(*[pltpu.with_memory_space_constraint(array, pltpu.VMEM) for array in results])
    return guided, fine, hidden.reshape(2, 1, 128, 2048)


def solution(mesh):
    placed = (
        P("cfg", "seq", None, None),
        P("cfg", None, None),
        P(),
        P("seq", None),
        P(),
        P(),
        P(),
        P(),
        P(),
        P(),
        P(),
        P(),
        P(("cfg", "seq"), None),
        P(),
        P(),
        P(),
        P(),
        P(),
        P(None, ("cfg", "seq")),
    )
    return jax.shard_map(
        per_device,
        mesh=mesh,
        in_specs=placed,
        out_specs=(P("seq", None), P("seq", "cfg", None), P("seq", "cfg", None, None)),
        check_vma=False,
    )
```

```python
import jax
import jax.numpy as jnp
from jax import lax
from jax.experimental import pallas as pl
from jax.experimental.pallas import tpu as pltpu
from jax.sharding import PartitionSpec as P

HEADS = 8
STEPS = 50
MESH = pl.DeviceIdType.MESH
LOG2E = 1.4426950408889634

epsilon = 1e-06
flow_shift = 5.0
highest = lax.Precision.HIGHEST
f32 = jnp.float32
bf16 = jnp.bfloat16

def remote(src, dst, send_sem, recv_sem, device):
    return pltpu.make_async_remote_copy(
        src_ref=src, dst_ref=dst, send_sem=send_sem, recv_sem=recv_sem,
        device_id=device, device_id_type=MESH,
    )


class Place:
    def __init__(self):
        self.x_lo = lax.axis_index("cfg")
        seq = lax.axis_index("seq")
        self.seq = seq
        self.core = lax.rem(seq, 2)
        self.x_hi = lax.rem(lax.div(seq, 2), 2)
        self.z = lax.rem(lax.div(seq, 4), 8)
        self.y = lax.div(seq, 32)
        self.x = self.x_hi * 2 + self.x_lo
        self.member = self.x_lo * 4 + self.x_hi * 2 + self.core
        self.line = lax.div(seq, 4)

    def at(self, x=None, y=None, z=None, core=None):
        x = self.x if x is None else x
        y = self.y if y is None else y
        z = self.z if z is None else z
        core = self.core if core is None else core
        return (lax.rem(x, 2), ((y * 8 + z) * 2 + lax.div(x, 2)) * 2 + core)

    def member_device(self, member):
        return (lax.div(member, 4), self.line * 4 + lax.rem(member, 4))


def greet(place):
    barrier = pltpu.get_barrier_semaphore()
    partners = [place.member_device(lax.rem(place.member + d, 8)) for d in range(1, 8)]
    partners += [place.at(y=lax.rem(place.y + d, 4)) for d in range(1, 4)]
    partners += [place.at(z=lax.rem(place.z + d, 8)) for d in range(1, 8)]
    for other in (lax.rem(place.seq + 1, 128), lax.rem(place.seq + 127, 128)):
        partners += [(place.x_lo, other), (1 - place.x_lo, other)]
    for partner in partners:
        pl.semaphore_signal(barrier, inc=1, device_id=partner, device_id_type=MESH)
    return barrier, len(partners)

def layer_norm(values):
    centred = values - jnp.mean(values, -1, keepdims=True)
    return centred * lax.rsqrt(jnp.mean(centred * centred, -1, keepdims=True) + epsilon)


def sigma_at(step_value):
    fraction = 1.0 - step_value / STEPS
    return flow_shift * fraction / (1.0 + (flow_shift - 1.0) * fraction)


def split_two(values):
    high = values.astype(bf16).astype(f32)
    return high, values - high


def dot_nt(a, b):
    return lax.dot_general(a, b, (((1,), (1,)), ((), ())), preferred_element_type=f32)


def dot_nn(a, b):
    return jnp.dot(a, b, preferred_element_type=f32)


TAPS = (((0,), (1, 2), ()), ((), (0, 1), (2,)))


def coarse_weights(up_ref, offset):
    eye = (
        lax.broadcasted_iota(jnp.int32, (32, 32), 0) == lax.broadcasted_iota(jnp.int32, (32, 32), 1)
    ).astype(f32)
    bands = []
    for a in range(2):
        for c in range(2):
            blocks = []
            for column in range(3):
                block = eye if offset == 1 and column == 1 else jnp.zeros((32, 32), f32)
                for r in TAPS[a][offset]:
                    for k in TAPS[c][column]:
                        tap = (3 * r + k) * 32
                        block = block + up_ref[:, tap : tap + 32]
                blocks.append(block)
            bands.append(jnp.concatenate(blocks, 1))
    return jnp.concatenate(bands, 0)


def kernel(
    weight_ref, output_ref, *refs
):
    stored, scalars, refs = refs[:14], refs[14:17], refs[17:]
    (guided_out, fine_out, hidden_out), held, refs = refs[:3], refs[3:17], refs[17:]
    (
        embed_ref, modulation_ref, bias_ref, latent_ref, hidden_ref, coarse_mod_ref, final_ref,
        text_keys_ref, key_gain_ref, text_values_ref, scales_ref, up_ref, up_bias_ref,
        query_gain_ref,
    ) = held
    step_ref, guide_ref, length_ref = scalars
    run(
        step_ref, guide_ref, length_ref, weight_ref, output_ref, stored, held,
        embed_ref, modulation_ref, bias_ref, latent_ref, hidden_ref, coarse_mod_ref, final_ref,
        text_keys_ref, key_gain_ref, text_values_ref, scales_ref, up_ref, up_bias_ref,
        query_gain_ref, guided_out, fine_out, hidden_out, *refs
    )


def run(
    step_ref, guide_ref, length_ref, weight_ref, output_ref, stored, held,
    embed_ref, modulation_ref, bias_ref, latent_ref, hidden_ref, coarse_mod_ref, final_ref,
    text_keys_ref, key_gain_ref, text_values_ref, scales_ref, up_ref, up_bias_ref,
    query_gain_ref, guided_out, fine_out, hidden_out,
    left, own_rows, group_rows, partial, z_parts, y_parts, folded,
    out_chunk, out_sibling, out_rows,
    velocity, latents, cells, grid_cells, pairs, query_tokens, key_tokens,
    key_left, centred_right, state_right, folded_right, state,
    query_buf, key_buf, value_buf, text_key_buf, text_value_buf, ones_buf, attended,
    *sems,
):
    (
        a_send, a_recv, rz_send, rz_recv, ry_send, ry_recv, gz_send, gz_recv, gx_send, gx_recv,
        s_send, s_recv, wz_send, wz_recv, wp_send, wp_recv, wq_send, wq_recv, ws_send, ws_recv,
        v_send, v_recv, l_send, l_recv, gs_send, gs_recv, load_sem,
    ) = sems
    loads = [
        pltpu.make_async_copy(source, target, load_sem.at[i])
        for i, (source, target) in enumerate(zip(stored, held))
    ]
    for load in loads:
        load.start()
    place = Place()
    core, z, y, member, seq, branch = (
        place.core, place.z, place.y, place.member, place.seq, place.x_lo
    )
    group_rows[...] = jnp.zeros_like(group_rows)
    barrier, count = greet(place)
    for part in range(8):
        own_rows[part] = weight_ref[:, part * 384 : (part + 1) * 384].astype(f32)
    turned = output_ref[...].astype(f32)
    out_chunk[0] = turned[:, :512]
    out_chunk[1] = turned[:, 512:]
    for load in loads[:4]:
        load.wait()
    for m in range(32):
        latents[1, m : m + 1, :] = latent_ref[m // 16 : m // 16 + 1, m % 16 * 128 : m % 16 * 128 + 128]
    pl.semaphore_wait(barrier, count)
    sibling = place.at(core=1 - core)
    swap = remote(out_chunk.at[1 - core], out_sibling, s_send, s_recv, sibling)
    swap.start()
    quarter = lax.rem(place.line, 4)
    spread = []
    for d in range(1, 8):
        target = lax.rem(member + d, 8)
        copy = remote(
            own_rows.at[target],
            group_rows.at[place.x_lo, quarter, place.x_hi * 2 + core],
            a_send.at[d], a_recv.at[d], place.member_device(target),
        )
        copy.start()
        spread.append(copy)
    after, before = lax.rem(seq + 1, 128), lax.rem(seq + 127, 128)
    latent_copies = [
        remote(latents.at[1], latents.at[0], l_send.at[0], l_recv.at[0], (branch, after)),
        remote(latents.at[1], latents.at[2], l_send.at[1], l_recv.at[1], (branch, before)),
    ]
    for copy in latent_copies:
        copy.start()
    group_rows[place.x_lo, quarter, place.x_hi * 2 + core] = own_rows[member]

    embed = embed_ref[...].astype(f32)
    scale = 1.0 + modulation_ref[1:2, :]
    embed_centred = embed - jnp.mean(embed, -1, keepdims=True)
    bias = bias_ref[...]
    bias_centred = bias - jnp.mean(bias, -1, keepdims=True)
    width = embed.shape[1]
    left[0:32] = embed_centred * scale
    left[32:40] = jnp.concatenate(
        [bias_centred * scale, modulation_ref[0:1, :], jnp.zeros((6, width), f32)], 0
    )

    for copy in spread:
        copy.wait()
    column = pl.multiple_of(lax.div(place.line, 4) * 128, 128)
    total = jnp.dot(
        left[:, pl.ds(column, 128)], group_rows[0].reshape(128, 384), precision=highest
    ) + jnp.dot(
        left[:, pl.ds(1024 + column, 128)], group_rows[1].reshape(128, 384), precision=highest
    )
    for row in range(5):
        for block in range(3):
            place_at = block * 4 + row if row < 4 else 12 + block
            partial[place_at] = total[row * 8 : row * 8 + 8, block * 128 : block * 128 + 128]
    partial[15] = jnp.zeros((8, 128), f32)
    scatter = []
    for d in range(1, 8):
        target = lax.rem(z + d, 8)
        copy = remote(
            partial.at[pl.ds(target * 2, 2)], z_parts.at[z],
            rz_send.at[d], rz_recv.at[d], place.at(z=target),
        )
        copy.start()
        scatter.append(copy)
    z_parts[z] = partial[pl.ds(z * 2, 2)]

    swap.wait()
    mine, other = out_chunk[core], out_sibling[...]
    first = core == 0
    out_rows[core, place.x_lo, y, z, place.x_hi] = jnp.concatenate(
        [jnp.where(first, mine, other), jnp.where(first, other, mine)], 0
    ).astype(bf16)
    along_z = []
    for d in range(1, 8):
        slot = out_rows.at[core, place.x_lo, y, z, place.x_hi]
        copy = remote(slot, slot, wz_send.at[d], wz_recv.at[d], place.at(z=lax.rem(z + d, 8)))
        copy.start()
        along_z.append(copy)

    for load in loads[4:7]:
        load.wait()
    for row in range(2):
        modulated = (
            layer_norm(hidden_ref[row * 64 : row * 64 + 64, :].astype(f32))
            * (1.0 + coarse_mod_ref[1:2, :])
            + coarse_mod_ref[0:1, :]
        ).astype(bf16)
        cells[row * 64 : row * 64 + 64, :] = dot_nt(modulated, final_ref[...])
    velocity[branch, 1] = jnp.concatenate(
        [cells[pl.ds(c, 32, stride=4), :] for c in range(4)], 1
    )
    velocity_copies = []
    targets = [
        ((1 - branch, seq), 1), ((branch, after), 0), ((1 - branch, after), 0),
        ((branch, before), 2), ((1 - branch, before), 2),
    ]
    for d, (target, slot) in enumerate(targets):
        copy = remote(
            velocity.at[branch, 1], velocity.at[branch, slot], v_send.at[d], v_recv.at[d], target
        )
        copy.start()
        velocity_copies.append(copy)

    for copy in scatter:
        copy.wait()
    y_parts[y] = jnp.sum(z_parts[...], 0)
    over_y = []
    for d in range(1, 4):
        copy = remote(
            y_parts.at[y], y_parts.at[y], ry_send.at[d], ry_recv.at[d],
            place.at(y=lax.rem(y + d, 4)),
        )
        copy.start()
        over_y.append(copy)

    for copy in along_z:
        copy.wait()
    first_at = y * (1 - core) + place.x * core
    second_at = place.x * (1 - core) + y * core

    def piece(p, q):
        px, py = q * (1 - core) + p * core, p * (1 - core) + q * core
        return out_rows.at[core, lax.rem(px, 2), py, :, lax.div(px, 2)]

    def piece_device(p, q):
        return place.at(x=q * (1 - core) + p * core, y=p * (1 - core) + q * core)

    along_p = []
    for d in range(1, 4):
        slot = piece(first_at, second_at)
        copy = remote(
            slot, slot, wp_send.at[d], wp_recv.at[d],
            piece_device(lax.rem(first_at + d, 4), second_at),
        )
        copy.start()
        along_p.append(copy)
    along_q = []

    def send_q(e):
        for d in range(1, 4):
            slot = piece(lax.rem(first_at + 4 - e, 4), second_at)
            copy = remote(
                slot, slot, wq_send.at[e, d], wq_recv.at[e, d],
                piece_device(first_at, lax.rem(second_at + d, 4)),
            )
            copy.start()
            along_q.append(copy)

    to_sibling = []

    def send_sibling(e, d):
        slot = piece(lax.rem(first_at + 4 - e, 4), lax.rem(second_at + 4 - d, 4))
        copy = remote(slot, slot, ws_send.at[e, d], ws_recv.at[e, d], sibling)
        copy.start()
        to_sibling.append(copy)


    for load in loads[7:]:
        load.wait()

    lane_zeros = jnp.zeros((61, width), f32)
    high, low = split_two(embed_centred)
    bias_high, bias_low = split_two(bias_centred)
    centred_right[...] = jnp.concatenate(
        [high, low, bias_high, bias_low, jnp.zeros((1, width), f32), lane_zeros], 0
    ).astype(bf16)
    bias_high, bias_rest = split_two(bias)
    bias_middle, bias_low = split_two(bias_rest)
    state_right[...] = jnp.concatenate(
        [embed, jnp.zeros((32, width), f32), bias_high, bias_middle, bias_low, lane_zeros], 0
    ).astype(bf16)
    same_head = (
        lax.div(lax.broadcasted_iota(jnp.int32, (256, 256), 0), 128)
        == lax.div(lax.broadcasted_iota(jnp.int32, (256, 256), 1), 128)
    ).astype(bf16)
    key_gain = jnp.concatenate([key_gain_ref[...]] * 2, 1)
    query_gain = jnp.concatenate([query_gain_ref[...]] * 2, 1) * (LOG2E * 128 ** (-0.5))

    def head_norm(values, gain):
        squares = dot_nn((values * values).astype(bf16), same_head)
        return (values * lax.rsqrt(squares * (1.0 / 128) + epsilon) * gain).astype(bf16)

    for pair in range(4):
        cols = slice(pair * 256, pair * 256 + 256)
        text_key_buf[:, cols] = head_norm(text_keys_ref[:, cols].astype(f32), key_gain)
    length = length_ref[0]
    real = lax.broadcasted_iota(jnp.int32, (256, 1), 0) < length
    text_value_buf[...] = jnp.where(real, text_values_ref[...].astype(f32), 0.0).astype(bf16)
    row_ok = [jnp.where(seq > 0, 1.0, 0.0), 1.0, 1.0, jnp.where(seq < 127, 1.0, 0.0)]
    for row in range(4):
        ones_buf[row * 256 : row * 256 + 256, :] = (
            jnp.ones((256, 128), f32) * row_ok[row]
        ).astype(bf16)
    ones_buf[1024:1280, :] = jnp.where(real, jnp.ones((256, 128), f32), 0.0).astype(bf16)

    for copy in over_y:
        copy.wait()
    summed = jnp.sum(y_parts[...], 0)
    high, low = split_two(summed)
    low = jnp.concatenate([jnp.zeros((2, 2, 128), f32), low[:, :6]], 1)
    folded[member, z] = jnp.where(z >= 6, high + low, summed).reshape(16, 128).astype(bf16)
    gather_z = []
    for d in range(1, 8):
        slot = folded.at[member, z]
        copy = remote(slot, slot, gz_send.at[d], gz_recv.at[d], place.at(z=lax.rem(z + d, 8)))
        copy.start()
        gather_z.append(copy)

    send_q(0)
    send_sibling(0, 0)

    for copy in latent_copies + velocity_copies:
        copy.wait()
    slots = (
        lax.broadcasted_iota(jnp.int32, (32, 128), 0) * 128
        + lax.broadcasted_iota(jnp.int32, (32, 128), 1)
    )
    guidance = jnp.sum(
        jnp.where(slots == guide_ref[0], scales_ref[...], 0.0), axis=(0, 1), keepdims=True
    )
    step = jnp.full((1, 128), step_ref[0], jnp.int32)
    sigma_step = sigma_at((step + 1).astype(f32)) - sigma_at(step.astype(f32))
    for block in range(3):
        conditional, unconditional = velocity[0, block], velocity[1, block]
        guided = unconditional + guidance * (conditional - unconditional)
        if block == 1:
            for m in range(32):
                guided_out[m // 16 : m // 16 + 1, m % 16 * 128 : m % 16 * 128 + 128] = guided[
                    m : m + 1, :
                ]
        stepped = latents[block] + sigma_step * guided
        if block == 0:
            stepped = jnp.where(seq > 0, stepped, 0.0)
        if block == 2:
            stepped = jnp.where(seq < 127, stepped, 0.0)
        for c in range(4):
            grid_cells[pl.ds(8 + block * 128 + c, 32, stride=4), :] = stepped[
                :, c * 32 : c * 32 + 32
            ]
    grid_cells[0:8, :] = jnp.zeros((8, 32), f32)
    grid_cells[392:400, :] = jnp.zeros((8, 32), f32)
    cell = lax.rem(lax.broadcasted_iota(jnp.int32, (384, 32), 0), 64)
    around = jnp.concatenate(
        [
            jnp.where(cell == 0, 0.0, grid_cells[7:391, :]),
            grid_cells[8:392, :],
            jnp.where(cell == 63, 0.0, grid_cells[9:393, :]),
        ],
        1,
    )
    fine = jnp.concatenate([up_bias_ref[...]] * 4, 1)
    for offset in range(3):
        fine = fine + lax.dot_general(
            around[offset * 64 : offset * 64 + 256],
            coarse_weights(up_ref, offset),
            (((1,), (1,)), ((), ())),
            precision=highest,
            preferred_element_type=f32,
        )
    own = fine[64:192]
    pairs[...] = jnp.where(branch == 0, own[:, :64], own[:, 64:])
    flat = jnp.concatenate([pairs[pl.ds(0, 64, stride=2), :], pairs[pl.ds(1, 64, stride=2), :]], 1)
    for m in range(64):
        fine_out[m // 32, :, m % 32 * 128 : m % 32 * 128 + 128] = flat[m : m + 1, :]

    lane = lax.broadcasted_iota(jnp.int32, (256, 128), 1)
    turns = [fine] + [pltpu.roll(fine, 32 * turn, axis=1) for turn in range(1, 4)]
    tail = jnp.where(lane < 67, 1.0, 0.0)
    groups = [
        jnp.where(lane < 32, turns[(4 - g) % 4], jnp.where(lane < 64, turns[(5 - g) % 4], tail))
        for g in range(4)
    ]
    for g in range(4):
        for row in range(4):
            start = row * 256 + g * 64
            key_tokens[start : start + 64, :] = groups[g][row * 64 : row * 64 + 64].astype(bf16)
    for c in range(2):
        chosen = jnp.where(branch == 0, groups[c], groups[2 + c])
        for row in range(2):
            query_tokens[pl.ds(row * 128 + c, 64, stride=2), :] = chosen[
                64 + row * 64 : 128 + row * 64
            ]
    own_tokens = query_tokens[...].astype(bf16)

    for copy in gather_z:
        copy.wait()
    gather_x, to_twin = [], []

    def send_twin(d):
        source = lax.rem(place.x + 4 - d, 4)
        slot = folded.at[lax.rem(source, 2) * 4 + lax.div(source, 2) * 2 + core]
        copy = remote(slot, slot, gs_send.at[d], gs_recv.at[d], sibling)
        copy.start()
        to_twin.append(copy)

    for d in range(1, 4):
        slot = folded.at[member]
        copy = remote(
            slot, slot, gx_send.at[d], gx_recv.at[d], place.at(x=lax.rem(place.x + d, 4))
        )
        copy.start()
        gather_x.append(copy)
    send_twin(0)

    for e in range(1, 4):
        along_p[e - 1].wait()
        send_q(e)
        send_sibling(e, 0)
    def rstd_of(tokens):
        centred = dot_nn(tokens, centred_right[...])
        return lax.rsqrt(jnp.mean(centred * centred, -1, keepdims=True) + epsilon)

    is_low = ((lane >= 32) & (lane < 64)) | (lane == 65)
    is_one = (lane == 67) | (lane == 68)

    def scaled(tokens):
        high, low = split_two(rstd_of(tokens) * tokens.astype(f32))
        return jnp.where(is_one, 1.0, jnp.where(is_low, low, high))

    own_left = scaled(own_tokens).astype(bf16)
    for row in range(4):
        rows = slice(row * 256, row * 256 + 256)
        key_left[rows, :] = (scaled(key_tokens[rows, :]) * row_ok[row]).astype(bf16)
    folded_right[64:128, :] = jnp.zeros((64, 3072), bf16)
    for block in range(8):
        cols = slice(block * 256, block * 256 + 256)
        state[:, cols] = dot_nn(own_tokens, state_right[:, cols])

    for d in range(1, 4):
        gather_x[d - 1].wait()
        send_twin(d)
    for copy in to_twin:
        copy.wait()
    for part in range(8):
        for block in range(3):
            at = part * 384 + block * 128
            rows = folded[part, block * 2 : block * 2 + 2].reshape(32, 128)
            folded_right[0:32, at : at + 128] = rows
            folded_right[32:64, at : at + 128] = rows
            rest = folded[part, 6 + block // 2].astype(f32)[block % 2 * 8 : block % 2 * 8 + 8]
            folded_right[64:80, at : at + 128] = jnp.concatenate(
                [rest[0:1], rest[0:1], rest[2:3], rest[1:2], rest[3:4], jnp.zeros((11, 128), f32)],
                0,
            ).astype(bf16)

    def project(tokens, start):
        return dot_nn(tokens, folded_right[:, start : start + 256])

    for pair in range(4):
        cols = slice(pair * 256, pair * 256 + 256)
        query_buf[:, cols] = head_norm(project(own_left, pair * 256), query_gain)
    for row in range(4):
        rows = slice(row * 256, row * 256 + 256)
        tokens = key_left[rows, :]
        for pair in range(4):
            cols = slice(pair * 256, pair * 256 + 256)
            key_buf[rows, cols] = head_norm(project(tokens, 1024 + pair * 256), key_gain)
            value_buf[rows, cols] = project(tokens, 2048 + pair * 256).astype(bf16)

    for head in range(HEADS):
        cols = slice(head * 128, head * 128 + 128)
        text_right = jnp.concatenate([text_value_buf[:, cols], ones_buf[1024:1280, :]], 1)
        for row in range(2):
            window = slice(row * 256, row * 256 + 768)
            query = query_buf[row * 128 : row * 128 + 128, cols]
            weights = jnp.exp2(dot_nt(query, key_buf[window, cols])).astype(bf16)
            text_weights = jnp.exp2(dot_nt(query, text_key_buf[:, cols])).astype(bf16)
            right = jnp.concatenate([value_buf[window, cols], ones_buf[window, :]], 1)
            sums = dot_nn(weights, right) + dot_nn(text_weights, text_right)
            attended[row * 128 : row * 128 + 128, cols] = (sums[:, :128] / sums[:, 128:]).astype(
                bf16
            )
        if head >= 5:
            for item in range((head - 5) * 4, (head - 5) * 4 + 4):
                along_q[item].wait()
                send_sibling(item // 3, item % 3 + 1)

    for copy in to_sibling:
        copy.wait()
    for block in range(8):
        cols = slice(block * 256, block * 256 + 256)
        output = jnp.zeros((256, 256), f32)
        for half in range(2):
            rows = out_rows[half, block // 4, block % 4].reshape(256, 512)
            output = output + dot_nt(attended[:, half * 512 : half * 512 + 512], rows)
        hidden_out[:, cols] = (state[:, cols] + modulation_ref[2:3, cols] * output).astype(bf16)


def store_kernel(*refs):
    copies = [
        pltpu.make_async_copy(refs[i], refs[3 + i], refs[6].at[i]) for i in (2, 1, 0)
    ]
    for copy in copies:
        copy.start()
    for copy in copies:
        copy.wait()


def in_hbm(arrays):
    return [pltpu.with_memory_space_constraint(array, pltpu.HBM) for array in arrays]


def per_device(
    coarse_hidden,
    coarse_modulation,
    final_weight,
    coarse_latent,
    step_index,
    guide_index,
    guide_scales,
    upsample_weight,
    upsample_bias,
    embed_weight,
    embed_bias,
    fine_modulation,
    project_weight,
    query_gain,
    key_gain,
    text_keys,
    text_values,
    text_length,
    output_weight,
):
    dma = pltpu.SemaphoreType.DMA
    sems = []
    for shape in [(8,), (8,), (4,), (8,), (4,)]:
        sems += [dma(shape), dma(shape)]
    sems += [dma, dma]
    for shape in [(8,), (4,), (4, 4), (4, 4), (5,), (2,), (4,)]:
        sems += [dma(shape), dma(shape)]
    sems += [dma((14,))]
    stored = [
        embed_weight, fine_modulation, embed_bias[None], coarse_latent,
        coarse_hidden.reshape(128, 2048), coarse_modulation[0], final_weight.T,
        text_keys, key_gain[None], text_values, guide_scales.reshape(32, 128),
        upsample_weight.T, upsample_bias[None], query_gain[None], step_index, guide_index,
        text_length,
    ]
    hbm = pl.BlockSpec(memory_space=pltpu.HBM)
    vmem = pl.BlockSpec(memory_space=pltpu.VMEM)
    guided, fine, hidden = pl.pallas_call(
        kernel,
        out_shape=(
            jax.ShapeDtypeStruct((2, 2048), f32),
            jax.ShapeDtypeStruct((2, 1, 4096), f32),
            jax.ShapeDtypeStruct((256, 2048), bf16),
        ),
        in_specs=[vmem] * 2 + [hbm] * 14 + [pl.BlockSpec(memory_space=pltpu.SMEM)] * 3,
        out_specs=(vmem, vmem, vmem),
        scratch_shapes=[pltpu.VMEM(array.shape, array.dtype) for array in stored[:14]]
        + [
            pltpu.VMEM((40, 2048), f32),
            pltpu.VMEM((8, 8, 384), f32),
            pltpu.VMEM((2, 4, 4, 8, 384), f32),
            pltpu.VMEM((16, 8, 128), f32),
            pltpu.VMEM((8, 2, 8, 128), f32),
            pltpu.VMEM((4, 2, 8, 128), f32),
            pltpu.VMEM((8, 8, 16, 128), bf16),
            pltpu.VMEM((2, 8, 512), f32),
            pltpu.VMEM((8, 512), f32),
            pltpu.VMEM((2, 2, 4, 8, 2, 16, 512), bf16),
            pltpu.VMEM((2, 3, 32, 128), f32),
            pltpu.VMEM((3, 32, 128), f32),
            pltpu.VMEM((128, 32), f32),
            pltpu.VMEM((400, 32), f32),
            pltpu.VMEM((128, 64), f32),
            pltpu.VMEM((256, 128), f32),
            pltpu.VMEM((1024, 128), bf16),
            pltpu.VMEM((1024, 128), bf16),
            pltpu.VMEM((128, 2048), bf16),
            pltpu.VMEM((128, 2048), bf16),
            pltpu.VMEM((128, 3072), bf16),
            pltpu.VMEM((256, 2048), f32),
            pltpu.VMEM((256, 1024), bf16),
            pltpu.VMEM((1024, 1024), bf16),
            pltpu.VMEM((1024, 1024), bf16),
            pltpu.VMEM((256, 1024), bf16),
            pltpu.VMEM((256, 1024), bf16),
            pltpu.VMEM((1280, 128), bf16),
            pltpu.VMEM((256, 1024), bf16),
        ]
        + sems,
        compiler_params=pltpu.CompilerParams(
            collective_id=0, has_side_effects=True, vmem_limit_bytes=48 * 1024 * 1024
        ),
    )(
        *in_hbm([project_weight, output_weight.T]), *in_hbm(stored[:14]), *stored[14:]
    )
    results = (guided, fine, hidden)
    guided, fine, hidden = pl.pallas_call(
        store_kernel,
        out_shape=[jax.ShapeDtypeStruct(array.shape, array.dtype) for array in results],
        in_specs=[vmem] * 3,
        out_specs=[hbm] * 3,
        scratch_shapes=[dma((3,))],
    )(*[pltpu.with_memory_space_constraint(array, pltpu.VMEM) for array in results])
    return guided, fine, hidden.reshape(2, 1, 128, 2048)


def solution(mesh):
    placed = (
        P("cfg", "seq", None, None),
        P("cfg", None, None),
        P(),
        P("seq", None),
        P(),
        P(),
        P(),
        P(),
        P(),
        P(),
        P(),
        P(),
        P(("cfg", "seq"), None),
        P(),
        P(),
        P(),
        P(),
        P(),
        P(None, ("cfg", "seq")),
    )
    return jax.shard_map(
        per_device,
        mesh=mesh,
        in_specs=placed,
        out_specs=(P("seq", None), P("seq", "cfg", None), P("seq", "cfg", None, None)),
        check_vma=False,
    )
```

```python
import jax
import jax.numpy as jnp
from jax import lax
from jax.experimental import pallas as pl
from jax.experimental.pallas import tpu as pltpu
from jax.sharding import PartitionSpec as P

HEADS = 8
STEPS = 50
MESH = pl.DeviceIdType.MESH
LOG2E = 1.4426950408889634

epsilon = 1e-06
flow_shift = 5.0
highest = lax.Precision.HIGHEST
f32 = jnp.float32
bf16 = jnp.bfloat16

def remote(src, dst, send_sem, recv_sem, device):
    return pltpu.make_async_remote_copy(
        src_ref=src, dst_ref=dst, send_sem=send_sem, recv_sem=recv_sem,
        device_id=device, device_id_type=MESH,
    )


class Place:
    def __init__(self):
        self.x_lo = lax.axis_index("cfg")
        seq = lax.axis_index("seq")
        self.seq = seq
        self.core = lax.rem(seq, 2)
        self.x_hi = lax.rem(lax.div(seq, 2), 2)
        self.z = lax.rem(lax.div(seq, 4), 8)
        self.y = lax.div(seq, 32)
        self.x = self.x_hi * 2 + self.x_lo
        self.member = self.x_lo * 4 + self.x_hi * 2 + self.core
        self.line = lax.div(seq, 4)

    def at(self, x=None, y=None, z=None, core=None):
        x = self.x if x is None else x
        y = self.y if y is None else y
        z = self.z if z is None else z
        core = self.core if core is None else core
        return (lax.rem(x, 2), ((y * 8 + z) * 2 + lax.div(x, 2)) * 2 + core)

    def member_device(self, member):
        return (lax.div(member, 4), self.line * 4 + lax.rem(member, 4))


def greet(place):
    barrier = pltpu.get_barrier_semaphore()
    partners = [place.member_device(lax.rem(place.member + d, 8)) for d in range(1, 8)]
    partners += [place.at(y=lax.rem(place.y + d, 4)) for d in range(1, 4)]
    partners += [place.at(z=lax.rem(place.z + d, 8)) for d in range(1, 8)]
    for other in (lax.rem(place.seq + 1, 128), lax.rem(place.seq + 127, 128)):
        partners += [(place.x_lo, other), (1 - place.x_lo, other)]
    for partner in partners:
        pl.semaphore_signal(barrier, inc=1, device_id=partner, device_id_type=MESH)
    return barrier, len(partners)

def layer_norm(values):
    centred = values - jnp.mean(values, -1, keepdims=True)
    return centred * lax.rsqrt(jnp.mean(centred * centred, -1, keepdims=True) + epsilon)


def sigma_at(step_value):
    fraction = 1.0 - step_value / STEPS
    return flow_shift * fraction / (1.0 + (flow_shift - 1.0) * fraction)


def split_two(values):
    high = values.astype(bf16).astype(f32)
    return high, values - high


def dot_nt(a, b):
    return lax.dot_general(a, b, (((1,), (1,)), ((), ())), preferred_element_type=f32)


def dot_nn(a, b):
    return jnp.dot(a, b, preferred_element_type=f32)


TAPS = (((0,), (1, 2), ()), ((), (0, 1), (2,)))


def coarse_weights(up_ref, offset):
    eye = (
        lax.broadcasted_iota(jnp.int32, (32, 32), 0) == lax.broadcasted_iota(jnp.int32, (32, 32), 1)
    ).astype(f32)
    bands = []
    for a in range(2):
        for c in range(2):
            blocks = []
            for column in range(3):
                block = eye if offset == 1 and column == 1 else jnp.zeros((32, 32), f32)
                for r in TAPS[a][offset]:
                    for k in TAPS[c][column]:
                        tap = (3 * r + k) * 32
                        block = block + up_ref[:, tap : tap + 32]
                blocks.append(block)
            bands.append(jnp.concatenate(blocks, 1))
    return jnp.concatenate(bands, 0)


def kernel(
    weight_ref, output_ref, *refs
):
    stored, scalars, refs = refs[:14], refs[14:17], refs[17:]
    (guided_out, fine_out, hidden_out), held, refs = refs[:3], refs[3:17], refs[17:]
    (
        embed_ref, modulation_ref, bias_ref, latent_ref, hidden_ref, coarse_mod_ref, final_ref,
        text_keys_ref, key_gain_ref, text_values_ref, scales_ref, up_ref, up_bias_ref,
        query_gain_ref,
    ) = held
    step_ref, guide_ref, length_ref = scalars
    run(
        step_ref, guide_ref, length_ref, weight_ref, output_ref, stored, held,
        embed_ref, modulation_ref, bias_ref, latent_ref, hidden_ref, coarse_mod_ref, final_ref,
        text_keys_ref, key_gain_ref, text_values_ref, scales_ref, up_ref, up_bias_ref,
        query_gain_ref, guided_out, fine_out, hidden_out, *refs
    )


def run(
    step_ref, guide_ref, length_ref, weight_ref, output_ref, stored, held,
    embed_ref, modulation_ref, bias_ref, latent_ref, hidden_ref, coarse_mod_ref, final_ref,
    text_keys_ref, key_gain_ref, text_values_ref, scales_ref, up_ref, up_bias_ref,
    query_gain_ref, guided_out, fine_out, hidden_out,
    left, own_rows, group_rows, partial, z_parts, y_parts, folded,
    out_chunk, out_sibling, out_rows,
    velocity, latents, cells, grid_cells, pairs, query_tokens, key_tokens,
    key_left, centred_right, state_right, folded_right, state,
    query_buf, key_buf, value_buf, text_key_buf, text_value_buf, ones_buf, attended,
    *sems,
):
    (
        a_send, a_recv, rz_send, rz_recv, ry_send, ry_recv, gz_send, gz_recv, gx_send, gx_recv,
        s_send, s_recv, wz_send, wz_recv, wp_send, wp_recv, wq_send, wq_recv, ws_send, ws_recv,
        v_send, v_recv, l_send, l_recv, gs_send, gs_recv, load_sem,
    ) = sems
    loads = [
        pltpu.make_async_copy(source, target, load_sem.at[i])
        for i, (source, target) in enumerate(zip(stored, held))
    ]
    for load in loads:
        load.start()
    place = Place()
    core, z, y, member, seq, branch = (
        place.core, place.z, place.y, place.member, place.seq, place.x_lo
    )
    group_rows[...] = jnp.zeros_like(group_rows)
    barrier, count = greet(place)
    for part in range(8):
        own_rows[part] = weight_ref[:, part * 384 : (part + 1) * 384].astype(f32)
    turned = output_ref[...].astype(f32)
    out_chunk[0] = turned[:, :512]
    out_chunk[1] = turned[:, 512:]
    for load in loads[:4]:
        load.wait()
    for m in range(32):
        latents[1, m : m + 1, :] = latent_ref[m // 16 : m // 16 + 1, m % 16 * 128 : m % 16 * 128 + 128]
    pl.semaphore_wait(barrier, count)
    sibling = place.at(core=1 - core)
    swap = remote(out_chunk.at[1 - core], out_sibling, s_send, s_recv, sibling)
    swap.start()
    quarter = lax.rem(place.line, 4)
    spread = []
    for d in range(1, 8):
        target = lax.rem(member + d, 8)
        copy = remote(
            own_rows.at[target],
            group_rows.at[place.x_lo, quarter, place.x_hi * 2 + core],
            a_send.at[d], a_recv.at[d], place.member_device(target),
        )
        copy.start()
        spread.append(copy)
    after, before = lax.rem(seq + 1, 128), lax.rem(seq + 127, 128)
    latent_copies = [
        remote(latents.at[1], latents.at[0], l_send.at[0], l_recv.at[0], (branch, after)),
        remote(latents.at[1], latents.at[2], l_send.at[1], l_recv.at[1], (branch, before)),
    ]
    for copy in latent_copies:
        copy.start()
    group_rows[place.x_lo, quarter, place.x_hi * 2 + core] = own_rows[member]

    embed = embed_ref[...].astype(f32)
    scale = 1.0 + modulation_ref[1:2, :]
    embed_centred = embed - jnp.mean(embed, -1, keepdims=True)
    bias = bias_ref[...]
    bias_centred = bias - jnp.mean(bias, -1, keepdims=True)
    width = embed.shape[1]
    left[0:32] = embed_centred * scale
    left[32:40] = jnp.concatenate(
        [bias_centred * scale, modulation_ref[0:1, :], jnp.zeros((6, width), f32)], 0
    )

    for copy in spread:
        copy.wait()
    column = pl.multiple_of(lax.div(place.line, 4) * 128, 128)
    total = jnp.zeros((40, 384), f32)
    for half in range(2):
        high, rest = split_two(left[:, pl.ds(half * 1024 + column, 128)])
        middle, low = split_two(rest)
        terms = dot_nn(
            jnp.concatenate([high, middle, low], 0).astype(bf16),
            group_rows[half].reshape(128, 384).astype(bf16),
        )
        total = total + (terms[:40] + terms[40:80] + terms[80:])
    for row in range(5):
        for block in range(3):
            place_at = block * 4 + row if row < 4 else 12 + block
            partial[place_at] = total[row * 8 : row * 8 + 8, block * 128 : block * 128 + 128]
    partial[15] = jnp.zeros((8, 128), f32)
    scatter = []
    for d in range(1, 8):
        target = lax.rem(z + d, 8)
        copy = remote(
            partial.at[pl.ds(target * 2, 2)], z_parts.at[z],
            rz_send.at[d], rz_recv.at[d], place.at(z=target),
        )
        copy.start()
        scatter.append(copy)
    z_parts[z] = partial[pl.ds(z * 2, 2)]

    swap.wait()
    mine, other = out_chunk[core], out_sibling[...]
    first = core == 0
    out_rows[core, place.x_lo, y, z, place.x_hi] = jnp.concatenate(
        [jnp.where(first, mine, other), jnp.where(first, other, mine)], 0
    ).astype(bf16)
    along_z = []
    for d in range(1, 8):
        slot = out_rows.at[core, place.x_lo, y, z, place.x_hi]
        copy = remote(slot, slot, wz_send.at[d], wz_recv.at[d], place.at(z=lax.rem(z + d, 8)))
        copy.start()
        along_z.append(copy)

    for load in loads[4:7]:
        load.wait()
    for row in range(2):
        modulated = (
            layer_norm(hidden_ref[row * 64 : row * 64 + 64, :].astype(f32))
            * (1.0 + coarse_mod_ref[1:2, :])
            + coarse_mod_ref[0:1, :]
        ).astype(bf16)
        cells[row * 64 : row * 64 + 64, :] = dot_nt(modulated, final_ref[...])
    velocity[branch, 1] = jnp.concatenate(
        [cells[pl.ds(c, 32, stride=4), :] for c in range(4)], 1
    )
    velocity_copies = []
    targets = [
        ((1 - branch, seq), 1), ((branch, after), 0), ((1 - branch, after), 0),
        ((branch, before), 2), ((1 - branch, before), 2),
    ]
    for d, (target, slot) in enumerate(targets):
        copy = remote(
            velocity.at[branch, 1], velocity.at[branch, slot], v_send.at[d], v_recv.at[d], target
        )
        copy.start()
        velocity_copies.append(copy)

    for copy in scatter:
        copy.wait()
    y_parts[y] = jnp.sum(z_parts[...], 0)
    over_y = []
    for d in range(1, 4):
        copy = remote(
            y_parts.at[y], y_parts.at[y], ry_send.at[d], ry_recv.at[d],
            place.at(y=lax.rem(y + d, 4)),
        )
        copy.start()
        over_y.append(copy)

    for copy in along_z:
        copy.wait()
    first_at = y * (1 - core) + place.x * core
    second_at = place.x * (1 - core) + y * core

    def piece(p, q):
        px, py = q * (1 - core) + p * core, p * (1 - core) + q * core
        return out_rows.at[core, lax.rem(px, 2), py, :, lax.div(px, 2)]

    def piece_device(p, q):
        return place.at(x=q * (1 - core) + p * core, y=p * (1 - core) + q * core)

    along_p = []
    for d in range(1, 4):
        slot = piece(first_at, second_at)
        copy = remote(
            slot, slot, wp_send.at[d], wp_recv.at[d],
            piece_device(lax.rem(first_at + d, 4), second_at),
        )
        copy.start()
        along_p.append(copy)
    along_q = []

    def send_q(e):
        for d in range(1, 4):
            slot = piece(lax.rem(first_at + 4 - e, 4), second_at)
            copy = remote(
                slot, slot, wq_send.at[e, d], wq_recv.at[e, d],
                piece_device(first_at, lax.rem(second_at + d, 4)),
            )
            copy.start()
            along_q.append(copy)

    to_sibling = []

    def send_sibling(e, d):
        slot = piece(lax.rem(first_at + 4 - e, 4), lax.rem(second_at + 4 - d, 4))
        copy = remote(slot, slot, ws_send.at[e, d], ws_recv.at[e, d], sibling)
        copy.start()
        to_sibling.append(copy)


    for load in loads[7:]:
        load.wait()

    lane_zeros = jnp.zeros((61, width), f32)
    high, low = split_two(embed_centred)
    bias_high, bias_low = split_two(bias_centred)
    centred_right[...] = jnp.concatenate(
        [high, low, bias_high, bias_low, jnp.zeros((1, width), f32), lane_zeros], 0
    ).astype(bf16)
    bias_high, bias_rest = split_two(bias)
    bias_middle, bias_low = split_two(bias_rest)
    state_right[...] = jnp.concatenate(
        [embed, jnp.zeros((32, width), f32), bias_high, bias_middle, bias_low, lane_zeros], 0
    ).astype(bf16)
    same_head = (
        lax.div(lax.broadcasted_iota(jnp.int32, (256, 256), 0), 128)
        == lax.div(lax.broadcasted_iota(jnp.int32, (256, 256), 1), 128)
    ).astype(bf16)
    key_gain = jnp.concatenate([key_gain_ref[...]] * 2, 1)
    query_gain = jnp.concatenate([query_gain_ref[...]] * 2, 1) * (LOG2E * 128 ** (-0.5))

    def head_norm(values, gain):
        squares = dot_nn((values * values).astype(bf16), same_head)
        return (values * lax.rsqrt(squares * (1.0 / 128) + epsilon) * gain).astype(bf16)

    for pair in range(4):
        cols = slice(pair * 256, pair * 256 + 256)
        text_key_buf[:, cols] = head_norm(text_keys_ref[:, cols].astype(f32), key_gain)
    length = length_ref[0]
    real = lax.broadcasted_iota(jnp.int32, (256, 1), 0) < length
    text_value_buf[...] = jnp.where(real, text_values_ref[...].astype(f32), 0.0).astype(bf16)
    row_ok = [jnp.where(seq > 0, 1.0, 0.0), 1.0, 1.0, jnp.where(seq < 127, 1.0, 0.0)]
    for row in range(4):
        ones_buf[row * 256 : row * 256 + 256, :] = (
            jnp.ones((256, 128), f32) * row_ok[row]
        ).astype(bf16)
    ones_buf[1024:1280, :] = jnp.where(real, jnp.ones((256, 128), f32), 0.0).astype(bf16)

    for copy in over_y:
        copy.wait()
    summed = jnp.sum(y_parts[...], 0)
    high, low = split_two(summed)
    low = jnp.concatenate([jnp.zeros((2, 2, 128), f32), low[:, :6]], 1)
    folded[member, z] = jnp.where(z >= 6, high + low, summed).reshape(16, 128).astype(bf16)
    gather_z = []
    for d in range(1, 8):
        slot = folded.at[member, z]
        copy = remote(slot, slot, gz_send.at[d], gz_recv.at[d], place.at(z=lax.rem(z + d, 8)))
        copy.start()
        gather_z.append(copy)

    send_q(0)
    send_sibling(0, 0)

    for copy in latent_copies + velocity_copies:
        copy.wait()
    slots = (
        lax.broadcasted_iota(jnp.int32, (32, 128), 0) * 128
        + lax.broadcasted_iota(jnp.int32, (32, 128), 1)
    )
    guidance = jnp.sum(
        jnp.where(slots == guide_ref[0], scales_ref[...], 0.0), axis=(0, 1), keepdims=True
    )
    step = jnp.full((1, 128), step_ref[0], jnp.int32)
    sigma_step = sigma_at((step + 1).astype(f32)) - sigma_at(step.astype(f32))
    for block in range(3):
        conditional, unconditional = velocity[0, block], velocity[1, block]
        guided = unconditional + guidance * (conditional - unconditional)
        if block == 1:
            for m in range(32):
                guided_out[m // 16 : m // 16 + 1, m % 16 * 128 : m % 16 * 128 + 128] = guided[
                    m : m + 1, :
                ]
        stepped = latents[block] + sigma_step * guided
        if block == 0:
            stepped = jnp.where(seq > 0, stepped, 0.0)
        if block == 2:
            stepped = jnp.where(seq < 127, stepped, 0.0)
        for c in range(4):
            grid_cells[pl.ds(8 + block * 128 + c, 32, stride=4), :] = stepped[
                :, c * 32 : c * 32 + 32
            ]
    grid_cells[0:8, :] = jnp.zeros((8, 32), f32)
    grid_cells[392:400, :] = jnp.zeros((8, 32), f32)
    cell = lax.rem(lax.broadcasted_iota(jnp.int32, (384, 32), 0), 64)
    around = jnp.concatenate(
        [
            jnp.where(cell == 0, 0.0, grid_cells[7:391, :]),
            grid_cells[8:392, :],
            jnp.where(cell == 63, 0.0, grid_cells[9:393, :]),
        ],
        1,
    )
    fine = jnp.concatenate([up_bias_ref[...]] * 4, 1)
    for offset in range(3):
        fine = fine + lax.dot_general(
            around[offset * 64 : offset * 64 + 256],
            coarse_weights(up_ref, offset),
            (((1,), (1,)), ((), ())),
            precision=highest,
            preferred_element_type=f32,
        )
    own = fine[64:192]
    pairs[...] = jnp.where(branch == 0, own[:, :64], own[:, 64:])
    flat = jnp.concatenate([pairs[pl.ds(0, 64, stride=2), :], pairs[pl.ds(1, 64, stride=2), :]], 1)
    for m in range(64):
        fine_out[m // 32, :, m % 32 * 128 : m % 32 * 128 + 128] = flat[m : m + 1, :]

    lane = lax.broadcasted_iota(jnp.int32, (256, 128), 1)
    turns = [fine] + [pltpu.roll(fine, 32 * turn, axis=1) for turn in range(1, 4)]
    tail = jnp.where(lane < 67, 1.0, 0.0)
    groups = [
        jnp.where(lane < 32, turns[(4 - g) % 4], jnp.where(lane < 64, turns[(5 - g) % 4], tail))
        for g in range(4)
    ]
    for g in range(4):
        for row in range(4):
            start = row * 256 + g * 64
            key_tokens[start : start + 64, :] = groups[g][row * 64 : row * 64 + 64].astype(bf16)
    for c in range(2):
        chosen = jnp.where(branch == 0, groups[c], groups[2 + c])
        for row in range(2):
            query_tokens[pl.ds(row * 128 + c, 64, stride=2), :] = chosen[
                64 + row * 64 : 128 + row * 64
            ]
    own_tokens = query_tokens[...].astype(bf16)

    for copy in gather_z:
        copy.wait()
    gather_x, to_twin = [], []

    def send_twin(d):
        source = lax.rem(place.x + 4 - d, 4)
        slot = folded.at[lax.rem(source, 2) * 4 + lax.div(source, 2) * 2 + core]
        copy = remote(slot, slot, gs_send.at[d], gs_recv.at[d], sibling)
        copy.start()
        to_twin.append(copy)

    for d in range(1, 4):
        slot = folded.at[member]
        copy = remote(
            slot, slot, gx_send.at[d], gx_recv.at[d], place.at(x=lax.rem(place.x + d, 4))
        )
        copy.start()
        gather_x.append(copy)
    send_twin(0)

    for e in range(1, 4):
        along_p[e - 1].wait()
        send_q(e)
        send_sibling(e, 0)
    def rstd_of(tokens):
        centred = dot_nn(tokens, centred_right[...])
        return lax.rsqrt(jnp.mean(centred * centred, -1, keepdims=True) + epsilon)

    is_low = ((lane >= 32) & (lane < 64)) | (lane == 65)
    is_one = (lane == 67) | (lane == 68)

    def scaled(tokens):
        high, low = split_two(rstd_of(tokens) * tokens.astype(f32))
        return jnp.where(is_one, 1.0, jnp.where(is_low, low, high))

    own_left = scaled(own_tokens).astype(bf16)
    for row in range(4):
        rows = slice(row * 256, row * 256 + 256)
        key_left[rows, :] = (scaled(key_tokens[rows, :]) * row_ok[row]).astype(bf16)
    folded_right[64:128, :] = jnp.zeros((64, 3072), bf16)
    for block in range(8):
        cols = slice(block * 256, block * 256 + 256)
        state[:, cols] = dot_nn(own_tokens, state_right[:, cols])

    for d in range(1, 4):
        gather_x[d - 1].wait()
        send_twin(d)
    for copy in to_twin:
        copy.wait()
    for part in range(8):
        for block in range(3):
            at = part * 384 + block * 128
            rows = folded[part, block * 2 : block * 2 + 2].reshape(32, 128)
            folded_right[0:32, at : at + 128] = rows
            folded_right[32:64, at : at + 128] = rows
            rest = folded[part, 6 + block // 2].astype(f32)[block % 2 * 8 : block % 2 * 8 + 8]
            folded_right[64:80, at : at + 128] = jnp.concatenate(
                [rest[0:1], rest[0:1], rest[2:3], rest[1:2], rest[3:4], jnp.zeros((11, 128), f32)],
                0,
            ).astype(bf16)

    def project(tokens, start):
        return dot_nn(tokens, folded_right[:, start : start + 256])

    for pair in range(4):
        cols = slice(pair * 256, pair * 256 + 256)
        query_buf[:, cols] = head_norm(project(own_left, pair * 256), query_gain)
    for row in range(4):
        rows = slice(row * 256, row * 256 + 256)
        tokens = key_left[rows, :]
        for pair in range(4):
            cols = slice(pair * 256, pair * 256 + 256)
            key_buf[rows, cols] = head_norm(project(tokens, 1024 + pair * 256), key_gain)
            value_buf[rows, cols] = project(tokens, 2048 + pair * 256).astype(bf16)

    for head in range(HEADS):
        cols = slice(head * 128, head * 128 + 128)
        text_right = jnp.concatenate([text_value_buf[:, cols], ones_buf[1024:1280, :]], 1)
        query = query_buf[:, cols]

        def weighted(part, window):
            weights = jnp.exp2(dot_nt(part, key_buf[window, cols])).astype(bf16)
            right = jnp.concatenate([value_buf[window, cols], ones_buf[window, :]], 1)
            return dot_nn(weights, right)

        text_weights = jnp.exp2(dot_nt(query, text_key_buf[:, cols])).astype(bf16)
        sums = (
            weighted(query, slice(256, 768))
            + dot_nn(text_weights, text_right)
            + jnp.concatenate(
                [weighted(query[:128], slice(0, 256)), weighted(query[128:], slice(768, 1024))], 0
            )
        )
        attended[:, cols] = (sums[:, :128] / sums[:, 128:]).astype(bf16)
        if head >= 5:
            for item in range((head - 5) * 4, (head - 5) * 4 + 4):
                along_q[item].wait()
                send_sibling(item // 3, item % 3 + 1)

    for copy in to_sibling:
        copy.wait()
    for block in range(8):
        cols = slice(block * 256, block * 256 + 256)
        output = jnp.zeros((256, 256), f32)
        for half in range(2):
            rows = out_rows[half, block // 4, block % 4].reshape(256, 512)
            output = output + dot_nt(attended[:, half * 512 : half * 512 + 512], rows)
        hidden_out[:, cols] = (state[:, cols] + modulation_ref[2:3, cols] * output).astype(bf16)


def store_kernel(*refs):
    copies = [
        pltpu.make_async_copy(refs[i], refs[3 + i], refs[6].at[i]) for i in (2, 1, 0)
    ]
    for copy in copies:
        copy.start()
    for copy in copies:
        copy.wait()


def in_hbm(arrays):
    return [pltpu.with_memory_space_constraint(array, pltpu.HBM) for array in arrays]


def per_device(
    coarse_hidden,
    coarse_modulation,
    final_weight,
    coarse_latent,
    step_index,
    guide_index,
    guide_scales,
    upsample_weight,
    upsample_bias,
    embed_weight,
    embed_bias,
    fine_modulation,
    project_weight,
    query_gain,
    key_gain,
    text_keys,
    text_values,
    text_length,
    output_weight,
):
    dma = pltpu.SemaphoreType.DMA
    sems = []
    for shape in [(8,), (8,), (4,), (8,), (4,)]:
        sems += [dma(shape), dma(shape)]
    sems += [dma, dma]
    for shape in [(8,), (4,), (4, 4), (4, 4), (5,), (2,), (4,)]:
        sems += [dma(shape), dma(shape)]
    sems += [dma((14,))]
    stored = [
        embed_weight, fine_modulation, embed_bias[None], coarse_latent,
        coarse_hidden.reshape(128, 2048), coarse_modulation[0], final_weight.T,
        text_keys, key_gain[None], text_values, guide_scales.reshape(32, 128),
        upsample_weight.T, upsample_bias[None], query_gain[None], step_index, guide_index,
        text_length,
    ]
    hbm = pl.BlockSpec(memory_space=pltpu.HBM)
    vmem = pl.BlockSpec(memory_space=pltpu.VMEM)
    guided, fine, hidden = pl.pallas_call(
        kernel,
        out_shape=(
            jax.ShapeDtypeStruct((2, 2048), f32),
            jax.ShapeDtypeStruct((2, 1, 4096), f32),
            jax.ShapeDtypeStruct((256, 2048), bf16),
        ),
        in_specs=[vmem] * 2 + [hbm] * 14 + [pl.BlockSpec(memory_space=pltpu.SMEM)] * 3,
        out_specs=(vmem, vmem, vmem),
        scratch_shapes=[pltpu.VMEM(array.shape, array.dtype) for array in stored[:14]]
        + [
            pltpu.VMEM((40, 2048), f32),
            pltpu.VMEM((8, 8, 384), f32),
            pltpu.VMEM((2, 4, 4, 8, 384), f32),
            pltpu.VMEM((16, 8, 128), f32),
            pltpu.VMEM((8, 2, 8, 128), f32),
            pltpu.VMEM((4, 2, 8, 128), f32),
            pltpu.VMEM((8, 8, 16, 128), bf16),
            pltpu.VMEM((2, 8, 512), f32),
            pltpu.VMEM((8, 512), f32),
            pltpu.VMEM((2, 2, 4, 8, 2, 16, 512), bf16),
            pltpu.VMEM((2, 3, 32, 128), f32),
            pltpu.VMEM((3, 32, 128), f32),
            pltpu.VMEM((128, 32), f32),
            pltpu.VMEM((400, 32), f32),
            pltpu.VMEM((128, 64), f32),
            pltpu.VMEM((256, 128), f32),
            pltpu.VMEM((1024, 128), bf16),
            pltpu.VMEM((1024, 128), bf16),
            pltpu.VMEM((128, 2048), bf16),
            pltpu.VMEM((128, 2048), bf16),
            pltpu.VMEM((128, 3072), bf16),
            pltpu.VMEM((256, 2048), f32),
            pltpu.VMEM((256, 1024), bf16),
            pltpu.VMEM((1024, 1024), bf16),
            pltpu.VMEM((1024, 1024), bf16),
            pltpu.VMEM((256, 1024), bf16),
            pltpu.VMEM((256, 1024), bf16),
            pltpu.VMEM((1280, 128), bf16),
            pltpu.VMEM((256, 1024), bf16),
        ]
        + sems,
        compiler_params=pltpu.CompilerParams(
            collective_id=0, has_side_effects=True, vmem_limit_bytes=48 * 1024 * 1024
        ),
    )(
        *in_hbm([project_weight, output_weight.T]), *in_hbm(stored[:14]), *stored[14:]
    )
    results = (guided, fine, hidden)
    guided, fine, hidden = pl.pallas_call(
        store_kernel,
        out_shape=[jax.ShapeDtypeStruct(array.shape, array.dtype) for array in results],
        in_specs=[vmem] * 3,
        out_specs=[hbm] * 3,
        scratch_shapes=[dma((3,))],
    )(*[pltpu.with_memory_space_constraint(array, pltpu.VMEM) for array in results])
    return guided, fine, hidden.reshape(2, 1, 128, 2048)


def solution(mesh):
    placed = (
        P("cfg", "seq", None, None),
        P("cfg", None, None),
        P(),
        P("seq", None),
        P(),
        P(),
        P(),
        P(),
        P(),
        P(),
        P(),
        P(),
        P(("cfg", "seq"), None),
        P(),
        P(),
        P(),
        P(),
        P(),
        P(None, ("cfg", "seq")),
    )
    return jax.shard_map(
        per_device,
        mesh=mesh,
        in_specs=placed,
        out_specs=(P("seq", None), P("seq", "cfg", None), P("seq", "cfg", None, None)),
        check_vma=False,
    )
```
